128 devices in a mesh: dp: 16 (over x, z_lo, core), tensor: 8 (over z_hi, y).
Axes of the slice: x: 4, y: 4, z: 4 (z_hi: 2, z_lo: 2; z = z_hi * 2 + z_lo), core: 2. Of those that a mesh axis runs over, the one named last changes fastest.
Arguments:
- layer_input: bfloat16 [64, 256, 4096], P('dp', None, 'tensor'), may hold values from -6 to 6
- output_cotangent: bfloat16 [64, 256, 4096], P('dp'), may hold values from -6 to 6
- gate_preact: bfloat16 [64, 256, 14336], P('dp', None, 'tensor'), may hold values from -8 to 8
- down_weight: bfloat16 [14336, 4096], P('tensor', 'dp'), may hold values from -0.046875 to 0.046875
- lengths: int32 [64], P('dp'), may hold values from 32 to 256, as said below
- input_signs: int32 [4096, 8], P('tensor'), may hold values from 0 to 1
- hidden_signs: int32 [14336, 8], P('tensor'), may hold values from 0 to 1
- basis_in: float32 [8, 8], replicated, may hold values from -2 to 2
- basis_out: float32 [8, 8], replicated, may hold values from -2 to 2
- eigenvalues: float32 [8, 8], replicated, may hold values from 0.05 to 5
- query_grads: float32 [4096, 64], P('tensor', 'dp'), may hold values from -6 to 6
Outputs:
- scores: float32 [64, 4096], P('dp', 'tensor')
The draws below stay inside these ranges and needn't reach their ends.
Inputs may be any that keep to these rules, and one draw needn't show every extreme that they name: `lengths`: some example has all 256 tokens.
All inputs are finite; a program needn't handle non-finite values.
Results may differ from the reference program's by a relative error of at most 0.003.
Values may be sent and summed in bfloat16 or wider, within the bound.
A program may use at most 256 MiB of HBM per device.

```python
import math
import jax
import jax.numpy as jnp
from jax import lax

D = 4096
FF = 14336
RA = 8
RG = 8
L = 256
QUERIES = 4096
EXAMPLES = 64


def draw_lengths(key, part):
    key = jax.random.fold_in(key, 11)
    values = jax.random.randint(key, (EXAMPLES,), L // 8, L + 1).astype(jnp.int32)
    return values.at[0].set(L)


def with_ends(values, own_key, smallest, top_value):
    dims = values.shape
    spot = [jax.random.randint(jax.random.fold_in(own_key, axis), (), 0, dims[axis]) for axis in range(len(dims))]
    values = values.at[tuple(spot)].set(smallest)
    longest = dims.index(max(dims))
    spot[longest] = (spot[longest] + 1) % dims[longest]
    return values.at[tuple(spot)].set(top_value)


def block_levels(rng, extent, pieces, smallest, largest):
    gain, own = 1.0, jax.random.fold_in(rng, 6)
    for dim, blocks in pieces:
        draws = jnp.exp(jax.random.uniform(jax.random.fold_in(own, dim), (blocks,), jnp.float32, smallest / len(pieces), largest / len(pieces)))
        gain = gain * jnp.repeat(draws, extent[dim] // blocks).reshape([-1 if axis == dim else 1 for axis in range(len(extent))])
    return gain


def noise(key, dims, spread, bound, shards=(), kind=jnp.bfloat16):
    result = jax.random.normal(key, dims, jnp.float32) * spread
    if len(shards) > 0:
        result = block_levels(key, dims, shards, -0.22, 0.18) * result
    return jnp.clip(result, min=-bound, max=bound).astype(kind)


def setup_inputs(seed: int = 0) -> dict:
    splits = jax.random.split(jax.random.key(seed), 12)
    return {
        "layer_input": noise(splits[0], (EXAMPLES, L, D), 1.0, 6.0, ((0, 16), (2, 8))),
        "output_cotangent": noise(splits[1], (EXAMPLES, L, D), 1.0, 6.0, ((0, 16),)),
        "gate_preact": noise(splits[2], (EXAMPLES, L, FF), 1.5, 8.0, ((0, 16), (2, 8))),
        "down_weight": noise(splits[3], (FF, D), FF ** -0.5, 0.046875, ((0, 8), (1, 16))),
        "lengths": draw_lengths(jax.random.fold_in(splits[11], 71), 0),
        "input_signs": with_ends(jax.random.randint(splits[5], (D, RA), 0, 2), jax.random.fold_in(splits[5], 1), 0, 1).astype(jnp.int32),
        "hidden_signs": with_ends(jax.random.randint(splits[6], (FF, RG), 0, 2), jax.random.fold_in(splits[6], 1), 0, 1).astype(jnp.int32),
        "basis_in": noise(splits[7], (RA, RA), RA ** -0.5, 2.0, (), jnp.float32),
        "basis_out": noise(splits[8], (RG, RG), RG ** -0.5, 2.0, (), jnp.float32),
        "eigenvalues": jnp.clip(jnp.exp(jax.random.uniform(splits[9], (RA, RG), jnp.float32, math.log(0.05), math.log(5.0))), 0.05, 5.0),
        "query_grads": noise(splits[10], (QUERIES, RA * RG), 1.0, 6.0, ((0, 8), (1, 16)), jnp.float32),
    }


damping_shift = 0.1


def reference(layer_input, output_cotangent, gate_preact, down_weight, lengths, input_signs, hidden_signs, basis_in, basis_out, eigenvalues, query_grads):
    sign_in = (2 * input_signs - 1).astype(jnp.bfloat16)
    sign_hid = (2 * hidden_signs - 1).astype(jnp.bfloat16)
    down_t = down_weight.T

    def per_example(items):
        inputs, cotangent, gate, count = items
        input_proj = jnp.dot(inputs, sign_in, preferred_element_type=jnp.float32) * (D ** -0.5)
        hidden_grad = jnp.dot(cotangent, down_t, preferred_element_type=jnp.float32)
        up_grad = (hidden_grad * jax.nn.silu(gate.astype(jnp.float32))).astype(jnp.bfloat16)
        output_proj = jnp.dot(up_grad, sign_hid, preferred_element_type=jnp.float32) * (FF ** -0.5)
        positions = jnp.arange(L, dtype=jnp.int32)
        weight = (positions < count).astype(jnp.float32) / count.astype(jnp.float32)
        return jnp.einsum("t,ta,tb->ab", weight, input_proj, output_proj, precision=lax.Precision.HIGHEST)

    example_grad = lax.map(per_example, (layer_input, output_cotangent, gate_preact, lengths))
    rotated = jnp.einsum("ai,eab,bj->eij", basis_in, example_grad, basis_out, precision=lax.Precision.HIGHEST)
    queries = query_grads.reshape(query_grads.shape[0], RA, RG)
    precond = jnp.einsum("ai,qab,bj->qij", basis_in, queries, basis_out, precision=lax.Precision.HIGHEST) / (eigenvalues + damping_shift)
    return jnp.einsum("eij,qij->eq", rotated, precond, precision=lax.Precision.HIGHEST)
```

```python
import functools

import jax
import jax.numpy as jnp
from jax import lax
from jax.experimental import pallas as pl
from jax.experimental.pallas import tpu as pltpu
from jax.sharding import PartitionSpec as P

MESH = pl.DeviceIdType.MESH
HIGH = lax.Precision.HIGHEST
F32, BF16 = jnp.float32, jnp.bfloat16
D, FF, RA, RG = 4096, 14336, 8, 8
SHIFT = 0.1
TOK, HID, COLS, SLOTS = 1024, 1792, 256, 256
BLOCK = 256
NT = (((1,), (1,)), ((), ()))

STAGES = [(256 * i, 256, "abcabd"[i]) for i in range(6)]
STAGES += [(1536, 96, "a"), (1632, 80, "b"), (1712, 80, "c")]
N = len(STAGES)
O, L, R, Z, FAR, ZL, ZR, ZF = range(8)
HOP2 = {
    "a": ((L, "xp", FAR), (Z, "xp", ZL), (Z, "xm", ZR)),
    "b": ((R, "xm", FAR), (Z, "xm", ZR), (Z, "xp", ZL)),
    "c": ((L, "xp", FAR), (Z, "xm", ZR), (L, "z", ZL)),
    "d": ((R, "xm", FAR), (Z, "xp", ZL), (R, "z", ZR)),
}
HOP1 = ((O, "xp", L), (O, "xm", R), (O, "z", Z))


def column(slot, sibling=0):
    return (slot // 4) * 2048 + sibling * 1024 + (slot % 4) * COLS


def kernel(
    li_hbm, ct_hbm, gate_hbm, w_hbm, len_ref, sin_hbm, shid_hbm, bi_hbm, bo_hbm, ev_hbm, q_hbm,
    o_ref,
    w, ct, gate, li, sin, shid, bi, bo, ev, qbuf, qfull, mat, ybuf, zbuf, gbuf, in64, s64, hid, out64,
    ss_w, rs_w, ss_s, rs_s, ss_q, rs_q, ss_y, rs_y, ss_z, rs_z, ss_g, rs_g, lsem,
):
    dp, tn = lax.axis_index("dp"), lax.axis_index("tensor")
    x, z, c = dp // 4, (dp // 2) % 2, dp % 2
    zh, y = tn // 4, tn % 4
    xp, xm = (x + 1) % 4, (x + 3) % 4
    at = lambda xx, zz, cc: xx * 4 + zz * 2 + cc
    dev = {
        "xp": (at(xp, z, c), tn),
        "xm": (at(xm, z, c), tn),
        "z": (at(x, 1 - z, c), tn),
        "sib": (at(x, z, 1 - c), tn),
    }

    loads = []

    def load(src, dst):
        cp = pltpu.make_async_copy(src, dst, lsem.at[len(loads)])
        loads.append(cp)
        cp.start()
        return cp

    own = [load(w_hbm.at[pl.ds(0, 512)], w.at[pl.ds(0, 512), pl.ds(0, COLS)])]
    own += [load(w_hbm.at[pl.ds(512, 1280)], w.at[pl.ds(512, 1280), pl.ds(0, COLS)])]

    barrier = pltpu.get_barrier_semaphore()
    for i in range(1, 16):
        pl.semaphore_signal(barrier, inc=1, device_id=((dp + i) % 16, tn), device_id_type=MESH)
    for i in range(1, 8):
        pl.semaphore_signal(barrier, inc=1, device_id=(dp, (tn + i) % 8), device_id_type=MESH)

    load_li = load(li_hbm, li)
    load_sin = load(sin_hbm, sin)
    load_q = load(q_hbm, qbuf.at[dp])
    load_small = [load(bi_hbm, bi), load(bo_hbm, bo), load(ev_hbm, ev), load(shid_hbm, shid)]
    load_c = []
    for half in range(2):
        cc = c if half == 0 else 1 - c
        for slot, (xx, zz) in enumerate(
            ((x, z), (xm, z), (xp, z), (x, 1 - z), ((x + 2) % 4, z), (xm, 1 - z), (xp, 1 - z), ((x + 2) % 4, 1 - z))
        ):
            first = pl.multiple_of(at(xx, zz, cc) * COLS, COLS)
            load_c.append(load(ct_hbm.at[:, pl.ds(first, COLS)], ct.at[:, pl.ds(column(slot, half), COLS)]))
    load_gate = load(gate_hbm, gate)

    pl.semaphore_wait(barrier, 22)

    def piece(stage, slot):
        first, rows, _ = STAGES[stage]
        return w.at[pl.ds(first, rows), pl.ds(column(slot), COLS)]

    sent = []

    def send(stage, src, to, dst):
        cp = pltpu.make_async_remote_copy(
            src_ref=piece(stage, src), dst_ref=piece(stage, dst),
            send_sem=ss_w.at[stage, dst], recv_sem=rs_w.at[stage, dst],
            device_id=dev[to], device_id_type=MESH,
        )
        cp.start()
        sent.append(cp)

    def arrive(stage, slot):
        pltpu.make_async_remote_copy(
            src_ref=piece(stage, slot), dst_ref=piece(stage, slot),
            send_sem=ss_w.at[stage, slot], recv_sem=rs_w.at[stage, slot],
            device_id=dev["z"], device_id_type=MESH,
        ).wait_recv()

    def share_copy(stage, group):
        first, rows, _ = STAGES[stage]
        return pltpu.make_async_remote_copy(
            src_ref=w.at[pl.ds(first, rows), pl.ds(group * 2048, 1024)],
            dst_ref=w.at[pl.ds(first, rows), pl.ds(group * 2048 + 1024, 1024)],
            send_sem=ss_s.at[stage, group], recv_sem=rs_s.at[stage, group],
            device_id=dev["sib"], device_id_type=MESH,
        )

    def share(stage, group):
        cp = share_copy(stage, group)
        cp.start()
        sent.append(cp)

    def shared(stage, group):
        share_copy(stage, group).wait_recv()

    def hop1(stage):
        for src, to, dst in HOP1:
            send(stage, src, to, dst)

    row8 = lax.broadcasted_iota(jnp.int32, (8, 64), 0)
    col8 = lax.broadcasted_iota(jnp.int32, (8, 64), 1)
    by_b = (col8 % 8 == row8).astype(F32)
    by_a = (col8 // 8 == row8).astype(F32)
    row64 = lax.broadcasted_iota(jnp.int32, (64, 8), 0)
    col64 = lax.broadcasted_iota(jnp.int32, (64, 8), 1)
    by_b_t = (row64 % 8 == col64).astype(F32)
    by_a_t = (row64 // 8 == col64).astype(F32)
    dot = functools.partial(jnp.dot, precision=HIGH, preferred_element_type=F32)

    q_sent, y_sent, z_sent = [], [], []

    def send_queries():
        for i in range(1, 16):
            cp = pltpu.make_async_remote_copy(
                src_ref=q_hbm, dst_ref=qbuf.at[dp], send_sem=ss_q.at[i], recv_sem=rs_q.at[dp],
                device_id=((dp + i) % 16, tn), device_id_type=MESH,
            )
            cp.start()
            q_sent.append(cp)

    def input_part():
        load_li.wait()
        load_sin.wait()
        sign = (2 * sin[...] - 1).astype(F32).astype(BF16)
        ybuf[y] = lax.dot_general(sign, li[...], NT, preferred_element_type=F32) * D ** (-0.5)
        for i in range(1, 4):
            cp = pltpu.make_async_remote_copy(
                src_ref=ybuf.at[y], dst_ref=ybuf.at[y], send_sem=ss_y.at[i], recv_sem=rs_y.at[y],
                device_id=(dp, zh * 4 + (y + i) % 4), device_id_type=MESH,
            )
            cp.start()
            y_sent.append(cp)

    def input_sum():
        for i in range(1, 4):
            other = (y + i) % 4
            pltpu.make_async_remote_copy(
                src_ref=ybuf.at[other], dst_ref=ybuf.at[other], send_sem=ss_y.at[i], recv_sem=rs_y.at[other],
                device_id=(dp, tn), device_id_type=MESH,
            ).wait_recv()
        zbuf[zh] = ybuf[0] + ybuf[1] + ybuf[2] + ybuf[3]
        cp = pltpu.make_async_remote_copy(
            src_ref=zbuf.at[zh], dst_ref=zbuf.at[zh], send_sem=ss_z, recv_sem=rs_z,
            device_id=(dp, (1 - zh) * 4 + y), device_id_type=MESH,
        )
        cp.start()
        z_sent.append(cp)

    def input_weigh():
        other = 1 - zh
        pltpu.make_async_remote_copy(
            src_ref=zbuf.at[other], dst_ref=zbuf.at[other], send_sem=ss_z, recv_sem=rs_z,
            device_id=(dp, other * 4 + y), device_id_type=MESH,
        ).wait_recv()
        full = zbuf[0] + zbuf[1]
        pos = lax.broadcasted_iota(jnp.int32, (8, SLOTS), 1)
        for e in range(TOK // SLOTS):
            count = len_ref[e]
            scale = FF ** (-0.5) / count.astype(F32)
            part = full[:, e * SLOTS : (e + 1) * SLOTS]
            part = jnp.where(pos < count, part * scale, 0.0)
            in64[pl.ds(e * SLOTS, SLOTS), :] = dot(part.T, by_a)

    def hidden_signs():
        load_small[3].wait()
        sign = (2 * shid[...] - 1).astype(F32)
        s64[...] = jnp.dot(by_b_t.astype(BF16), sign.astype(BF16), preferred_element_type=F32).astype(BF16)

    def query_matrix():
        for cp in load_small[:3]:
            cp.wait()
        load_q.wait()
        for i in range(1, 16):
            other = (dp + i) % 16
            pltpu.make_async_remote_copy(
                src_ref=q_hbm, dst_ref=qbuf.at[other], send_sem=ss_q.at[i], recv_sem=rs_q.at[other],
                device_id=(dp, tn), device_id_type=MESH,
            ).wait_recv()
        for i in range(16):
            qfull[pl.ds(4 * i, 4), :] = qbuf[i]
        kron = dot(dot(by_a_t, bi[...]), by_a) * dot(dot(by_b_t, bo[...]), by_b)
        values = jnp.sum(dot(ev[...], by_b) * by_a, axis=0, keepdims=True)
        both = lax.dot_general(kron / (values + SHIFT), kron, NT, precision=HIGH, preferred_element_type=F32)
        mat[...] = jnp.zeros_like(mat)
        mat[pl.ds(0, 64), :] = dot(both, qfull[...])

    def finish(j, product):
        cols = pl.ds(j * BLOCK, BLOCK)
        g = gate[:, cols].astype(F32)
        up = (product * (g * (0.5 + 0.5 * jnp.tanh(0.5 * g)))).astype(BF16)
        part = lax.dot_general(up, s64[:, cols], NT, preferred_element_type=F32)
        if j == 0:
            out64[...] = part
        else:
            out64[...] += part

    def block(j):
        if j == 0:
            for cp in load_c:
                cp.wait()
            load_gate.wait()
        shared(j, 0)
        shared(j, 1)
        finish(j, lax.dot_general(ct[...], w[pl.ds(j * BLOCK, BLOCK), :], NT, preferred_element_type=F32))

    last = HID // BLOCK - 1
    last_rows = pl.ds(last * BLOCK, BLOCK)

    own[0].wait()
    hop1(0)
    hop1(1)
    own[1].wait()
    for k in range(N + 3):
        if k > 0 and k + 1 < N:
            hop1(k + 1)
        if k < N:
            for slot in (L, R, Z):
                arrive(k, slot)
            for src, to, dst in HOP2[STAGES[k][2]]:
                send(k, src, to, dst)
            share(k, 0)
        if 0 <= k - 1 < N:
            for slot in (FAR, ZL, ZR):
                arrive(k - 1, slot)
            send(k - 1, FAR, "z", ZF)
        if 0 <= k - 2 < N:
            arrive(k - 2, ZF)
            share(k - 2, 1)
        if k == 0:
            send_queries()
            input_part()
            hidden_signs()
        if k == 1:
            input_sum()
        if k == 2:
            input_weigh()
            query_matrix()
        if 0 <= k - 3 < last:
            block(k - 3)
        if k == N:
            for s in range(last, N):
                shared(s, 0)
            hid[...] = lax.dot_general(
                ct[:, pl.ds(0, 2048)], w[last_rows, pl.ds(0, 2048)], NT, preferred_element_type=F32
            )
    for s in range(last, N):
        shared(s, 1)
    finish(
        last,
        hid[...]
        + lax.dot_general(
            ct[:, pl.ds(2048, 2048)], w[last_rows, pl.ds(2048, 2048)], NT, preferred_element_type=F32
        ),
    )

    rows = [
        jnp.sum(in64[pl.ds(e * SLOTS, SLOTS), :] * out64[pl.ds(e * SLOTS, SLOTS), :], axis=0, keepdims=True)
        for e in range(TOK // SLOTS)
    ]
    gbuf[tn] = jnp.zeros((8, 128), F32)
    for e in range(TOK // SLOTS):
        gbuf[tn, pl.ds(e, 1), pl.ds(0, 64)] = rows[e]
    g_sent = []
    for i in range(1, 8):
        cp = pltpu.make_async_remote_copy(
            src_ref=gbuf.at[tn], dst_ref=gbuf.at[tn], send_sem=ss_g.at[i], recv_sem=rs_g.at[tn],
            device_id=(dp, (tn + i) % 8), device_id_type=MESH,
        )
        cp.start()
        g_sent.append(cp)
    for cp in sent + q_sent + y_sent + z_sent:
        cp.wait_send()
    for i in range(1, 8):
        other = (tn + i) % 8
        pltpu.make_async_remote_copy(
            src_ref=gbuf.at[other], dst_ref=gbuf.at[other], send_sem=ss_g.at[i], recv_sem=rs_g.at[other],
            device_id=(dp, tn), device_id_type=MESH,
        ).wait_recv()
    total = gbuf[0]
    for i in range(1, 8):
        total = total + gbuf[i]
    o_ref[...] = dot(total, mat[...])[:4, :]
    for cp in g_sent:
        cp.wait_send()


def on_device(
    layer_input, output_cotangent, gate_preact, down_weight, lengths, input_signs, hidden_signs,
    basis_in, basis_out, eigenvalues, query_grads,
):
    any_spec = pl.BlockSpec(memory_space=pl.ANY)
    vmem, dma = pltpu.VMEM, pltpu.SemaphoreType.DMA
    specs = [any_spec] * 11
    specs[4] = pl.BlockSpec(memory_space=pltpu.SMEM)
    return pl.pallas_call(
        kernel,
        out_shape=jax.ShapeDtypeStruct((4, 512), F32),
        in_specs=specs,
        out_specs=pl.BlockSpec(memory_space=pltpu.VMEM),
        scratch_shapes=[
            vmem((HID, D), BF16),
            vmem((TOK, D), BF16),
            vmem((TOK, HID), BF16),
            vmem((TOK, 512), BF16),
            vmem((8, 512), jnp.int32),
            vmem((8, HID), jnp.int32),
            vmem((8, 8), F32),
            vmem((8, 8), F32),
            vmem((8, 8), F32),
            vmem((16, 4, 512), F32),
            vmem((64, 512), F32),
            vmem((128, 512), F32),
            vmem((4, 8, TOK), F32),
            vmem((2, 8, TOK), F32),
            vmem((8, 8, 128), F32),
            vmem((TOK, 64), F32),
            vmem((64, HID), BF16),
            vmem((TOK, BLOCK), F32),
            vmem((TOK, 64), F32),
            dma((N, 8)), dma((N, 8)), dma((N, 2)), dma((N, 2)), dma((16,)), dma((16,)),
            dma((4,)), dma((4,)), dma, dma, dma((8,)), dma((8,)), dma((32,)),
        ],
        compiler_params=pltpu.CompilerParams(
            collective_id=0, has_side_effects=True, vmem_limit_bytes=56 * 1024 * 1024
        ),
        cost_estimate=pl.CostEstimate(flops=2 * TOK * HID * D, bytes_accessed=30_000_000, transcendentals=TOK * HID),
        name="scores",
    )(
        layer_input.reshape(TOK, 512),
        output_cotangent.reshape(TOK, D),
        gate_preact.reshape(TOK, HID),
        down_weight,
        lengths,
        input_signs.T,
        hidden_signs.T,
        basis_in,
        basis_out,
        eigenvalues,
        query_grads.T,
    )


def solution(mesh):
    in_specs = (
        P("dp", None, "tensor"),
        P("dp", None, None),
        P("dp", None, "tensor"),
        P("tensor", "dp"),
        P("dp"),
        P("tensor", None),
        P("tensor", None),
        P(),
        P(),
        P(),
        P("tensor", "dp"),
    )
    return jax.shard_map(
        on_device, mesh=mesh, in_specs=in_specs, out_specs=P("dp", "tensor"), check_vma=False
    )
```

```python
import functools

import jax
import jax.numpy as jnp
from jax import lax
from jax.experimental import pallas as pl
from jax.experimental.pallas import tpu as pltpu
from jax.sharding import PartitionSpec as P

MESH = pl.DeviceIdType.MESH
HIGH = lax.Precision.HIGHEST
F32, BF16 = jnp.float32, jnp.bfloat16
D, FF, RA, RG = 4096, 14336, 8, 8
SHIFT = 0.1
TOK, HID, COLS, SLOTS = 1024, 1792, 256, 256
BLOCK = 256
NT = (((1,), (1,)), ((), ()))

SIZES = (256, 256, 256, 256, 256, 256, 128, 64, 64)
N = len(SIZES)
STAGES = [(sum(SIZES[:i]), rows) for i, rows in enumerate(SIZES)]
LAST = HID // BLOCK - 1
IN_LAST = [i for i, (first, _) in enumerate(STAGES) if first >= LAST * BLOCK]
O, L, R, Z, FAR, ZL, ZR, ZF = range(8)


def split(rows):
    units = rows // 16
    return 16 * round(units * 5 / 6)


def copies(stage):
    rows = SIZES[stage]
    half, part = rows // 2, split(rows)
    return [
        (O, 0, rows, "xp", L),
        (O, 0, rows, "xm", R),
        (O, 0, rows, "z", Z),
        (L, 0, half, "xp", FAR),
        (R, half, rows, "xm", FAR),
        (Z, 0, part, "xp", ZL),
        (Z, 0, part, "xm", ZR),
        (L, part, rows, "z", ZL),
        (R, part, rows, "z", ZR),
        (FAR, 0, rows, "z", ZF),
    ]


HOP1, FROM_L, FROM_R, FROM_Z, HOP3 = (0, 1, 2), (3, 7), (4, 8), (5, 6), (9,)
TO_FAR, TO_ZLR = (3, 4), (5, 6, 7, 8)


def column(slot, sibling=0):
    return (slot // 4) * 2048 + sibling * 1024 + (slot % 4) * COLS


def kernel(
    li_hbm, ct_hbm, gate_hbm, w_hbm, len_ref, sin_hbm, shid_hbm, bi_hbm, bo_hbm, ev_hbm, q_hbm,
    o_ref,
    w, ct, gate, li, sin, shid, bi, bo, ev, qbuf, qfull, mat, ybuf, zbuf, gbuf, in64, s64, hid, out64,
    ss_w, rs_w, ss_s, rs_s, ss_q, rs_q, ss_y, rs_y, ss_z, rs_z, ss_g, rs_g, lsem,
):
    dp, tn = lax.axis_index("dp"), lax.axis_index("tensor")
    x, z, c = dp // 4, (dp // 2) % 2, dp % 2
    zh, y = tn // 4, tn % 4
    xp, xm = (x + 1) % 4, (x + 3) % 4
    at = lambda xx, zz, cc: xx * 4 + zz * 2 + cc
    dev = {
        "xp": (at(xp, z, c), tn),
        "xm": (at(xm, z, c), tn),
        "z": (at(x, 1 - z, c), tn),
        "sib": (at(x, z, 1 - c), tn),
    }

    loads = []

    def load(src, dst):
        cp = pltpu.make_async_copy(src, dst, lsem.at[len(loads)])
        loads.append(cp)
        cp.start()
        return cp

    own = [load(w_hbm.at[pl.ds(0, 512)], w.at[pl.ds(0, 512), pl.ds(0, COLS)])]
    own += [load(w_hbm.at[pl.ds(512, 1280)], w.at[pl.ds(512, 1280), pl.ds(0, COLS)])]

    barrier = pltpu.get_barrier_semaphore()
    for i in range(1, 16):
        pl.semaphore_signal(barrier, inc=1, device_id=((dp + i) % 16, tn), device_id_type=MESH)
    for i in range(1, 8):
        pl.semaphore_signal(barrier, inc=1, device_id=(dp, (tn + i) % 8), device_id_type=MESH)

    load_li = load(li_hbm, li)
    load_sin = load(sin_hbm, sin)
    load_q = load(q_hbm, qbuf.at[dp])
    load_small = [load(bi_hbm, bi), load(bo_hbm, bo), load(ev_hbm, ev), load(shid_hbm, shid)]
    load_c = []
    for half in range(2):
        cc = c if half == 0 else 1 - c
        for slot, (xx, zz) in enumerate(
            ((x, z), (xm, z), (xp, z), (x, 1 - z), ((x + 2) % 4, z), (xm, 1 - z), (xp, 1 - z), ((x + 2) % 4, 1 - z))
        ):
            first = pl.multiple_of(at(xx, zz, cc) * COLS, COLS)
            load_c.append(load(ct_hbm.at[:, pl.ds(first, COLS)], ct.at[:, pl.ds(column(slot, half), COLS)]))
    load_gate = load(gate_hbm, gate)

    pl.semaphore_wait(barrier, 22)

    def remote(stage, i):
        src, low, high, to, dst = copies(stage)[i]
        rows = pl.ds(STAGES[stage][0] + low, high - low)
        return pltpu.make_async_remote_copy(
            src_ref=w.at[rows, pl.ds(column(src), COLS)], dst_ref=w.at[rows, pl.ds(column(dst), COLS)],
            send_sem=ss_w.at[stage, i], recv_sem=rs_w.at[stage, i],
            device_id=dev[to], device_id_type=MESH,
        )

    def send(stage, which):
        for i in which:
            remote(stage, i).start()

    def arrive(stage, which):
        for i in which:
            remote(stage, i).wait_recv()

    def sent(stage):
        for i in range(10):
            remote(stage, i).wait_send()
        for group in range(2):
            share_copy(stage, group).wait_send()

    def share_copy(stage, group):
        first, rows = STAGES[stage]
        return pltpu.make_async_remote_copy(
            src_ref=w.at[pl.ds(first, rows), pl.ds(group * 2048, 1024)],
            dst_ref=w.at[pl.ds(first, rows), pl.ds(group * 2048 + 1024, 1024)],
            send_sem=ss_s.at[stage, group], recv_sem=rs_s.at[stage, group],
            device_id=dev["sib"], device_id_type=MESH,
        )

    def share(stage, group):
        share_copy(stage, group).start()

    def shared(stage, group):
        share_copy(stage, group).wait_recv()

    row8 = lax.broadcasted_iota(jnp.int32, (8, 64), 0)
    col8 = lax.broadcasted_iota(jnp.int32, (8, 64), 1)
    by_b = (col8 % 8 == row8).astype(F32)
    by_a = (col8 // 8 == row8).astype(F32)
    row64 = lax.broadcasted_iota(jnp.int32, (64, 8), 0)
    col64 = lax.broadcasted_iota(jnp.int32, (64, 8), 1)
    by_b_t = (row64 % 8 == col64).astype(F32)
    by_a_t = (row64 // 8 == col64).astype(F32)
    dot = functools.partial(jnp.dot, precision=HIGH, preferred_element_type=F32)

    def query_copy(i, owner):
        return pltpu.make_async_remote_copy(
            src_ref=q_hbm, dst_ref=qbuf.at[owner], send_sem=ss_q.at[i], recv_sem=rs_q.at[owner],
            device_id=((dp + i) % 16, tn), device_id_type=MESH,
        )

    def y_copy(i, owner):
        return pltpu.make_async_remote_copy(
            src_ref=ybuf.at[owner], dst_ref=ybuf.at[owner], send_sem=ss_y.at[i], recv_sem=rs_y.at[owner],
            device_id=(dp, zh * 4 + (y + i) % 4), device_id_type=MESH,
        )

    def z_copy(owner):
        return pltpu.make_async_remote_copy(
            src_ref=zbuf.at[owner], dst_ref=zbuf.at[owner], send_sem=ss_z, recv_sem=rs_z,
            device_id=(dp, (1 - zh) * 4 + y), device_id_type=MESH,
        )

    def send_queries():
        for i in range(1, 16):
            query_copy(i, dp).start()

    def input_part():
        load_li.wait()
        load_sin.wait()
        sign = (2 * sin[...] - 1).astype(F32).astype(BF16)
        ybuf[y] = lax.dot_general(sign, li[...], NT, preferred_element_type=F32) * D ** (-0.5)
        for i in range(1, 4):
            y_copy(i, y).start()

    def input_sum():
        for i in range(1, 4):
            y_copy(i, (y + i) % 4).wait_recv()
        zbuf[zh] = ybuf[0] + ybuf[1] + ybuf[2] + ybuf[3]
        z_copy(zh).start()

    def input_weigh():
        z_copy(1 - zh).wait_recv()
        full = zbuf[0] + zbuf[1]
        pos = lax.broadcasted_iota(jnp.int32, (8, SLOTS), 1)
        for e in range(TOK // SLOTS):
            count = len_ref[e]
            scale = FF ** (-0.5) / count.astype(F32)
            part = full[:, e * SLOTS : (e + 1) * SLOTS]
            part = jnp.where(pos < count, part * scale, 0.0)
            in64[pl.ds(e * SLOTS, SLOTS), :] = dot(part.T, by_a)

    def hidden_signs():
        load_small[3].wait()
        sign = (2 * shid[...] - 1).astype(F32)
        s64[...] = jnp.dot(by_b_t.astype(BF16), sign.astype(BF16), preferred_element_type=F32).astype(BF16)

    def query_matrix():
        for cp in load_small[:3]:
            cp.wait()
        load_q.wait()
        for i in range(1, 16):
            query_copy(i, (dp + i) % 16).wait_recv()
        for i in range(16):
            qfull[pl.ds(4 * i, 4), :] = qbuf[i]
        kron = dot(dot(by_a_t, bi[...]), by_a) * dot(dot(by_b_t, bo[...]), by_b)
        values = jnp.sum(dot(ev[...], by_b) * by_a, axis=0, keepdims=True)
        both = lax.dot_general(kron / (values + SHIFT), kron, NT, precision=HIGH, preferred_element_type=F32)
        mat[...] = jnp.zeros_like(mat)
        mat[pl.ds(0, 64), :] = dot(both, qfull[...])

    def first_half(j):
        rows = pl.ds(pl.multiple_of(j * BLOCK, BLOCK), BLOCK)
        hid[j % 4] = lax.dot_general(
            ct[:, pl.ds(0, 2048)], w[rows, pl.ds(0, 2048)], NT, preferred_element_type=F32
        )

    def second_half(j):
        rows = pl.ds(pl.multiple_of(j * BLOCK, BLOCK), BLOCK)
        product = hid[j % 4] + lax.dot_general(
            ct[:, pl.ds(2048, 2048)], w[rows, pl.ds(2048, 2048)], NT, preferred_element_type=F32
        )
        g = gate[:, rows].astype(F32)
        up = (product * (g * (0.5 + 0.5 * jnp.tanh(0.5 * g)))).astype(BF16)
        out64[...] += lax.dot_general(up, s64[:, rows], NT, preferred_element_type=F32)

    def step_a(k):
        if k + 1 < N:
            send(k + 1, HOP1)
        if k < N:
            arrive(k, (0,))
            send(k, FROM_L)
            arrive(k, (1,))
            send(k, FROM_R)
            arrive(k, (2,))
            send(k, FROM_Z)
            share(k, 0)
        if k == N - 1:
            for s in (k - 1, k):
                arrive(s, TO_FAR)
                send(s, HOP3)
        if k == 0:
            send_queries()
        if k == 1:
            for cp in load_c:
                cp.wait()
        if 1 <= k <= LAST:
            shared(k - 1, 0)
        if k == N - 1:
            for s in IN_LAST:
                shared(s, 0)

    def step_b(k):
        if k == 0:
            input_part()
            hidden_signs()
        if 1 <= k < N - 1:
            arrive(k - 1, TO_FAR)
            send(k - 1, HOP3)
        if k == 1:
            input_sum()
        if k == 2:
            input_weigh()
            load_gate.wait()
        if 3 <= k < N:
            shared(k - 3, 1)
        if k == N:
            for s in IN_LAST:
                shared(s, 1)

    def step_c(k):
        if 1 <= k < N:
            arrive(k - 1, TO_ZLR)
        if 2 <= k < N:
            arrive(k - 2, (9,))
            share(k - 2, 1)
        if k == N - 1:
            arrive(k, TO_ZLR)
            for s in (k - 1, k):
                arrive(s, (9,))
                share(s, 1)
        if k == 4:
            query_matrix()
        if 4 <= k < N:
            sent(k - 4)

    def step(k, _):
        def only(part):
            for i in range(N + 1):
                pl.when(k == i)(functools.partial(part, i))

        only(step_a)
        first = jnp.where(k == N - 1, LAST, jnp.where(k <= LAST, k - 1, -1))
        pl.when(first >= 0)(lambda: first_half(first))
        only(step_b)
        pl.when(k >= 3)(lambda: second_half(k - 3))
        only(step_c)
        return 0

    out64[...] = jnp.zeros_like(out64)
    own[0].wait()
    send(0, HOP1)
    own[1].wait()
    lax.fori_loop(0, N + 1, step, 0)

    rows = [
        jnp.sum(in64[pl.ds(e * SLOTS, SLOTS), :] * out64[pl.ds(e * SLOTS, SLOTS), :], axis=0, keepdims=True)
        for e in range(TOK // SLOTS)
    ]
    gbuf[tn] = jnp.zeros((8, 128), F32)
    for e in range(TOK // SLOTS):
        gbuf[tn, pl.ds(e, 1), pl.ds(0, 64)] = rows[e]
    g_sent = []
    for i in range(1, 8):
        cp = pltpu.make_async_remote_copy(
            src_ref=gbuf.at[tn], dst_ref=gbuf.at[tn], send_sem=ss_g.at[i], recv_sem=rs_g.at[tn],
            device_id=(dp, (tn + i) % 8), device_id_type=MESH,
        )
        cp.start()
        g_sent.append(cp)
    for s in range(N - 4, N):
        sent(s)
    for i in range(1, 16):
        query_copy(i, dp).wait_send()
    for i in range(1, 4):
        y_copy(i, y).wait_send()
    z_copy(zh).wait_send()
    for i in range(1, 8):
        other = (tn + i) % 8
        pltpu.make_async_remote_copy(
            src_ref=gbuf.at[other], dst_ref=gbuf.at[other], send_sem=ss_g.at[i], recv_sem=rs_g.at[other],
            device_id=(dp, tn), device_id_type=MESH,
        ).wait_recv()
    total = gbuf[0]
    for i in range(1, 8):
        total = total + gbuf[i]
    o_ref[...] = dot(total, mat[...])[:4, :]
    for cp in g_sent:
        cp.wait_send()


def on_device(
    layer_input, output_cotangent, gate_preact, down_weight, lengths, input_signs, hidden_signs,
    basis_in, basis_out, eigenvalues, query_grads,
):
    any_spec = pl.BlockSpec(memory_space=pl.ANY)
    vmem, dma = pltpu.VMEM, pltpu.SemaphoreType.DMA
    specs = [any_spec] * 11
    specs[4] = pl.BlockSpec(memory_space=pltpu.SMEM)
    return pl.pallas_call(
        kernel,
        out_shape=jax.ShapeDtypeStruct((4, 512), F32),
        in_specs=specs,
        out_specs=pl.BlockSpec(memory_space=pltpu.VMEM),
        scratch_shapes=[
            vmem((HID, D), BF16),
            vmem((TOK, D), BF16),
            vmem((TOK, HID), BF16),
            vmem((TOK, 512), BF16),
            vmem((8, 512), jnp.int32),
            vmem((8, HID), jnp.int32),
            vmem((8, 8), F32),
            vmem((8, 8), F32),
            vmem((8, 8), F32),
            vmem((16, 4, 512), F32),
            vmem((64, 512), F32),
            vmem((128, 512), F32),
            vmem((4, 8, TOK), F32),
            vmem((2, 8, TOK), F32),
            vmem((8, 8, 128), F32),
            vmem((TOK, 64), F32),
            vmem((64, HID), BF16),
            vmem((4, TOK, BLOCK), F32),
            vmem((TOK, 64), F32),
            dma((N, 10)), dma((N, 10)), dma((N, 2)), dma((N, 2)), dma((16,)), dma((16,)),
            dma((4,)), dma((4,)), dma, dma, dma((8,)), dma((8,)), dma((32,)),
        ],
        compiler_params=pltpu.CompilerParams(
            collective_id=0, has_side_effects=True, vmem_limit_bytes=56 * 1024 * 1024
        ),
        cost_estimate=pl.CostEstimate(flops=2 * TOK * HID * D, bytes_accessed=30_000_000, transcendentals=TOK * HID),
        name="scores",
    )(
        layer_input.reshape(TOK, 512),
        output_cotangent.reshape(TOK, D),
        gate_preact.reshape(TOK, HID),
        down_weight,
        lengths,
        input_signs.T,
        hidden_signs.T,
        basis_in,
        basis_out,
        eigenvalues,
        query_grads.T,
    )


def solution(mesh):
    in_specs = (
        P("dp", None, "tensor"),
        P("dp", None, None),
        P("dp", None, "tensor"),
        P("tensor", "dp"),
        P("dp"),
        P("tensor", None),
        P("tensor", None),
        P(),
        P(),
        P(),
        P("tensor", "dp"),
    )
    return jax.shard_map(
        on_device, mesh=mesh, in_specs=in_specs, out_specs=P("dp", "tensor"), check_vma=False
    )
```

```python
import functools

import jax
import jax.numpy as jnp
from jax import lax
from jax.experimental import pallas as pl
from jax.experimental.pallas import tpu as pltpu
from jax.sharding import PartitionSpec as P

MESH = pl.DeviceIdType.MESH
HIGH = lax.Precision.HIGHEST
F32, BF16 = jnp.float32, jnp.bfloat16
D, FF, RA, RG = 4096, 14336, 8, 8
SHIFT = 0.1
TOK, HID, COLS, SLOTS = 1024, 1792, 256, 256
BLOCK = 256
NT = (((1,), (1,)), ((), ()))

N = HID // BLOCK
ALONG_X = (14, 13, 13, 13, 14, 14, 13)
SCHEDULE = (
    (
        (
            (0, 0, 0), (0, 0, 1), (0, 0, 2), (0, 1, 0), (0, 1, 1), (0, 1, 2), (2, 1, 0), (2, 0, 0),
            (0, 2, 0), (0, 2, 1), (0, 2, 2), (0, 0, 3), (0, 0, 4), (0, 0, 9), (0, 0, 8), (0, 3, 2),
            (0, 3, 0), (0, 3, 1), (2, 2, 0), (0, 1, 9), (0, 1, 8), (0, 1, 3), (0, 1, 4), (0, 4, 2),
            (0, 2, 3), (0, 2, 4), (1, 0, 0), (2, 4, 0), (0, 4, 0), (0, 4, 1), (0, 0, 7),
        ),
        (0, 0),
    ),
    (
        (
            (0, 3, 3), (0, 3, 4), (0, 1, 7), (1, 1, 0), (2, 3, 0), (0, 0, 5), (0, 0, 6), (1, 2, 0),
            (0, 2, 7),
        ),
        (0, 1),
    ),
    (
        (
            (0, 4, 3), (0, 5, 0), (0, 4, 4), (0, 5, 1), (1, 0, 2),
        ),
        (0, 2),
    ),
    (
        (
            (0, 3, 7), (1, 3, 0), (0, 1, 5), (0, 1, 6), (1, 1, 2), (0, 2, 8), (1, 0, 1), (0, 2, 9),
        ),
        (0, 3),
    ),
    (
        (
            (0, 6, 0), (0, 6, 1), (0, 4, 7), (1, 2, 2), (1, 4, 0),
        ),
        (1, 0),
    ),
    (
        (
            (0, 5, 3), (0, 5, 4), (0, 5, 2), (1, 3, 2),
        ),
        (0, 4),
    ),
    (
        (
            (0, 2, 5), (0, 2, 6), (0, 3, 9), (0, 3, 8), (1, 1, 1), (0, 6, 2), (0, 3, 5), (0, 3, 6),
            (1, 4, 2),
        ),
        (1, 1),
    ),
    (
        (
            (0, 6, 3), (0, 6, 4), (0, 5, 7), (0, 4, 5), (0, 4, 6), (1, 5, 0), (1, 2, 1), (0, 4, 9),
            (0, 4, 8), (0, 5, 9), (0, 5, 5), (0, 5, 6), (0, 5, 8),
        ),
        (0, 5),
    ),
    (
        (
            (0, 6, 8), (0, 6, 9), (1, 3, 1),
        ),
        (1, 2),
    ),
    (
        (
            (0, 6, 5), (0, 6, 6), (0, 6, 7), (1, 6, 0),
        ),
        (1, 3),
    ),
    (
        (
            (1, 4, 1), (1, 5, 2),
        ),
        (0, 6),
    ),
    (
        (
            (1, 5, 1),
        ),
        (1, 4),
    ),
    (
        (
            (1, 6, 2), (1, 6, 1),
        ),
        (1, 5),
    ),
    (
        (
        ),
        (1, 6),
    ),
)
O, L, R, Z, FAR, ZL, ZR, ZF = range(8)


FAR_FIRST = (2, 1, 3, 0)


def copies(stage):
    rows, half = BLOCK, BLOCK // 2
    part = 16 * ALONG_X[stage]
    return [
        (O, 0, rows, "xp", L),
        (O, 0, rows, "xm", R),
        (O, 0, rows, "z", Z),
        (L, 0, half, "xp", FAR),
        (R, half, rows, "xm", FAR),
        (Z, 0, part, "xp", ZL),
        (Z, 0, part, "xm", ZR),
        (FAR, 0, rows, "z", ZF),
    ] + [(L, part, rows, "z", ZL), (R, part, rows, "z", ZR)] * (part < rows)


AFTER = ((), (), (), (0,), (1,), (2,), (2,), (3, 4), (0,), (1,))
GROUPS = ((0, 1280), (2560, 512), (3072, 256))
BROUGHT = ((0, 1, 2, 3, 4), (5, 6, 8, 9), (7,))


def plan():
    arrived, steps = set(), []
    for actions, _ in SCHEDULE:
        steps.append([])
        for what, at, which in actions:
            needed = ((AFTER, BROUGHT, ((),))[what])[which]
            new = [i for i in needed if i < len(copies(at)) and (at, i) not in arrived]
            arrived.update((at, i) for i in new)
            steps[-1].append((new, (what, at, which)))
    return steps


PLAN = plan()


def column(slot):
    return slot * COLS if slot < 5 else 2560 + (slot - 5) * COLS


def sibling_column(col):
    return col + (1280 if col < 1280 else 768)


def kernel(
    li_hbm, ct_hbm, gate_hbm, w_hbm, len_ref, sin_hbm, shid_hbm, bi_hbm, bo_hbm, ev_hbm, q_hbm,
    o_ref,
    w, ct, gate, li, sin, shid, bi, bo, ev, qbuf, qfull, mat, ybuf, zbuf, gbuf, in64, s64, hid, act, out64,
    ss_w, rs_w, ss_s, rs_s, ss_q, rs_q, ss_y, rs_y, ss_z, rs_z, ss_g, rs_g, lsem,
):
    dp, tn = lax.axis_index("dp"), lax.axis_index("tensor")
    x, z, c = dp // 4, (dp // 2) % 2, dp % 2
    zh, y = tn // 4, tn % 4
    xp, xm = (x + 1) % 4, (x + 3) % 4
    at = lambda xx, zz, cc: xx * 4 + zz * 2 + cc
    dev = {
        "xp": (at(xp, z, c), tn),
        "xm": (at(xm, z, c), tn),
        "z": (at(x, 1 - z, c), tn),
        "sib": (at(x, z, 1 - c), tn),
    }

    loads = []

    def load(src, dst):
        cp = pltpu.make_async_copy(src, dst, lsem.at[len(loads)])
        loads.append(cp)
        cp.start()
        return cp

    own = load(w_hbm, w.at[:, pl.ds(0, COLS)])

    barrier = pltpu.get_barrier_semaphore()
    for i in range(1, 16):
        pl.semaphore_signal(barrier, inc=1, device_id=((dp + i) % 16, tn), device_id_type=MESH)
    for i in range(1, 8):
        pl.semaphore_signal(barrier, inc=1, device_id=(dp, (tn + i) % 8), device_id_type=MESH)

    load_li = load(li_hbm, li)
    load_sin = load(sin_hbm, sin)
    load_q = load(q_hbm, qbuf.at[dp])
    load_small = [load(bi_hbm, bi), load(bo_hbm, bo), load(ev_hbm, ev), load(shid_hbm, shid)]
    load_c = []
    for half in range(2):
        cc = c if half == 0 else 1 - c
        for slot, (xx, zz) in enumerate(
            ((x, z), (xm, z), (xp, z), (x, 1 - z), ((x + 2) % 4, z), (xm, 1 - z), (xp, 1 - z), ((x + 2) % 4, 1 - z))
        ):
            first = pl.multiple_of(at(xx, zz, cc) * COLS, COLS)
            load_c.append(load(ct_hbm.at[:, pl.ds(first, COLS)], ct.at[:, pl.ds(sibling_column(column(slot)) if half else column(slot), COLS)]))
    load_gate = load(gate_hbm, gate)

    pl.semaphore_wait(barrier, 22)

    def remote(stage, i):
        src, low, high, to, dst = copies(stage)[i]
        rows = pl.ds(stage * BLOCK + low, high - low)
        return pltpu.make_async_remote_copy(
            src_ref=w.at[rows, pl.ds(column(src), COLS)], dst_ref=w.at[rows, pl.ds(column(dst), COLS)],
            send_sem=ss_w.at[stage, i], recv_sem=rs_w.at[stage, i],
            device_id=dev[to], device_id_type=MESH,
        )

    def share_copy(stage, group):
        rows = pl.ds(stage * BLOCK, BLOCK)
        col, cols = GROUPS[group]
        return pltpu.make_async_remote_copy(
            src_ref=w.at[rows, pl.ds(col, cols)], dst_ref=w.at[rows, pl.ds(sibling_column(col), cols)],
            send_sem=ss_s.at[stage, group], recv_sem=rs_s.at[stage, group],
            device_id=dev["sib"], device_id_type=MESH,
        )

    def shared(stage, group):
        share_copy(stage, group).wait_recv()

    def sent(stage):
        for i in range(len(copies(stage))):
            remote(stage, i).wait_send()
        for group in range(3):
            share_copy(stage, group).wait_send()

    row8 = lax.broadcasted_iota(jnp.int32, (8, 128), 0)
    col8 = lax.broadcasted_iota(jnp.int32, (8, 128), 1)
    by_b = (col8 % 8 == row8).astype(F32)
    by_a = (col8 % 64 // 8 == row8).astype(F32)
    row_t = lax.broadcasted_iota(jnp.int32, (128, 8), 0)
    col_t = lax.broadcasted_iota(jnp.int32, (128, 8), 1)
    by_b_t = (row_t % 8 == col_t).astype(F32)
    by_a_t = (row_t % 64 // 8 == col_t).astype(F32)
    dot = functools.partial(jnp.dot, precision=HIGH, preferred_element_type=F32)

    def query_copy(i, owner):
        return pltpu.make_async_remote_copy(
            src_ref=q_hbm, dst_ref=qbuf.at[owner], send_sem=ss_q.at[i], recv_sem=rs_q.at[owner],
            device_id=((dp + i) % 16, tn), device_id_type=MESH,
        )

    def y_copy(i, owner):
        return pltpu.make_async_remote_copy(
            src_ref=ybuf.at[owner], dst_ref=ybuf.at[owner], send_sem=ss_y.at[i], recv_sem=rs_y.at[owner],
            device_id=(dp, zh * 4 + (y + i) % 4), device_id_type=MESH,
        )

    def z_copy(owner):
        return pltpu.make_async_remote_copy(
            src_ref=zbuf.at[owner], dst_ref=zbuf.at[owner], send_sem=ss_z, recv_sem=rs_z,
            device_id=(dp, (1 - zh) * 4 + y), device_id_type=MESH,
        )

    def send_queries():
        for i in range(1, 16):
            query_copy(i, dp).start()

    def input_part():
        load_li.wait()
        load_sin.wait()
        sign = (2 * sin[...] - 1).astype(F32).astype(BF16)
        ybuf[y] = lax.dot_general(sign, li[...], NT, preferred_element_type=F32) * D ** (-0.5)
        for i in range(1, 4):
            y_copy(i, y).start()

    def input_sum():
        for i in range(1, 4):
            y_copy(i, (y + i) % 4).wait_recv()
        zbuf[zh] = ybuf[0] + ybuf[1] + ybuf[2] + ybuf[3]
        z_copy(zh).start()

    def input_weigh():
        z_copy(1 - zh).wait_recv()
        full = zbuf[0] + zbuf[1]
        pos = lax.broadcasted_iota(jnp.int32, (8, SLOTS), 1)
        for e in range(TOK // SLOTS):
            count = len_ref[e]
            scale = FF ** (-0.5) / count.astype(F32)
            part = full[:, e * SLOTS : (e + 1) * SLOTS]
            part = jnp.where(pos < count, part * scale, 0.0)
            in64[pl.ds(e * SLOTS, SLOTS), :] = dot(part.T, by_a)

    def hidden_signs():
        load_small[3].wait()
        sign = (2 * shid[...] - 1).astype(F32)
        s64[...] = jnp.dot(by_b_t.astype(BF16), sign.astype(BF16), preferred_element_type=F32).astype(BF16)

    def query_matrix():
        for cp in load_small[:3]:
            cp.wait()
        load_q.wait()
        for i in range(1, 16):
            query_copy(i, (dp + i) % 16).wait_recv()
        for i in range(16):
            qfull[pl.ds(4 * i, 4), :] = qbuf[i]
        kron = dot(dot(by_a_t, bi[...]), by_a[:, :64]) * dot(dot(by_b_t, bo[...]), by_b[:, :64])
        values = jnp.sum(dot(ev[...], by_b[:, :64]) * by_a[:, :64], axis=0, keepdims=True)
        both = lax.dot_general(kron / (values + SHIFT), kron[:64], NT, precision=HIGH, preferred_element_type=F32)
        twice = dot(both, qfull[...])
        top = twice.astype(BF16)
        rest = (twice - top.astype(F32)).astype(BF16)
        both_parts = jnp.concatenate([top[:64], rest[:64]], axis=0)
        mat[pl.ds(0, 128), :] = both_parts
        mat[pl.ds(128, 128), :] = both_parts

    def first_part(j):
        rows = pl.ds(pl.multiple_of(j * BLOCK, BLOCK), BLOCK)
        hid[j % 4] = lax.dot_general(
            ct[:, pl.ds(0, 2560)], w[rows, pl.ds(0, 2560)], NT, preferred_element_type=F32
        )
        g = gate[:, rows].astype(F32)
        act[j % 4] = g * (0.5 + 0.5 * jnp.tanh(0.5 * g))

    def second_part(j):
        rows = pl.ds(pl.multiple_of(j * BLOCK, BLOCK), BLOCK)
        product = hid[j % 4] + lax.dot_general(
            ct[:, pl.ds(2560, 1536)], w[rows, pl.ds(2560, 1536)], NT, preferred_element_type=F32
        )
        up = (product * act[j % 4]).astype(BF16)
        out64[...] += lax.dot_general(up, s64[:, rows], NT, preferred_element_type=F32)

    def step_actions(i):
        part, j = SCHEDULE[i][1]
        for arrivals, (what, at, which) in PLAN[i]:
            for copy in arrivals:
                remote(at, copy).wait_recv()
            if what == 0:
                remote(at, which).start()
            elif what == 1:
                share_copy(at, which).start()
            else:
                small[at]()
        if i == len(SCHEDULE) - 1:
            for stage in range(5):
                sent(stage)
        if part == 0 and j == 0:
            for cp in load_c:
                cp.wait()
            load_gate.wait()
        for group in ((0,), (1, 2))[part]:
            shared(j, group)

    def block_of(step, part):
        j = jnp.int32(-1)
        for i, (_, (which, block)) in enumerate(SCHEDULE):
            if which == part:
                j = jnp.where(step == i, block, j)
        return j

    def step(k, _):
        for i in range(len(SCHEDULE)):
            pl.when(k == i)(functools.partial(step_actions, i))
        first, second = block_of(k, 0), block_of(k, 1)
        pl.when(first >= 0)(lambda: first_part(first))
        pl.when(second >= 0)(lambda: second_part(second))
        return 0

    def input_start():
        send_queries()
        input_part()

    small = (input_start, hidden_signs, input_sum, input_weigh, query_matrix)
    out64[...] = jnp.zeros_like(out64)
    own.wait()
    lax.fori_loop(0, len(SCHEDULE), step, 0)

    rows = [
        jnp.sum(in64[pl.ds(e * SLOTS, SLOTS), :] * out64[pl.ds(e * SLOTS, SLOTS), :], axis=0, keepdims=True)
        for e in range(TOK // SLOTS)
    ]
    gbuf[tn] = jnp.zeros((8, 128), F32)
    for e in range(TOK // SLOTS):
        gbuf[tn, pl.ds(e, 1), :] = rows[e]

    def g_copy(i, owner):
        return pltpu.make_async_remote_copy(
            src_ref=gbuf.at[owner], dst_ref=gbuf.at[owner], send_sem=ss_g.at[i], recv_sem=rs_g.at[owner],
            device_id=(dp, (zh + 1 - i // 4) % 2 * 4 + (y + FAR_FIRST[i % 4]) % 4), device_id_type=MESH,
        )

    for i in range(7):
        g_copy(i, tn).start()
    for stage in range(5, N):
        sent(stage)
    for i in range(1, 16):
        query_copy(i, dp).wait_send()
    for i in range(1, 4):
        y_copy(i, y).wait_send()
    z_copy(zh).wait_send()
    for i in range(1, 8):
        g_copy(0, (tn + i) % 8).wait_recv()
    total = gbuf[0]
    for i in range(1, 8):
        total = total + gbuf[i]
    top = total.astype(BF16)
    rest = (total - top.astype(F32)).astype(BF16)
    both = jnp.concatenate([top, rest], axis=1)
    o_ref[...] = jnp.dot(both, mat[...], preferred_element_type=F32)[:4, :]
    for i in range(7):
        g_copy(i, tn).wait_send()


def on_device(
    layer_input, output_cotangent, gate_preact, down_weight, lengths, input_signs, hidden_signs,
    basis_in, basis_out, eigenvalues, query_grads,
):
    any_spec = pl.BlockSpec(memory_space=pl.ANY)
    vmem, dma = pltpu.VMEM, pltpu.SemaphoreType.DMA
    specs = [any_spec] * 11
    specs[4] = pl.BlockSpec(memory_space=pltpu.SMEM)
    return pl.pallas_call(
        kernel,
        out_shape=jax.ShapeDtypeStruct((4, 512), F32),
        in_specs=specs,
        out_specs=pl.BlockSpec(memory_space=pltpu.VMEM),
        scratch_shapes=[
            vmem((HID, D), BF16),
            vmem((TOK, D), BF16),
            vmem((TOK, HID), BF16),
            vmem((TOK, 512), BF16),
            vmem((8, 512), jnp.int32),
            vmem((8, HID), jnp.int32),
            vmem((8, 8), F32),
            vmem((8, 8), F32),
            vmem((8, 8), F32),
            vmem((16, 4, 512), F32),
            vmem((64, 512), F32),
            vmem((256, 512), BF16),
            vmem((4, 8, TOK), F32),
            vmem((2, 8, TOK), F32),
            vmem((8, 8, 128), F32),
            vmem((TOK, 128), F32),
            vmem((128, HID), BF16),
            vmem((4, TOK, BLOCK), F32),
            vmem((4, TOK, BLOCK), F32),
            vmem((TOK, 128), F32),
            dma((N, 10)), dma((N, 10)), dma((N, 3)), dma((N, 3)), dma((16,)), dma((16,)),
            dma((4,)), dma((4,)), dma, dma, dma((8,)), dma((8,)), dma((32,)),
        ],
        compiler_params=pltpu.CompilerParams(
            collective_id=0, has_side_effects=True, vmem_limit_bytes=56 * 1024 * 1024
        ),
        cost_estimate=pl.CostEstimate(flops=2 * TOK * HID * D, bytes_accessed=30_000_000, transcendentals=TOK * HID),
        name="scores",
    )(
        layer_input.reshape(TOK, 512),
        output_cotangent.reshape(TOK, D),
        gate_preact.reshape(TOK, HID),
        down_weight,
        lengths,
        input_signs.T,
        hidden_signs.T,
        basis_in,
        basis_out,
        eigenvalues,
        query_grads.T,
    )


def solution(mesh):
    in_specs = (
        P("dp", None, "tensor"),
        P("dp", None, None),
        P("dp", None, "tensor"),
        P("tensor", "dp"),
        P("dp"),
        P("tensor", None),
        P("tensor", None),
        P(),
        P(),
        P(),
        P("tensor", "dp"),
    )
    return jax.shard_map(
        on_device, mesh=mesh, in_specs=in_specs, out_specs=P("dp", "tensor"), check_vma=False
    )
```

```python
import functools

import jax
import jax.numpy as jnp
from jax import lax
from jax.experimental import pallas as pl
from jax.experimental.pallas import tpu as pltpu
from jax.sharding import PartitionSpec as P

MESH = pl.DeviceIdType.MESH
HIGH = lax.Precision.HIGHEST
F32, BF16 = jnp.float32, jnp.bfloat16
D, FF, RA, RG = 4096, 14336, 8, 8
SHIFT = 0.1
TOK, HID, COLS, SLOTS = 1024, 1792, 256, 256
BLOCK = 256
NT = (((1,), (1,)), ((), ()))

N = HID // BLOCK
PEER, GATES = N - 1, N
ALONG_X = (16, 16, 16, 16, 16)
SCHEDULE = (
    (
        (
            (0, 0, 0), (0, 0, 1), (0, 0, 2), (0, 6, 0), (0, 1, 0), (0, 1, 1), (0, 1, 2), (2, 0, 0),
            (0, 2, 0), (0, 2, 1), (0, 2, 2), (0, 7, 0), (0, 6, 1), (2, 3, 0), (0, 0, 5), (0, 0, 6),
            (0, 3, 2), (2, 1, 0), (2, 2, 0), (0, 7, 1), (0, 0, 3), (0, 0, 4), (0, 7, 4), (0, 7, 2),
            (0, 1, 3), (0, 1, 4), (2, 4, 0), (2, 5, 0), (0, 2, 3), (0, 2, 4), (0, 4, 2), (0, 7, 3),
            (0, 3, 0), (0, 3, 1), (1, 0, 1), (0, 7, 5), (1, 0, 0), (2, 6, 0), (0, 6, 2), (0, 4, 0),
            (0, 4, 1), (1, 1, 0),
        ),
        (0, 0),
    ),
    (
        (
            (0, 0, 7), (0, 0, 8), (0, 7, 6), (1, 2, 0),
        ),
        (0, 1),
    ),
    (
        (
            (0, 3, 3), (0, 3, 4), (0, 7, 7), (2, 7, 0), (0, 5, 0), (0, 5, 1), (0, 5, 2),
        ),
        (0, 2),
    ),
    (
        (
            (0, 4, 3), (0, 4, 4), (0, 6, 3), (1, 0, 2), (0, 1, 5), (0, 1, 6), (0, 1, 7), (1, 3, 0),
        ),
        (1, 0),
    ),
    (
        (
        ),
        (0, 3),
    ),
    (
        (
            (0, 5, 3), (0, 2, 5), (0, 5, 4), (0, 2, 6), (0, 2, 7), (1, 4, 0), (1, 6, 1), (1, 6, 2),
            (0, 3, 7), (0, 3, 5), (0, 3, 6), (1, 1, 1), (1, 1, 2),
        ),
        (0, 4),
    ),
    (
        (
            (0, 4, 7), (1, 5, 0),
        ),
        (1, 1),
    ),
    (
        (
            (0, 4, 5), (0, 4, 6), (1, 2, 2), (1, 6, 0), (1, 2, 1), (0, 5, 7),
        ),
        (0, 5),
    ),
    (
        (
            (0, 5, 5), (0, 5, 6), (1, 3, 2),
        ),
        (0, 6),
    ),
    (
        (
            (1, 3, 1),
        ),
        (1, 6),
    ),
    (
        (
            (1, 4, 2), (1, 4, 1),
        ),
        (1, 2),
    ),
    (
        (
            (1, 5, 2),
        ),
        (1, 3),
    ),
    (
        (
            (1, 5, 1),
        ),
        (1, 4),
    ),
    (
        (
        ),
        (1, 5),
    ),
)

O, L, R, FAR, Z, ZL, ZR, ZF = range(8)
FAR_FIRST = (2, 1, 3, 0)


def copies(stage):
    rows, half = BLOCK, BLOCK // 2
    hop1 = [(O, 0, rows, "xp", L), (O, 0, rows, "xm", R), (O, 0, rows, "z", Z)]
    far = [(L, 0, half, "xp", FAR), (R, half, rows, "xm", FAR)]
    if stage == 0:
        return hop1 + far + [
            (Z, 0, rows, "xp", ZL),
            (Z, 0, rows, "xm", ZR),
            (ZL, 0, half, "xp", ZF),
            (ZR, half, rows, "xm", ZF),
        ]
    if stage == PEER:
        return [(O, 0, rows, "cross", Z), (Z, 0, rows, "cross", O), (L, 0, rows, "cross", ZL), (ZL, 0, rows, "cross", L)]
    if stage == GATES:
        return [None] * 8
    part = 16 * ALONG_X[stage - 1]
    return hop1 + far + [
        (Z, 0, part, "xp", ZL),
        (Z, 0, part, "xm", ZR),
        (FAR, 0, rows, "z", ZF),
    ] + [(L, part, rows, "z", ZL), (R, part, rows, "z", ZR)] * (part < rows)


def after(stage, i):
    if stage == PEER:
        return [(0, j) for j in ((), (2,), (0, 1, 3, 4), (5, 6, 7, 8))[i]]
    if stage == GATES:
        return [(GATES, i - 4)] if i >= 4 else []
    if stage == 0:
        return [(0, j) for j in ((), (), (), (0,), (1,), (2,), (2,), (5,), (6,))[i]]
    return [(stage, j) for j in ((), (), (), (0,), (1,), (2,), (2,), (3, 4), (0,), (1,))[i]]


GROUPS = ((0, 1280), (2560, 512), (3072, 256))


def brought(stage, group):
    if stage == PEER:
        which = ((0, 1, 3), (2,), (2,))[group]
    elif stage == 0:
        which = ((0, 1, 2, 3, 4), (5, 6), (7, 8))[group]
    else:
        which = ((0, 1, 2, 3, 4), (5, 6, 8, 9), (7,))[group]
    return [(stage, i) for i in which if i < len(copies(stage))]


def plan():
    arrived, steps = set(), []
    for actions, (part, block) in SCHEDULE:
        steps.append([])
        for what, at, which in actions + ((3, part, block),):
            needed = ()
            if what == 0:
                needed = after(at, which)
            elif what == 1:
                needed = brought(at, which)
            elif what == 3 and part == 0 and block == PEER:
                needed = [(GATES, i) for i in range(4, 8)]
            new = [x for x in needed if x not in arrived]
            arrived.update(new)
            steps[-1].append((new, (what, at, which)))
    return steps


PLAN = plan()


def column(slot):
    return slot * COLS if slot < 5 else 2560 + (slot - 5) * COLS


def sibling_column(col):
    return col + (1280 if col < 1280 else 768)


def kernel(
    li_hbm, ct_hbm, gate_hbm, w_hbm, len_ref, sin_hbm, shid_hbm, bi_hbm, bo_hbm, ev_hbm, q_hbm,
    o_ref,
    w, ct, gate, give_w, give_gate, relay, li, sin, shid, bi, bo, ev, qbuf, qfull, mat, ybuf, zbuf, gbuf, in64, s64, hid, act, out64,
    ss_w, rs_w, ss_s, rs_s, ss_q, rs_q, ss_y, rs_y, ss_z, rs_z, ss_h, rs_h, ss_g, rs_g, lsem,
):
    dp, tn = lax.axis_index("dp"), lax.axis_index("tensor")
    x, z, c = dp // 4, (dp // 2) % 2, dp % 2
    zh, y = tn // 4, tn % 4
    xp, xm = (x + 1) % 4, (x + 3) % 4
    at = lambda xx, zz, cc: xx * 4 + zz * 2 + cc
    dev = {
        "xp": (at(xp, z, c), tn),
        "xm": (at(xm, z, c), tn),
        "z": (at(x, 1 - z, c), tn),
        "sib": (at(x, z, 1 - c), tn),
        "cross": (at(x, 1 - z, c), (1 - zh) * 4 + y),
        "peer": (dp, (1 - zh) * 4 + y),
    }

    loads = []

    def load(src, dst):
        cp = pltpu.make_async_copy(src, dst, lsem.at[len(loads)])
        loads.append(cp)
        cp.start()
        return cp

    kept = pl.multiple_of((5 + z) * BLOCK, BLOCK)
    given = pl.multiple_of((6 - z) * BLOCK, BLOCK)
    plain = (N - 2) * BLOCK
    own = [
        load(w_hbm.at[pl.ds(kept, BLOCK)], w.at[pl.ds(0, BLOCK), pl.ds(0, COLS)]),
        load(w_hbm.at[pl.ds(given, BLOCK)], give_w),
        load(w_hbm.at[pl.ds(0, plain)], w.at[pl.ds(BLOCK, plain), pl.ds(0, COLS)]),
    ]

    barrier = pltpu.get_barrier_semaphore()
    for name in ("xp", "xm", "z", "sib", "cross"):
        pl.semaphore_signal(barrier, inc=1, device_id=dev[name], device_id_type=MESH)
    for i in range(1, 8):
        pl.semaphore_signal(barrier, inc=1, device_id=(dp, (tn + i) % 8), device_id_type=MESH)

    def quarter(i):
        return pl.ds(i * SLOTS, SLOTS)

    load_give = [load(gate_hbm.at[quarter(i), pl.ds(given, BLOCK)], give_gate.at[quarter(i)]) for i in range(4)]
    load_li = load(li_hbm, li)
    load_sin = load(sin_hbm, sin)
    q_me = c * 8 + z * 4 + x
    load_q = load(q_hbm, qbuf.at[q_me])
    load_small = [load(bi_hbm, bi), load(bo_hbm, bo), load(ev_hbm, ev)]
    load_shid = [
        load(shid_hbm.at[:, pl.ds(kept, BLOCK)], shid.at[:, pl.ds(0, BLOCK)]),
        load(shid_hbm.at[:, pl.ds(0, plain)], shid.at[:, pl.ds(BLOCK, plain)]),
    ]
    load_c = []
    for half in range(2):
        cc = c if half == 0 else 1 - c
        far = (x + 2) % 4
        for slot, (xx, zz) in enumerate(
            ((x, z), (xm, z), (xp, z), (far, z), (x, 1 - z), (xm, 1 - z), (xp, 1 - z), (far, 1 - z))
        ):
            first = pl.multiple_of(at(xx, zz, cc) * COLS, COLS)
            col = sibling_column(column(slot)) if half else column(slot)
            load_c.append(load(ct_hbm.at[:, pl.ds(first, COLS)], ct.at[:, pl.ds(col, COLS)]))
    load_gate = [
        load(gate_hbm.at[:, pl.ds(kept, BLOCK)], gate.at[:, pl.ds(0, BLOCK)]),
        load(gate_hbm.at[:, pl.ds(0, plain)], gate.at[:, pl.ds(BLOCK, plain)]),
    ]

    pl.semaphore_wait(barrier, 12)

    def remote(stage, i):
        if stage == GATES:
            rows = quarter(i % 4)
            to = ("cross", "z")[i // 4]
            src = (give_gate, relay)[i // 4].at[rows]
            dst = (relay.at[rows], gate.at[rows, pl.ds(PEER * BLOCK, BLOCK)])[i // 4]
        else:
            piece, low, high, to, there = copies(stage)[i]
            from_rows = pl.ds((0 if stage == PEER else stage * BLOCK) + low, high - low)
            rows = pl.ds(stage * BLOCK + low, high - low)
            cols = 3 * COLS if stage == PEER and i >= 2 else COLS
            src = w.at[from_rows, pl.ds(column(piece), cols)]
            if stage == 0 and i == 2:
                src = give_w
            dst = w.at[rows, pl.ds(column(there), cols)]
        return pltpu.make_async_remote_copy(
            src_ref=src, dst_ref=dst, send_sem=ss_w.at[stage, i], recv_sem=rs_w.at[stage, i],
            device_id=dev[to], device_id_type=MESH,
        )

    def share_copy(stage, group):
        rows = pl.ds(stage * BLOCK, BLOCK)
        col, cols = GROUPS[group]
        return pltpu.make_async_remote_copy(
            src_ref=w.at[rows, pl.ds(col, cols)], dst_ref=w.at[rows, pl.ds(sibling_column(col), cols)],
            send_sem=ss_s.at[stage, group], recv_sem=rs_s.at[stage, group],
            device_id=dev["sib"], device_id_type=MESH,
        )

    def shared(stage, group):
        share_copy(stage, group).wait_recv()

    def sent(stage):
        for i in range(len(copies(stage))):
            remote(stage, i).wait_send()
        for group in range(3 if stage < N else 0):
            share_copy(stage, group).wait_send()

    row8 = lax.broadcasted_iota(jnp.int32, (8, 128), 0)
    col8 = lax.broadcasted_iota(jnp.int32, (8, 128), 1)
    by_b = (col8 % 8 == row8).astype(F32)
    by_a = (col8 % 64 // 8 == row8).astype(F32)
    row_t = lax.broadcasted_iota(jnp.int32, (128, 8), 0)
    col_t = lax.broadcasted_iota(jnp.int32, (128, 8), 1)
    by_b_t = (row_t % 8 == col_t).astype(F32)
    by_a_t = (row_t % 64 // 8 == col_t).astype(F32)
    dot = functools.partial(jnp.dot, precision=HIGH, preferred_element_type=F32)

    def query_copy(i, receiving=False):
        mine = c * 8 + z * 4
        src, dst, to = (
            (q_hbm, qbuf.at[mine + (xm if receiving else x)], "xp"),
            (q_hbm, qbuf.at[mine + (xp if receiving else x)], "xm"),
            (qbuf.at[mine + xm], qbuf.at[mine + ((x + 2) % 4 if receiving else xm)], "xp"),
            (qbuf.at[pl.ds(mine, 4)], qbuf.at[pl.ds(c * 8 + (1 - z) * 4 if receiving else mine, 4)], "z"),
            (qbuf.at[pl.ds(c * 8, 8)], qbuf.at[pl.ds((1 - c) * 8 if receiving else c * 8, 8)], "sib"),
        )[i]
        return pltpu.make_async_remote_copy(
            src_ref=src, dst_ref=dst, send_sem=ss_q.at[i], recv_sem=rs_q.at[i],
            device_id=dev[to], device_id_type=MESH,
        )

    def query_far():
        query_copy(0, True).wait_recv()
        query_copy(2).start()

    def query_z():
        query_copy(1, True).wait_recv()
        query_copy(2, True).wait_recv()
        load_q.wait()
        query_copy(3).start()

    def query_sibling():
        query_copy(3, True).wait_recv()
        query_copy(4).start()

    def y_copy(i, owner):
        return pltpu.make_async_remote_copy(
            src_ref=ybuf.at[owner], dst_ref=ybuf.at[owner], send_sem=ss_y.at[i], recv_sem=rs_y.at[owner],
            device_id=(dp, zh * 4 + (y + i) % 4), device_id_type=MESH,
        )

    def z_copy(owner):
        return pltpu.make_async_remote_copy(
            src_ref=zbuf.at[owner], dst_ref=zbuf.at[owner], send_sem=ss_z, recv_sem=rs_z,
            device_id=(dp, (1 - zh) * 4 + y), device_id_type=MESH,
        )

    def signs_copy():
        return pltpu.make_async_remote_copy(
            src_ref=shid_hbm.at[:, pl.ds(given, BLOCK)], dst_ref=shid.at[:, pl.ds(PEER * BLOCK, BLOCK)],
            send_sem=ss_h, recv_sem=rs_h, device_id=dev["peer"], device_id_type=MESH,
        )

    def input_part():
        load_li.wait()
        load_sin.wait()
        sign = (2 * sin[...] - 1).astype(F32).astype(BF16)
        ybuf[y] = lax.dot_general(sign, li[...], NT, preferred_element_type=F32) * D ** (-0.5)
        for i in range(1, 4):
            y_copy(i, y).start()

    def input_sum():
        for i in range(1, 4):
            y_copy(i, (y + i) % 4).wait_recv()
        zbuf[zh] = ybuf[0] + ybuf[1] + ybuf[2] + ybuf[3]
        z_copy(zh).start()

    def input_weigh():
        z_copy(1 - zh).wait_recv()
        full = zbuf[0] + zbuf[1]
        pos = lax.broadcasted_iota(jnp.int32, (8, SLOTS), 1)
        for e in range(TOK // SLOTS):
            count = len_ref[e]
            scale = FF ** (-0.5) / count.astype(F32)
            part = full[:, e * SLOTS : (e + 1) * SLOTS]
            part = jnp.where(pos < count, part * scale, 0.0)
            in64[pl.ds(e * SLOTS, SLOTS), :] = dot(part.T, by_a)

    def hidden_signs():
        for cp in load_shid:
            cp.wait()
        signs_copy().wait_recv()
        sign = (2 * shid[...] - 1).astype(F32)
        s64[...] = jnp.dot(by_b_t.astype(BF16), sign.astype(BF16), preferred_element_type=F32).astype(BF16)

    def query_matrix():
        for cp in load_small:
            cp.wait()
        query_copy(4, True).wait_recv()
        for i in range(16):
            owner = i % 4 * 4 + i // 4 % 2 * 2 + i // 8
            qfull[pl.ds(4 * owner, 4), :] = qbuf[i]
        kron = dot(dot(by_a_t, bi[...]), by_a[:, :64]) * dot(dot(by_b_t, bo[...]), by_b[:, :64])
        values = jnp.sum(dot(ev[...], by_b[:, :64]) * by_a[:, :64], axis=0, keepdims=True)
        both = lax.dot_general(kron / (values + SHIFT), kron[:64], NT, precision=HIGH, preferred_element_type=F32)
        twice = dot(both, qfull[...])
        top = twice.astype(BF16)
        rest = (twice - top.astype(F32)).astype(BF16)
        both_parts = jnp.concatenate([top[:64], rest[:64]], axis=0)
        mat[pl.ds(0, 128), :] = both_parts
        mat[pl.ds(128, 128), :] = both_parts

    def first_part(j):
        rows = pl.ds(pl.multiple_of(j * BLOCK, BLOCK), BLOCK)
        hid[j] = lax.dot_general(
            ct[:, pl.ds(0, 2560)], w[rows, pl.ds(0, 2560)], NT, preferred_element_type=F32
        )
        g = gate[:, rows].astype(F32)
        act[j] = g * (0.5 + 0.5 * jnp.tanh(0.5 * g))

    def second_part(j):
        rows = pl.ds(pl.multiple_of(j * BLOCK, BLOCK), BLOCK)
        product = hid[j] + lax.dot_general(
            ct[:, pl.ds(2560, 1536)], w[rows, pl.ds(2560, 1536)], NT, preferred_element_type=F32
        )
        up = (product * act[j]).astype(BF16)
        out64[...] += lax.dot_general(up, s64[:, rows], NT, preferred_element_type=F32)

    def step_actions(i):
        part, j = SCHEDULE[i][1]
        for arrivals, (what, at, which) in PLAN[i]:
            for stage, copy in arrivals:
                remote(stage, copy).wait_recv()
            if what == 0:
                if at == GATES and which < 4:
                    load_give[which].wait()
                remote(at, which).start()
            elif what == 1:
                share_copy(at, which).start()
            elif what == 2:
                small[at]()
        if i == len(SCHEDULE) - 1:
            for stage in range(5):
                sent(stage)
        if i == 0:
            for cp in load_c + load_gate:
                cp.wait()
        for group in ((0,), (1, 2))[part]:
            shared(j, group)

    def block_of(step, part):
        j = jnp.int32(-1)
        for i, (_, (which, block)) in enumerate(SCHEDULE):
            if which == part:
                j = jnp.where(step == i, block, j)
        return j

    def step(k, _):
        for i in range(len(SCHEDULE)):
            pl.when(k == i)(functools.partial(step_actions, i))
        first, second = block_of(k, 0), block_of(k, 1)
        pl.when(first >= 0)(lambda: first_part(first))
        pl.when(second >= 0)(lambda: second_part(second))
        return 0

    def input_start():
        query_copy(0).start()
        query_copy(1).start()
        signs_copy().start()
        input_part()

    small = (
        input_start, query_far, input_sum, hidden_signs, query_z, input_weigh, query_sibling, query_matrix,
    )
    out64[...] = jnp.zeros_like(out64)
    for cp in own:
        cp.wait()
    lax.fori_loop(0, len(SCHEDULE), step, 0)

    rows = [
        jnp.sum(in64[pl.ds(e * SLOTS, SLOTS), :] * out64[pl.ds(e * SLOTS, SLOTS), :], axis=0, keepdims=True)
        for e in range(TOK // SLOTS)
    ]
    gbuf[tn] = jnp.zeros((8, 128), F32)
    for e in range(TOK // SLOTS):
        gbuf[tn, pl.ds(e, 1), :] = rows[e]

    def g_copy(i, owner):
        return pltpu.make_async_remote_copy(
            src_ref=gbuf.at[owner], dst_ref=gbuf.at[owner], send_sem=ss_g.at[i], recv_sem=rs_g.at[owner],
            device_id=(dp, (zh + 1 - i // 4) % 2 * 4 + (y + FAR_FIRST[i % 4]) % 4), device_id_type=MESH,
        )

    for i in range(7):
        g_copy(i, tn).start()
    for stage in range(5, N + 1):
        sent(stage)
    signs_copy().wait_send()
    for i in range(5):
        query_copy(i).wait_send()
    for i in range(1, 4):
        y_copy(i, y).wait_send()
    z_copy(zh).wait_send()
    for i in range(1, 8):
        g_copy(0, (tn + i) % 8).wait_recv()
    total = gbuf[0]
    for i in range(1, 8):
        total = total + gbuf[i]
    top = total.astype(BF16)
    rest = (total - top.astype(F32)).astype(BF16)
    both = jnp.concatenate([top, rest], axis=1)
    o_ref[...] = jnp.dot(both, mat[...], preferred_element_type=F32)[:4, :]
    for i in range(7):
        g_copy(i, tn).wait_send()


def on_device(
    layer_input, output_cotangent, gate_preact, down_weight, lengths, input_signs, hidden_signs,
    basis_in, basis_out, eigenvalues, query_grads,
):
    any_spec = pl.BlockSpec(memory_space=pl.ANY)
    vmem, dma = pltpu.VMEM, pltpu.SemaphoreType.DMA
    specs = [any_spec] * 11
    specs[4] = pl.BlockSpec(memory_space=pltpu.SMEM)
    return pl.pallas_call(
        kernel,
        out_shape=jax.ShapeDtypeStruct((4, 512), F32),
        in_specs=specs,
        out_specs=pl.BlockSpec(memory_space=pltpu.VMEM),
        scratch_shapes=[
            vmem((HID, D), BF16),
            vmem((TOK, D), BF16),
            vmem((TOK, HID), BF16),
            vmem((BLOCK, COLS), BF16),
            vmem((TOK, BLOCK), BF16),
            vmem((TOK, BLOCK), BF16),
            vmem((TOK, 512), BF16),
            vmem((8, 512), jnp.int32),
            vmem((8, HID), jnp.int32),
            vmem((8, 8), F32),
            vmem((8, 8), F32),
            vmem((8, 8), F32),
            vmem((16, 4, 512), F32),
            vmem((64, 512), F32),
            vmem((256, 512), BF16),
            vmem((4, 8, TOK), F32),
            vmem((2, 8, TOK), F32),
            vmem((8, 8, 128), F32),
            vmem((TOK, 128), F32),
            vmem((128, HID), BF16),
            vmem((N, TOK, BLOCK), F32),
            vmem((N, TOK, BLOCK), F32),
            vmem((TOK, 128), F32),
            dma((N + 1, 10)), dma((N + 1, 10)), dma((N, 3)), dma((N, 3)), dma((5,)), dma((5,)),
            dma((4,)), dma((4,)), dma, dma, dma, dma, dma((8,)), dma((8,)), dma((40,)),
        ],
        compiler_params=pltpu.CompilerParams(
            collective_id=0, has_side_effects=True, vmem_limit_bytes=56 * 1024 * 1024
        ),
        cost_estimate=pl.CostEstimate(flops=2 * TOK * HID * D, bytes_accessed=30_000_000, transcendentals=TOK * HID),
        name="scores",
    )(
        layer_input.reshape(TOK, 512),
        output_cotangent.reshape(TOK, D),
        gate_preact.reshape(TOK, HID),
        down_weight,
        lengths,
        input_signs.T,
        hidden_signs.T,
        basis_in,
        basis_out,
        eigenvalues,
        query_grads.T,
    )


def solution(mesh):
    in_specs = (
        P("dp", None, "tensor"),
        P("dp", None, None),
        P("dp", None, "tensor"),
        P("tensor", "dp"),
        P("dp"),
        P("tensor", None),
        P("tensor", None),
        P(),
        P(),
        P(),
        P("tensor", "dp"),
    )
    return jax.shard_map(
        on_device, mesh=mesh, in_specs=in_specs, out_specs=P("dp", "tensor"), check_vma=False
    )
```

```python
import functools

import jax
import jax.numpy as jnp
from jax import lax
from jax.experimental import pallas as pl
from jax.experimental.pallas import tpu as pltpu
from jax.sharding import PartitionSpec as P

MESH = pl.DeviceIdType.MESH
HIGH = lax.Precision.HIGHEST
F32, BF16 = jnp.float32, jnp.bfloat16
D, FF, RA, RG = 4096, 14336, 8, 8
SHIFT = 0.1
TOK, HID, COLS, SLOTS = 1024, 1792, 256, 256
BLOCK = 256
NT = (((1,), (1,)), ((), ()))

N = HID // BLOCK
PEER, GATES = N - 1, N
ALONG_X = (15, 15, 16, 16, 16)
SCHEDULE = (
    (
        (
            (0, 0, 0), (0, 1, 0), (0, 0, 1), (0, 1, 1), (0, 0, 2), (0, 1, 2), (0, 6, 0), (2, 0, 0),
            (0, 2, 0), (0, 2, 1), (0, 2, 2), (0, 7, 0), (0, 7, 1), (2, 2, 0), (0, 0, 3), (0, 0, 4),
            (0, 3, 2), (0, 6, 1), (0, 0, 5), (0, 0, 6), (2, 1, 0), (2, 3, 0), (0, 7, 4), (0, 7, 2),
            (0, 1, 4), (0, 1, 3), (0, 2, 4), (0, 2, 3), (2, 5, 0), (0, 7, 5), (0, 6, 2), (1, 0, 0),
            (0, 3, 1), (0, 3, 0), (0, 4, 2), (1, 0, 1), (2, 4, 0),
        ),
        (0, 0),
    ),
    (
        (
            (0, 0, 7), (0, 0, 8), (0, 4, 1), (1, 1, 0), (0, 4, 0), (1, 2, 0), (0, 7, 6),
        ),
        (0, 1),
    ),
    (
        (
            (0, 3, 3), (0, 5, 0), (0, 3, 4), (0, 5, 1), (0, 1, 7), (0, 7, 3),
        ),
        (0, 2),
    ),
    (
        (
            (0, 6, 3), (1, 0, 2), (0, 5, 2), (2, 6, 0), (0, 1, 6), (0, 1, 5),
        ),
        (1, 0),
    ),
    (
        (
            (0, 1, 8), (0, 1, 9), (1, 3, 0), (1, 6, 1), (1, 6, 2), (0, 4, 3), (0, 4, 4), (0, 2, 7),
            (2, 7, 0), (0, 5, 3), (0, 5, 4), (1, 1, 2),
        ),
        (0, 3),
    ),
    (
        (
            (0, 2, 5), (0, 2, 6), (0, 7, 7), (1, 1, 1), (0, 3, 6), (0, 3, 5), (0, 2, 8), (0, 2, 9),
            (0, 3, 7), (1, 4, 0),
        ),
        (1, 1),
    ),
    (
        (
            (1, 2, 2), (1, 5, 0), (0, 4, 6), (0, 4, 5),
        ),
        (0, 4),
    ),
    (
        (
            (0, 4, 7), (1, 6, 0),
        ),
        (0, 5),
    ),
    (
        (
            (0, 5, 5), (0, 5, 6), (0, 5, 7), (1, 2, 1),
        ),
        (2, 6),
    ),
    (
        (
            (1, 3, 1), (1, 3, 2), (1, 4, 1),
        ),
        (1, 2),
    ),
    (
        (
            (1, 4, 2),
        ),
        (1, 3),
    ),
    (
        (
            (1, 5, 1), (1, 5, 2),
        ),
        (1, 4),
    ),
    (
        (
        ),
        (1, 5),
    ),
)

O, L, R, FAR, Z, ZL, ZR, ZF = range(8)
FAR_FIRST = (2, 1, 3, 0)


def copies(stage):
    rows, half = BLOCK, BLOCK // 2
    hop1 = [(O, 0, rows, "xp", L), (O, 0, rows, "xm", R), (O, 0, rows, "z", Z)]
    far = [(L, 0, half, "xp", FAR), (R, half, rows, "xm", FAR)]
    if stage == 0:
        return hop1 + far + [
            (Z, 0, rows, "xp", ZL),
            (Z, 0, rows, "xm", ZR),
            (ZL, 0, half, "xp", ZF),
            (ZR, half, rows, "xm", ZF),
        ]
    if stage == PEER:
        return [(O, 0, rows, "cross", Z), (Z, 0, rows, "cross", O), (L, 0, rows, "cross", ZL), (ZL, 0, rows, "cross", L)]
    if stage == GATES:
        return [None] * 8
    part = 16 * ALONG_X[stage - 1]
    return hop1 + far + [
        (Z, 0, part, "xp", ZL),
        (Z, 0, part, "xm", ZR),
        (FAR, 0, rows, "z", ZF),
    ] + [(L, part, rows, "z", ZL), (R, part, rows, "z", ZR)] * (part < rows)


def after(stage, i):
    if stage == PEER:
        return [(0, j) for j in ((), (2,), (0, 1, 3, 4), (5, 6, 7, 8))[i]]
    if stage == GATES:
        return [(GATES, i - 4)] if i >= 4 else []
    if stage == 0:
        return [(0, j) for j in ((), (), (), (0,), (1,), (2,), (2,), (5,), (6,))[i]]
    return [(stage, j) for j in ((), (), (), (0,), (1,), (2,), (2,), (3, 4), (0,), (1,))[i]]


GROUPS = ((0, 1280), (2560, 512), (3072, 256))


def brought(stage, group):
    if stage == PEER:
        which = ((0, 1, 3), (2,), (2,))[group]
    elif stage == 0:
        which = ((0, 1, 2, 3, 4), (5, 6), (7, 8))[group]
    else:
        which = ((0, 1, 2, 3, 4), (5, 6, 8, 9), (7,))[group]
    return [(stage, i) for i in which if i < len(copies(stage))]


def plan():
    arrived, steps = set(), []
    for actions, (part, block) in SCHEDULE:
        steps.append([])
        for what, at, which in actions + ((3, part, block),):
            needed = ()
            if what == 0:
                needed = after(at, which)
            elif what == 1:
                needed = brought(at, which)
            elif what == 3 and part != 1 and block == PEER:
                needed = [(GATES, i) for i in range(4, 8)]
            new = [x for x in needed if x not in arrived]
            arrived.update(new)
            steps[-1].append((new, (what, at, which)))
    return steps


PLAN = plan()
EARLY = [what == 0 and at == 0 and not new for new, (what, at, _) in PLAN[0]].index(False)


def column(slot):
    return slot * COLS if slot < 5 else 2560 + (slot - 5) * COLS


def sibling_column(col):
    return col + (1280 if col < 1280 else 768)


def kernel(
    li_hbm, ct_hbm, gate_hbm, w_hbm, len_ref, sin_hbm, shid_hbm, bi_hbm, bo_hbm, ev_hbm, q_hbm,
    o_ref,
    w, ct, gate, give_w, give_gate, relay, li, sin, shid, bi, bo, ev, qbuf, qfull, mat, ybuf, zbuf, gbuf, in64, s64, hid, act, out64,
    ss_w, rs_w, ss_s, rs_s, ss_q, rs_q, ss_y, rs_y, ss_z, rs_z, ss_h, rs_h, ss_g, rs_g, lsem,
):
    dp, tn = lax.axis_index("dp"), lax.axis_index("tensor")
    x, z, c = dp // 4, (dp // 2) % 2, dp % 2
    zh, y = tn // 4, tn % 4
    xp, xm = (x + 1) % 4, (x + 3) % 4
    at = lambda xx, zz, cc: xx * 4 + zz * 2 + cc
    dev = {
        "xp": (at(xp, z, c), tn),
        "xm": (at(xm, z, c), tn),
        "z": (at(x, 1 - z, c), tn),
        "sib": (at(x, z, 1 - c), tn),
        "cross": (at(x, 1 - z, c), (1 - zh) * 4 + y),
        "peer": (dp, (1 - zh) * 4 + y),
    }

    kept = pl.multiple_of((5 + z) * BLOCK, BLOCK)
    given = pl.multiple_of((6 - z) * BLOCK, BLOCK)
    plain = (N - 2) * BLOCK
    q_me = c * 8 + z * 4 + x

    def quarter(i):
        return pl.ds(i * SLOTS, SLOTS)

    def loads():
        found, count = {}, 0

        def load(name, src, dst):
            nonlocal count
            found.setdefault(name, []).append(functools.partial(pltpu.make_async_copy, src, dst, lsem.at[count]))
            count += 1

        load("own", w_hbm.at[pl.ds(kept, BLOCK)], w.at[pl.ds(0, BLOCK), pl.ds(0, COLS)])
        load("own", w_hbm.at[pl.ds(given, BLOCK)], give_w)
        load("plain", w_hbm.at[pl.ds(0, plain)], w.at[pl.ds(BLOCK, plain), pl.ds(0, COLS)])
        for i in range(4):
            load("give", gate_hbm.at[quarter(i), pl.ds(given, BLOCK)], give_gate.at[quarter(i)])
        load("input", li_hbm, li)
        load("input", sin_hbm, sin)
        load("query", q_hbm, qbuf.at[q_me])
        load("signs", shid_hbm.at[:, pl.ds(kept, BLOCK)], shid.at[:, pl.ds(0, BLOCK)])
        load("signs", shid_hbm.at[:, pl.ds(0, plain)], shid.at[:, pl.ds(BLOCK, plain)])
        for half in range(2):
            cc = c if half == 0 else 1 - c
            far = (x + 2) % 4
            for slot, (xx, zz) in enumerate(
                ((x, z), (xm, z), (xp, z), (far, z), (x, 1 - z), (xm, 1 - z), (xp, 1 - z), (far, 1 - z))
            ):
                first = pl.multiple_of(at(xx, zz, cc) * COLS, COLS)
                col = sibling_column(column(slot)) if half else column(slot)
                load("c", ct_hbm.at[:, pl.ds(first, COLS)], ct.at[:, pl.ds(col, COLS)])
        load("gate", gate_hbm.at[:, pl.ds(kept, BLOCK)], gate.at[:, pl.ds(0, BLOCK)])
        load("gate", gate_hbm.at[:, pl.ds(0, plain)], gate.at[:, pl.ds(BLOCK, plain)])
        for src, dst in ((bi_hbm, bi), (bo_hbm, bo), (ev_hbm, ev)):
            load("small", src, dst)
        return found

    def start(*names):
        for name in names:
            for make in loads()[name]:
                make().start()

    def loaded(*names):
        for name in names:
            for make in loads()[name]:
                make().wait()

    start("own", "plain")
    barrier = pltpu.get_barrier_semaphore()
    for name in ("xp", "xm", "z", "sib", "cross"):
        pl.semaphore_signal(barrier, inc=1, device_id=dev[name], device_id_type=MESH)
    for i in range(1, 8):
        pl.semaphore_signal(barrier, inc=1, device_id=(dp, (tn + i) % 8), device_id_type=MESH)
    pl.semaphore_wait(barrier, 12)
    loaded("own")

    def remote(stage, i):
        if stage == GATES:
            rows = quarter(i % 4)
            to = ("cross", "z")[i // 4]
            src = (give_gate, relay)[i // 4].at[rows]
            dst = (relay.at[rows], gate.at[rows, pl.ds(PEER * BLOCK, BLOCK)])[i // 4]
        else:
            piece, low, high, to, there = copies(stage)[i]
            from_rows = pl.ds((0 if stage == PEER else stage * BLOCK) + low, high - low)
            rows = pl.ds(stage * BLOCK + low, high - low)
            cols = 3 * COLS if stage == PEER and i >= 2 else COLS
            src = w.at[from_rows, pl.ds(column(piece), cols)]
            if stage == 0 and i == 2:
                src = give_w
            dst = w.at[rows, pl.ds(column(there), cols)]
        return pltpu.make_async_remote_copy(
            src_ref=src, dst_ref=dst, send_sem=ss_w.at[stage, i], recv_sem=rs_w.at[stage, i],
            device_id=dev[to], device_id_type=MESH,
        )

    def share_copy(stage, group):
        rows = pl.ds(stage * BLOCK, BLOCK)
        col, cols = GROUPS[group]
        return pltpu.make_async_remote_copy(
            src_ref=w.at[rows, pl.ds(col, cols)], dst_ref=w.at[rows, pl.ds(sibling_column(col), cols)],
            send_sem=ss_s.at[stage, group], recv_sem=rs_s.at[stage, group],
            device_id=dev["sib"], device_id_type=MESH,
        )

    def shared(stage, group):
        share_copy(stage, group).wait_recv()

    def sent(stage):
        for i in range(len(copies(stage))):
            remote(stage, i).wait_send()
        for group in range(3 if stage < N else 0):
            share_copy(stage, group).wait_send()

    row8 = lax.broadcasted_iota(jnp.int32, (8, 128), 0)
    col8 = lax.broadcasted_iota(jnp.int32, (8, 128), 1)
    by_b = (col8 % 8 == row8).astype(F32)
    by_a = (col8 % 64 // 8 == row8).astype(F32)
    row_t = lax.broadcasted_iota(jnp.int32, (128, 8), 0)
    col_t = lax.broadcasted_iota(jnp.int32, (128, 8), 1)
    by_b_t = (row_t % 8 == col_t).astype(F32)
    by_a_t = (row_t % 64 // 8 == col_t).astype(F32)
    dot = functools.partial(jnp.dot, precision=HIGH, preferred_element_type=F32)

    def query_copy(i, receiving=False):
        mine = c * 8 + z * 4
        src, dst, to = (
            (q_hbm, qbuf.at[mine + (xm if receiving else x)], "xp"),
            (q_hbm, qbuf.at[mine + (xp if receiving else x)], "xm"),
            (qbuf.at[mine + xm], qbuf.at[mine + ((x + 2) % 4 if receiving else xm)], "xp"),
            (qbuf.at[pl.ds(mine, 4)], qbuf.at[pl.ds(c * 8 + (1 - z) * 4 if receiving else mine, 4)], "z"),
            (qbuf.at[pl.ds(c * 8, 8)], qbuf.at[pl.ds((1 - c) * 8 if receiving else c * 8, 8)], "sib"),
        )[i]
        return pltpu.make_async_remote_copy(
            src_ref=src, dst_ref=dst, send_sem=ss_q.at[i], recv_sem=rs_q.at[i],
            device_id=dev[to], device_id_type=MESH,
        )

    def query_far():
        query_copy(0, True).wait_recv()
        query_copy(2).start()

    def query_z():
        query_copy(1, True).wait_recv()
        query_copy(2, True).wait_recv()
        loaded("query")
        query_copy(3).start()

    def query_sibling():
        query_copy(3, True).wait_recv()
        query_copy(4).start()

    def y_copy(i, owner):
        return pltpu.make_async_remote_copy(
            src_ref=ybuf.at[owner], dst_ref=ybuf.at[owner], send_sem=ss_y.at[i], recv_sem=rs_y.at[owner],
            device_id=(dp, zh * 4 + (y + i) % 4), device_id_type=MESH,
        )

    def z_copy(owner):
        return pltpu.make_async_remote_copy(
            src_ref=zbuf.at[owner], dst_ref=zbuf.at[owner], send_sem=ss_z, recv_sem=rs_z,
            device_id=(dp, (1 - zh) * 4 + y), device_id_type=MESH,
        )

    def signs_copy():
        return pltpu.make_async_remote_copy(
            src_ref=shid_hbm.at[:, pl.ds(given, BLOCK)], dst_ref=shid.at[:, pl.ds(PEER * BLOCK, BLOCK)],
            send_sem=ss_h, recv_sem=rs_h, device_id=dev["peer"], device_id_type=MESH,
        )

    def input_part():
        loaded("input")
        sign = (2 * sin[...] - 1).astype(F32).astype(BF16)
        ybuf[y] = lax.dot_general(sign, li[...], NT, preferred_element_type=F32) * D ** (-0.5)
        for i in range(1, 4):
            y_copy(i, y).start()

    def input_sum():
        for i in range(1, 4):
            y_copy(i, (y + i) % 4).wait_recv()
        zbuf[zh] = ybuf[0] + ybuf[1] + ybuf[2] + ybuf[3]
        z_copy(zh).start()

    def input_weigh():
        z_copy(1 - zh).wait_recv()
        full = zbuf[0] + zbuf[1]
        pos = lax.broadcasted_iota(jnp.int32, (8, SLOTS), 1)
        for e in range(TOK // SLOTS):
            count = len_ref[e]
            scale = FF ** (-0.5) / count.astype(F32)
            part = full[:, e * SLOTS : (e + 1) * SLOTS]
            part = jnp.where(pos < count, part * scale, 0.0)
            in64[pl.ds(e * SLOTS, SLOTS), :] = dot(part.T, by_a)

    def hidden_signs():
        loaded("signs")
        signs_copy().wait_recv()
        sign = (2 * shid[...] - 1).astype(F32)
        s64[...] = jnp.dot(by_b_t.astype(BF16), sign.astype(BF16), preferred_element_type=F32).astype(BF16)

    def query_matrix():
        loaded("small")
        query_copy(4, True).wait_recv()
        for i in range(16):
            owner = i % 4 * 4 + i // 4 % 2 * 2 + i // 8
            qfull[pl.ds(4 * owner, 4), :] = qbuf[i]
        kron = dot(dot(by_a_t, bi[...]), by_a[:, :64]) * dot(dot(by_b_t, bo[...]), by_b[:, :64])
        values = jnp.sum(dot(ev[...], by_b[:, :64]) * by_a[:, :64], axis=0, keepdims=True)
        both = lax.dot_general(kron / (values + SHIFT), kron[:64], NT, precision=HIGH, preferred_element_type=F32)
        twice = dot(both, qfull[...])
        top = twice.astype(BF16)
        rest = (twice - top.astype(F32)).astype(BF16)
        both_parts = jnp.concatenate([top[:64], rest[:64]], axis=0)
        mat[pl.ds(0, 128), :] = both_parts
        mat[pl.ds(128, 128), :] = both_parts

    def activation(rows):
        g = gate[:, rows].astype(F32)
        return g * (0.5 + 0.5 * jnp.tanh(0.5 * g))

    def project(rows, product, factor):
        up = (product * factor).astype(BF16)
        out64[...] += lax.dot_general(up, s64[:, rows], NT, preferred_element_type=F32)

    def first_part(j):
        rows = pl.ds(pl.multiple_of(j * BLOCK, BLOCK), BLOCK)
        hid[j] = lax.dot_general(
            ct[:, pl.ds(0, 2560)], w[rows, pl.ds(0, 2560)], NT, preferred_element_type=F32
        )
        act[j] = activation(rows)

    def second_part(j):
        rows = pl.ds(pl.multiple_of(j * BLOCK, BLOCK), BLOCK)
        product = hid[j] + lax.dot_general(
            ct[:, pl.ds(2560, 1536)], w[rows, pl.ds(2560, 1536)], NT, preferred_element_type=F32
        )
        project(rows, product, act[j])

    def whole(j):
        rows = pl.ds(pl.multiple_of(j * BLOCK, BLOCK), BLOCK)
        product = lax.dot_general(ct[...], w[rows, :], NT, preferred_element_type=F32)
        project(rows, product, activation(rows))

    def step_actions(i):
        part, j = SCHEDULE[i][1]
        for n, (arrivals, (what, at, which)) in enumerate(PLAN[i]):
            if i == 0 and n == EARLY:
                start("give", "input", "query", "signs", "c", "gate", "small")
                loaded("plain")
            for stage, copy in arrivals:
                remote(stage, copy).wait_recv()
            if what == 0:
                if at == GATES and which < 4:
                    loads()["give"][which]().wait()
                remote(at, which).start()
            elif what == 1:
                share_copy(at, which).start()
            elif what == 2:
                small[at]()
        if i == len(SCHEDULE) - 1:
            for stage in range(5):
                sent(stage)
        if i == 0:
            loaded("c", "gate")
        for group in ((0,), (1, 2), (0, 1, 2))[part]:
            shared(j, group)

    def block_of(step, part):
        j = jnp.int32(-1)
        for i, (_, (which, block)) in enumerate(SCHEDULE):
            if which == part:
                j = jnp.where(step == i, block, j)
        return j

    def step(k, _):
        for i in range(len(SCHEDULE)):
            pl.when(k == i)(functools.partial(step_actions, i))
        for part, compute in enumerate((first_part, second_part, whole)):
            j = block_of(k, part)
            pl.when(j >= 0)(functools.partial(compute, j))
        return 0

    def input_start():
        query_copy(0).start()
        query_copy(1).start()
        signs_copy().start()
        input_part()

    small = (
        input_start, query_far, input_sum, hidden_signs, query_z, input_weigh, query_sibling, query_matrix,
    )
    out64[...] = jnp.zeros_like(out64)
    lax.fori_loop(0, len(SCHEDULE), step, 0)

    rows = [
        jnp.sum(in64[pl.ds(e * SLOTS, SLOTS), :] * out64[pl.ds(e * SLOTS, SLOTS), :], axis=0, keepdims=True)
        for e in range(TOK // SLOTS)
    ]
    gbuf[tn] = jnp.zeros((8, 128), F32)
    for e in range(TOK // SLOTS):
        gbuf[tn, pl.ds(e, 1), :] = rows[e]

    def g_copy(i, owner):
        return pltpu.make_async_remote_copy(
            src_ref=gbuf.at[owner], dst_ref=gbuf.at[owner], send_sem=ss_g.at[i], recv_sem=rs_g.at[owner],
            device_id=(dp, (zh + 1 - i // 4) % 2 * 4 + (y + FAR_FIRST[i % 4]) % 4), device_id_type=MESH,
        )

    for i in range(7):
        g_copy(i, tn).start()
    for stage in range(5, N + 1):
        sent(stage)
    signs_copy().wait_send()
    for i in range(5):
        query_copy(i).wait_send()
    for i in range(1, 4):
        y_copy(i, y).wait_send()
    z_copy(zh).wait_send()
    for i in range(1, 8):
        g_copy(0, (tn + i) % 8).wait_recv()
    total = gbuf[0]
    for i in range(1, 8):
        total = total + gbuf[i]
    top = total.astype(BF16)
    rest = (total - top.astype(F32)).astype(BF16)
    both = jnp.concatenate([top, rest], axis=1)
    o_ref[...] = jnp.dot(both, mat[...], preferred_element_type=F32)[:4, :]
    for i in range(7):
        g_copy(i, tn).wait_send()


def on_device(
    layer_input, output_cotangent, gate_preact, down_weight, lengths, input_signs, hidden_signs,
    basis_in, basis_out, eigenvalues, query_grads,
):
    any_spec = pl.BlockSpec(memory_space=pl.ANY)
    vmem, dma = pltpu.VMEM, pltpu.SemaphoreType.DMA
    specs = [any_spec] * 11
    specs[4] = pl.BlockSpec(memory_space=pltpu.SMEM)
    return pl.pallas_call(
        kernel,
        out_shape=pltpu.VMEM((4, 512), F32),
        in_specs=specs,
        out_specs=pl.BlockSpec(memory_space=pltpu.VMEM),
        scratch_shapes=[
            vmem((HID, D), BF16),
            vmem((TOK, D), BF16),
            vmem((TOK, HID), BF16),
            vmem((BLOCK, COLS), BF16),
            vmem((TOK, BLOCK), BF16),
            vmem((TOK, BLOCK), BF16),
            vmem((TOK, 512), BF16),
            vmem((8, 512), jnp.int32),
            vmem((8, HID), jnp.int32),
            vmem((8, 8), F32),
            vmem((8, 8), F32),
            vmem((8, 8), F32),
            vmem((16, 4, 512), F32),
            vmem((64, 512), F32),
            vmem((256, 512), BF16),
            vmem((4, 8, TOK), F32),
            vmem((2, 8, TOK), F32),
            vmem((8, 8, 128), F32),
            vmem((TOK, 128), F32),
            vmem((128, HID), BF16),
            vmem((N, TOK, BLOCK), F32),
            vmem((N, TOK, BLOCK), F32),
            vmem((TOK, 128), F32),
            dma((N + 1, 10)), dma((N + 1, 10)), dma((N, 3)), dma((N, 3)), dma((5,)), dma((5,)),
            dma((4,)), dma((4,)), dma, dma, dma, dma, dma((8,)), dma((8,)), dma((40,)),
        ],
        compiler_params=pltpu.CompilerParams(
            collective_id=0, has_side_effects=True, vmem_limit_bytes=56 * 1024 * 1024
        ),
        cost_estimate=pl.CostEstimate(flops=2 * TOK * HID * D, bytes_accessed=30_000_000, transcendentals=TOK * HID),
        name="scores",
    )(
        layer_input.reshape(TOK, 512),
        output_cotangent.reshape(TOK, D),
        gate_preact.reshape(TOK, HID),
        down_weight,
        lengths,
        input_signs.T,
        hidden_signs.T,
        basis_in,
        basis_out,
        eigenvalues,
        query_grads.T,
    )


def solution(mesh):
    in_specs = (
        P("dp", None, "tensor"),
        P("dp", None, None),
        P("dp", None, "tensor"),
        P("tensor", "dp"),
        P("dp"),
        P("tensor", None),
        P("tensor", None),
        P(),
        P(),
        P(),
        P("tensor", "dp"),
    )
    return jax.shard_map(
        on_device, mesh=mesh, in_specs=in_specs, out_specs=P("dp", "tensor"), check_vma=False
    )
```

```python
import functools

import jax
import jax.numpy as jnp
from jax import lax
from jax.experimental import pallas as pl
from jax.experimental.pallas import tpu as pltpu
from jax.sharding import PartitionSpec as P

MESH = pl.DeviceIdType.MESH
HIGH = lax.Precision.HIGHEST
F32, BF16 = jnp.float32, jnp.bfloat16
D, FF, RA, RG = 4096, 14336, 8, 8
SHIFT = 0.1
TOK, HID, COLS, SLOTS = 1024, 1792, 256, 256
BLOCK = 256
NT = (((1,), (1,)), ((), ()))

N = HID // BLOCK
PEER, GATES = N - 1, N
ALONG_X = (15, 15, 16, 16, 16)
SCHEDULE = (
    (
        (
            (0, 0, 0), (0, 1, 0), (0, 0, 1), (0, 1, 1), (0, 0, 2), (0, 1, 2), (0, 6, 0), (2, 0, 0),
            (0, 2, 0), (0, 2, 1), (0, 2, 2), (0, 7, 0), (0, 7, 1), (2, 2, 0), (0, 0, 3), (0, 0, 4),
            (0, 3, 2), (0, 6, 1), (0, 0, 5), (0, 0, 6), (2, 1, 0), (2, 3, 0), (0, 7, 4), (0, 7, 2),
            (0, 1, 4), (0, 1, 3), (0, 2, 4), (0, 2, 3), (2, 5, 0), (0, 7, 5), (0, 6, 2), (1, 0, 0),
            (0, 3, 1), (0, 3, 0), (0, 4, 2), (1, 0, 1), (2, 4, 0),
        ),
        (0, 0),
    ),
    (
        (
            (0, 0, 7), (0, 0, 8), (0, 4, 1), (1, 1, 0), (0, 4, 0), (1, 2, 0), (0, 7, 6),
        ),
        (0, 1),
    ),
    (
        (
            (0, 3, 3), (0, 5, 0), (0, 3, 4), (0, 5, 1), (0, 1, 7), (0, 7, 3),
        ),
        (0, 2),
    ),
    (
        (
            (0, 6, 3), (1, 0, 2), (0, 5, 2), (2, 6, 0), (0, 1, 6), (0, 1, 5),
        ),
        (1, 0),
    ),
    (
        (
            (0, 1, 8), (0, 1, 9), (1, 3, 0), (1, 6, 1), (1, 6, 2), (0, 4, 3), (0, 4, 4), (0, 2, 7),
            (2, 7, 0), (0, 5, 3), (0, 5, 4), (1, 1, 2),
        ),
        (0, 3),
    ),
    (
        (
            (0, 2, 5), (0, 2, 6), (0, 7, 7), (1, 1, 1), (0, 3, 6), (0, 3, 5), (0, 2, 8), (0, 2, 9),
            (0, 3, 7), (1, 4, 0),
        ),
        (1, 1),
    ),
    (
        (
            (1, 2, 2), (1, 5, 0), (0, 4, 6), (0, 4, 5),
        ),
        (0, 4),
    ),
    (
        (
            (0, 4, 7), (1, 6, 0),
        ),
        (0, 5),
    ),
    (
        (
            (0, 5, 5), (0, 5, 6), (0, 5, 7), (1, 2, 1),
        ),
        (2, 6),
    ),
    (
        (
            (1, 3, 1), (1, 3, 2), (1, 4, 1),
        ),
        (1, 2),
    ),
    (
        (
            (1, 4, 2),
        ),
        (1, 3),
    ),
    (
        (
            (1, 5, 1), (1, 5, 2),
        ),
        (1, 4),
    ),
    (
        (
        ),
        (1, 5),
    ),
)

O, L, R, FAR, Z, ZL, ZR, ZF = range(8)
FAR_FIRST = (2, 1, 3, 0)


def copies(stage):
    rows, half = BLOCK, BLOCK // 2
    hop1 = [(O, 0, rows, "xp", L), (O, 0, rows, "xm", R), (O, 0, rows, "z", Z)]
    far = [(L, 0, half, "xp", FAR), (R, half, rows, "xm", FAR)]
    if stage == 0:
        return hop1 + far + [
            (Z, 0, rows, "xp", ZL),
            (Z, 0, rows, "xm", ZR),
            (ZL, 0, half, "xp", ZF),
            (ZR, half, rows, "xm", ZF),
        ]
    if stage == PEER:
        return [(O, 0, rows, "cross", Z), (Z, 0, rows, "cross", O), (L, 0, rows, "cross", ZL), (ZL, 0, rows, "cross", L)]
    if stage == GATES:
        return [None] * 8
    part = 16 * ALONG_X[stage - 1]
    return hop1 + far + [
        (Z, 0, part, "xp", ZL),
        (Z, 0, part, "xm", ZR),
        (FAR, 0, rows, "z", ZF),
    ] + [(L, part, rows, "z", ZL), (R, part, rows, "z", ZR)] * (part < rows)


def after(stage, i):
    if stage == PEER:
        return [(0, j) for j in ((), (2,), (0, 1, 3, 4), (5, 6, 7, 8))[i]]
    if stage == GATES:
        return [(GATES, i - 4)] if i >= 4 else []
    if stage == 0:
        return [(0, j) for j in ((), (), (), (0,), (1,), (2,), (2,), (5,), (6,))[i]]
    return [(stage, j) for j in ((), (), (), (0,), (1,), (2,), (2,), (3, 4), (0,), (1,))[i]]


GROUPS = ((0, 1280), (2560, 512), (3072, 256))


def brought(stage, group):
    if stage == PEER:
        which = ((0, 1, 3), (2,), (2,))[group]
    elif stage == 0:
        which = ((0, 1, 2, 3, 4), (5, 6), (7, 8))[group]
    else:
        which = ((0, 1, 2, 3, 4), (5, 6, 8, 9), (7,))[group]
    return [(stage, i) for i in which if i < len(copies(stage))]


def bundle(stage, i):
    if stage == PEER:
        return (0, 0, 1, 0)[i]
    if stage == GATES:
        return min(i, 4)
    if stage == 0:
        return (0, 1, 2, 3, 3, 4, 4, 5, 5)[i]
    return (0, 1, 2, 3, 3, 4, 4, 5, 4, 4)[i]


def receive_sem(stage, which):
    return stage * 6 + which if stage <= PEER else PEER * 6 + 2 + which


RECEIVE_SEMS = PEER * 6 + 2 + 5


def plan():
    arrived, steps = set(), []
    for actions, (part, block) in SCHEDULE:
        steps.append([])
        for what, at, which in actions + ((3, part, block),):
            needed = ()
            if what == 0:
                needed = after(at, which)
            elif what == 1:
                needed = brought(at, which)
            elif what == 3 and part != 1 and block == PEER:
                needed = [(GATES, i) for i in range(4, 8)]
            new = sorted({(at, bundle(at, i)) for at, i in needed} - arrived)
            arrived.update(new)
            steps[-1].append((new, (what, at, which)))
    return steps


PLAN = plan()
GIVE_FIRST = min(
    (i, n) for i, step in enumerate(PLAN) for n, (_, (what, at, which)) in enumerate(step) if (what, at) == (0, GATES) and which < 4
)
EARLY = [what == 0 and at == 0 and not new for new, (what, at, _) in PLAN[0]].index(False)


def column(slot):
    return slot * COLS if slot < 5 else 2560 + (slot - 5) * COLS


def sibling_column(col):
    return col + (1280 if col < 1280 else 768)


def kernel(
    li_hbm, ct_hbm, gate_hbm, w_hbm, len_ref, sin_hbm, shid_hbm, bi_hbm, bo_hbm, ev_hbm, q_hbm,
    o_ref,
    w, ct, gate, give_w, give_gate, relay, li, sin, shid, bi, bo, ev, qbuf, qfull, mat, ybuf, zbuf, gbuf, in64, s64, hid, act, out64,
    ss_w, rs_w, ss_s, rs_s, ss_q, rs_q, ss_y, rs_y, rs_z, ss_h, rs_h, ss_g, rs_g, lsem,
):
    dp, tn = lax.axis_index("dp"), lax.axis_index("tensor")
    x, z, c = dp // 4, (dp // 2) % 2, dp % 2
    zh, y = tn // 4, tn % 4
    xp, xm = (x + 1) % 4, (x + 3) % 4
    at = lambda xx, zz, cc: xx * 4 + zz * 2 + cc
    dev = {
        "xp": (at(xp, z, c), tn),
        "xm": (at(xm, z, c), tn),
        "z": (at(x, 1 - z, c), tn),
        "sib": (at(x, z, 1 - c), tn),
        "cross": (at(x, 1 - z, c), (1 - zh) * 4 + y),
        "peer": (dp, (1 - zh) * 4 + y),
    }

    kept = pl.multiple_of((5 + z) * BLOCK, BLOCK)
    given = pl.multiple_of((6 - z) * BLOCK, BLOCK)
    plain = (N - 2) * BLOCK
    q_me = c * 8 + z * 4 + x

    def quarter(i):
        return pl.ds(i * SLOTS, SLOTS)

    def done(ref, sem):
        pltpu.make_async_copy(ref, ref, sem).wait()

    NAMES = ("own", "plain", "give", "input", "insigns", "query", "signs", "c", "gate", "bi", "bo", "ev")

    def start(*names):
        for name in names:
            for src, dst in copies_in[name]():
                pltpu.make_async_copy(src, dst, lsem.at[NAMES.index(name)]).start()

    def loaded(*names):
        whole_of = {
            "own": w.at[pl.ds(0, 2 * BLOCK), pl.ds(0, COLS)],
            "plain": w.at[pl.ds(BLOCK, plain), pl.ds(0, COLS)],
            "give": give_gate, "input": li, "insigns": sin, "query": qbuf.at[q_me],
            "signs": shid.at[:, pl.ds(0, plain + BLOCK)], "c": ct, "gate": gate.at[:, pl.ds(0, plain + BLOCK)],
            "bi": bi, "bo": bo, "ev": ev,
        }
        for name in names:
            done(whole_of[name], lsem.at[NAMES.index(name)])

    def load_c():
        found = []
        far = (x + 2) % 4
        for half in range(2):
            cc = c if half == 0 else 1 - c
            for slot, (xx, zz) in enumerate(
                ((x, z), (xm, z), (xp, z), (far, z), (x, 1 - z), (xm, 1 - z), (xp, 1 - z), (far, 1 - z))
            ):
                first = pl.multiple_of(at(xx, zz, cc) * COLS, COLS)
                col = sibling_column(column(slot)) if half else column(slot)
                found.append((ct_hbm.at[:, pl.ds(first, COLS)], ct.at[:, pl.ds(col, COLS)]))
        return found

    def by_place(src, dst):
        return [
            (src.at[:, pl.ds(kept, BLOCK)], dst.at[:, pl.ds(0, BLOCK)]),
            (src.at[:, pl.ds(0, plain)], dst.at[:, pl.ds(BLOCK, plain)]),
        ]

    copies_in = {
        "own": lambda: [
            (w_hbm.at[pl.ds(kept, BLOCK)], w.at[pl.ds(0, BLOCK), pl.ds(0, COLS)]),
            (w_hbm.at[pl.ds(given, BLOCK)], give_w),
        ],
        "plain": lambda: [(w_hbm.at[pl.ds(0, plain)], w.at[pl.ds(BLOCK, plain), pl.ds(0, COLS)])],
        "give": lambda: [(gate_hbm.at[:, pl.ds(given, BLOCK)], give_gate)],
        "input": lambda: [(li_hbm, li)],
        "insigns": lambda: [(sin_hbm, sin)],
        "query": lambda: [(q_hbm, qbuf.at[q_me])],
        "signs": lambda: by_place(shid_hbm, shid),
        "c": load_c,
        "gate": lambda: by_place(gate_hbm, gate),
        "bi": lambda: [(bi_hbm, bi)],
        "bo": lambda: [(bo_hbm, bo)],
        "ev": lambda: [(ev_hbm, ev)],
    }

    start("own", "plain")
    barrier = pltpu.get_barrier_semaphore()
    for name in ("xp", "xm", "z", "sib", "cross"):
        pl.semaphore_signal(barrier, inc=1, device_id=dev[name], device_id_type=MESH)
    for i in range(1, 8):
        pl.semaphore_signal(barrier, inc=1, device_id=(dp, (tn + i) % 8), device_id_type=MESH)
    pl.semaphore_wait(barrier, 12)
    loaded("own")

    def remote(stage, i):
        if stage == GATES:
            rows = quarter(i % 4)
            to = ("cross", "z")[i // 4]
            src = (give_gate, relay)[i // 4].at[rows]
            dst = (relay.at[rows], gate.at[rows, pl.ds(PEER * BLOCK, BLOCK)])[i // 4]
        else:
            piece, low, high, to, there = copies(stage)[i]
            from_rows = pl.ds((0 if stage == PEER else stage * BLOCK) + low, high - low)
            rows = pl.ds(stage * BLOCK + low, high - low)
            cols = 3 * COLS if stage == PEER and i >= 2 else COLS
            src = w.at[from_rows, pl.ds(column(piece), cols)]
            if stage == 0 and i == 2:
                src = give_w
            dst = w.at[rows, pl.ds(column(there), cols)]
        return pltpu.make_async_remote_copy(
            src_ref=src, dst_ref=dst, send_sem=ss_w, recv_sem=rs_w.at[receive_sem(stage, bundle(stage, i))],
            device_id=dev[to], device_id_type=MESH,
        )

    def arrive(stage, which):
        if stage == GATES:
            ref = relay.at[quarter(which)] if which < 4 else gate.at[:, pl.ds(PEER * BLOCK, BLOCK)]
        else:
            if stage == PEER:
                col, cols = ((0, 5 * COLS), (column(ZL), 3 * COLS))[which]
            else:
                col, cols = (column((L, R, Z, FAR, ZL, ZF)[which]), 2 * COLS if which == 4 else COLS)
            ref = w.at[pl.ds(stage * BLOCK, BLOCK), pl.ds(col, cols)]
        done(ref, rs_w.at[receive_sem(stage, which)])

    def share_copy(stage, group):
        rows = pl.ds(stage * BLOCK, BLOCK)
        col, cols = GROUPS[group]
        return pltpu.make_async_remote_copy(
            src_ref=w.at[rows, pl.ds(col, cols)], dst_ref=w.at[rows, pl.ds(sibling_column(col), cols)],
            send_sem=ss_s, recv_sem=rs_s.at[stage, min(group, 1)],
            device_id=dev["sib"], device_id_type=MESH,
        )

    def shared(stage, part):
        col, cols = ((0, 1280), (2560, 768))[part]
        done(w.at[pl.ds(stage * BLOCK, BLOCK), pl.ds(sibling_column(col), cols)], rs_s.at[stage, part])

    row8 = lax.broadcasted_iota(jnp.int32, (8, 128), 0)
    col8 = lax.broadcasted_iota(jnp.int32, (8, 128), 1)
    by_b = (col8 % 8 == row8).astype(F32)
    by_a = (col8 % 64 // 8 == row8).astype(F32)
    row_t = lax.broadcasted_iota(jnp.int32, (128, 8), 0)
    col_t = lax.broadcasted_iota(jnp.int32, (128, 8), 1)
    by_b_t = (row_t % 8 == col_t).astype(F32)
    by_a_t = (row_t % 64 // 8 == col_t).astype(F32)
    dot = functools.partial(jnp.dot, precision=HIGH, preferred_element_type=F32)

    def query_copy(i, receiving=False):
        mine = c * 8 + z * 4
        src, dst, to = (
            (q_hbm, qbuf.at[mine + (xm if receiving else x)], "xp"),
            (q_hbm, qbuf.at[mine + (xp if receiving else x)], "xm"),
            (qbuf.at[mine + xm], qbuf.at[mine + ((x + 2) % 4 if receiving else xm)], "xp"),
            (qbuf.at[pl.ds(mine, 4)], qbuf.at[pl.ds(c * 8 + (1 - z) * 4 if receiving else mine, 4)], "z"),
            (qbuf.at[pl.ds(c * 8, 8)], qbuf.at[pl.ds((1 - c) * 8 if receiving else c * 8, 8)], "sib"),
        )[i]
        return pltpu.make_async_remote_copy(
            src_ref=src, dst_ref=dst, send_sem=ss_q, recv_sem=rs_q.at[(0, 1, 1, 2, 3)[i]],
            device_id=dev[to], device_id_type=MESH,
        )

    def query_far():
        query_copy(0, True).wait_recv()
        query_copy(2).start()

    def query_z():
        done(qbuf.at[pl.ds(c * 8 + z * 4, 2)], rs_q.at[1])
        loaded("query")
        query_copy(3).start()

    def query_sibling():
        query_copy(3, True).wait_recv()
        query_copy(4).start()

    def y_copy(i, owner):
        return pltpu.make_async_remote_copy(
            src_ref=ybuf.at[owner], dst_ref=ybuf.at[owner], send_sem=ss_y, recv_sem=rs_y,
            device_id=(dp, zh * 4 + (y + i) % 4), device_id_type=MESH,
        )

    def z_copy(owner):
        return pltpu.make_async_remote_copy(
            src_ref=zbuf.at[owner], dst_ref=zbuf.at[owner], send_sem=ss_y, recv_sem=rs_z,
            device_id=(dp, (1 - zh) * 4 + y), device_id_type=MESH,
        )

    def signs_copy():
        return pltpu.make_async_remote_copy(
            src_ref=shid_hbm.at[:, pl.ds(given, BLOCK)], dst_ref=shid.at[:, pl.ds(PEER * BLOCK, BLOCK)],
            send_sem=ss_h, recv_sem=rs_h, device_id=dev["peer"], device_id_type=MESH,
        )

    def input_part():
        loaded("input", "insigns")
        sign = (2 * sin[...] - 1).astype(F32).astype(BF16)
        ybuf[y] = lax.dot_general(sign, li[...], NT, preferred_element_type=F32) * D ** (-0.5)
        for i in range(1, 4):
            y_copy(i, y).start()

    def input_sum():
        done(ybuf.at[pl.ds(0, 3)], rs_y)
        zbuf[zh] = ybuf[0] + ybuf[1] + ybuf[2] + ybuf[3]
        z_copy(zh).start()

    def input_weigh():
        z_copy(1 - zh).wait_recv()
        full = zbuf[0] + zbuf[1]
        pos = lax.broadcasted_iota(jnp.int32, (8, SLOTS), 1)
        for e in range(TOK // SLOTS):
            count = len_ref[e]
            scale = FF ** (-0.5) / count.astype(F32)
            part = full[:, e * SLOTS : (e + 1) * SLOTS]
            part = jnp.where(pos < count, part * scale, 0.0)
            in64[pl.ds(e * SLOTS, SLOTS), :] = dot(part.T, by_a)

    def hidden_signs():
        loaded("signs")
        signs_copy().wait_recv()
        sign = (2 * shid[...] - 1).astype(F32)
        s64[...] = jnp.dot(by_b_t.astype(BF16), sign.astype(BF16), preferred_element_type=F32).astype(BF16)

    def query_matrix():
        loaded("bi", "bo", "ev")
        query_copy(4, True).wait_recv()
        for i in range(16):
            owner = i % 4 * 4 + i // 4 % 2 * 2 + i // 8
            qfull[pl.ds(4 * owner, 4), :] = qbuf[i]
        kron = dot(dot(by_a_t, bi[...]), by_a[:, :64]) * dot(dot(by_b_t, bo[...]), by_b[:, :64])
        values = jnp.sum(dot(ev[...], by_b[:, :64]) * by_a[:, :64], axis=0, keepdims=True)
        both = lax.dot_general(kron / (values + SHIFT), kron[:64], NT, precision=HIGH, preferred_element_type=F32)
        twice = dot(both, qfull[...])
        top = twice.astype(BF16)
        rest = (twice - top.astype(F32)).astype(BF16)
        both_parts = jnp.concatenate([top[:64], rest[:64]], axis=0)
        mat[pl.ds(0, 128), :] = both_parts
        mat[pl.ds(128, 128), :] = both_parts

    def activation(rows):
        g = gate[:, rows].astype(F32)
        return g * (0.5 + 0.5 * jnp.tanh(0.5 * g))

    def project(rows, product, factor):
        up = (product * factor).astype(BF16)
        out64[...] += lax.dot_general(up, s64[:, rows], NT, preferred_element_type=F32)

    def first_part(j):
        rows = pl.ds(pl.multiple_of(j * BLOCK, BLOCK), BLOCK)
        hid[j] = lax.dot_general(
            ct[:, pl.ds(0, 2560)], w[rows, pl.ds(0, 2560)], NT, preferred_element_type=F32
        )
        act[j] = activation(rows)

    def second_part(j):
        rows = pl.ds(pl.multiple_of(j * BLOCK, BLOCK), BLOCK)
        product = hid[j] + lax.dot_general(
            ct[:, pl.ds(2560, 1536)], w[rows, pl.ds(2560, 1536)], NT, preferred_element_type=F32
        )
        project(rows, product, act[j])

    def whole(j):
        rows = pl.ds(pl.multiple_of(j * BLOCK, BLOCK), BLOCK)
        product = lax.dot_general(ct[...], w[rows, :], NT, preferred_element_type=F32)
        project(rows, product, activation(rows))

    def step_actions(i):
        part, j = SCHEDULE[i][1]
        for n, (arrivals, (what, at, which)) in enumerate(PLAN[i]):
            if i == 0 and n == EARLY:
                start("give", "input", "insigns", "query", "signs", "c", "gate", "bi", "bo", "ev")
                loaded("plain")
            for stage, copy in arrivals:
                arrive(stage, copy)
            if what == 0:
                if (i, n) == GIVE_FIRST:
                    loaded("give")
                remote(at, which).start()
            elif what == 1:
                share_copy(at, which).start()
            elif what == 2:
                small[at]()
        if i == 0:
            loaded("c", "gate")
        for half in ((0,), (1,), (0, 1))[part]:
            shared(j, half)

    def block_of(step, part):
        j = jnp.int32(-1)
        for i, (_, (which, block)) in enumerate(SCHEDULE):
            if which == part:
                j = jnp.where(step == i, block, j)
        return j

    def step(k, _):
        for i in range(len(SCHEDULE)):
            pl.when(k == i)(functools.partial(step_actions, i))
        for part, compute in enumerate((first_part, second_part, whole)):
            j = block_of(k, part)
            pl.when(j >= 0)(functools.partial(compute, j))
        return 0

    def input_start():
        query_copy(0).start()
        query_copy(1).start()
        signs_copy().start()
        input_part()

    small = (
        input_start, query_far, input_sum, hidden_signs, query_z, input_weigh, query_sibling, query_matrix,
    )
    out64[...] = jnp.zeros_like(out64)
    lax.fori_loop(0, len(SCHEDULE), step, 0)

    rows = [
        jnp.sum(in64[pl.ds(e * SLOTS, SLOTS), :] * out64[pl.ds(e * SLOTS, SLOTS), :], axis=0, keepdims=True)
        for e in range(TOK // SLOTS)
    ]
    gbuf[tn] = jnp.zeros((8, 128), F32)
    for e in range(TOK // SLOTS):
        gbuf[tn, pl.ds(e, 1), :] = rows[e]

    def g_copy(i, owner):
        return pltpu.make_async_remote_copy(
            src_ref=gbuf.at[owner], dst_ref=gbuf.at[owner], send_sem=ss_g, recv_sem=rs_g,
            device_id=(dp, (zh + 1 - i // 4) % 2 * 4 + (y + FAR_FIRST[i % 4]) % 4), device_id_type=MESH,
        )

    for i in range(7):
        g_copy(i, tn).start()
    done(w.at[pl.ds(0, 928)], ss_w)
    done(w.at[:, pl.ds(0, 2048)], ss_s)
    done(qbuf.at[pl.ds(0, 15)], ss_q)
    done(ybuf, ss_y)
    signs_copy().wait_send()
    done(gbuf.at[pl.ds(0, 7)], rs_g)
    total = gbuf[0]
    for i in range(1, 8):
        total = total + gbuf[i]
    top = total.astype(BF16)
    rest = (total - top.astype(F32)).astype(BF16)
    both = jnp.concatenate([top, rest], axis=1)
    o_ref[...] = jnp.dot(both, mat[...], preferred_element_type=F32)[:4, :]
    done(gbuf.at[pl.ds(0, 7)], ss_g)


def on_device(
    layer_input, output_cotangent, gate_preact, down_weight, lengths, input_signs, hidden_signs,
    basis_in, basis_out, eigenvalues, query_grads,
):
    any_spec = pl.BlockSpec(memory_space=pl.ANY)
    vmem, dma = pltpu.VMEM, pltpu.SemaphoreType.DMA
    specs = [any_spec] * 11
    specs[4] = pl.BlockSpec(memory_space=pltpu.SMEM)
    return pl.pallas_call(
        kernel,
        out_shape=pltpu.VMEM((4, 512), F32),
        in_specs=specs,
        out_specs=pl.BlockSpec(memory_space=pltpu.VMEM),
        scratch_shapes=[
            vmem((HID, D), BF16),
            vmem((TOK, D), BF16),
            vmem((TOK, HID), BF16),
            vmem((BLOCK, COLS), BF16),
            vmem((TOK, BLOCK), BF16),
            vmem((TOK, BLOCK), BF16),
            vmem((TOK, 512), BF16),
            vmem((8, 512), jnp.int32),
            vmem((8, HID), jnp.int32),
            vmem((8, 8), F32),
            vmem((8, 8), F32),
            vmem((8, 8), F32),
            vmem((16, 4, 512), F32),
            vmem((64, 512), F32),
            vmem((256, 512), BF16),
            vmem((4, 8, TOK), F32),
            vmem((2, 8, TOK), F32),
            vmem((8, 8, 128), F32),
            vmem((TOK, 128), F32),
            vmem((128, HID), BF16),
            vmem((N, TOK, BLOCK), F32),
            vmem((N, TOK, BLOCK), F32),
            vmem((TOK, 128), F32),
            dma, dma((RECEIVE_SEMS,)), dma, dma((N, 2)), dma, dma((4,)), dma, dma, dma, dma, dma, dma, dma, dma((12,)),
        ],
        compiler_params=pltpu.CompilerParams(
            collective_id=0, has_side_effects=True, vmem_limit_bytes=56 * 1024 * 1024
        ),
        cost_estimate=pl.CostEstimate(flops=2 * TOK * HID * D, bytes_accessed=30_000_000, transcendentals=TOK * HID),
        name="scores",
    )(
        layer_input.reshape(TOK, 512),
        output_cotangent.reshape(TOK, D),
        gate_preact.reshape(TOK, HID),
        down_weight,
        lengths,
        input_signs.T,
        hidden_signs.T,
        basis_in,
        basis_out,
        eigenvalues,
        query_grads.T,
    )


def solution(mesh):
    in_specs = (
        P("dp", None, "tensor"),
        P("dp", None, None),
        P("dp", None, "tensor"),
        P("tensor", "dp"),
        P("dp"),
        P("tensor", None),
        P("tensor", None),
        P(),
        P(),
        P(),
        P("tensor", "dp"),
    )
    return jax.shard_map(
        on_device, mesh=mesh, in_specs=in_specs, out_specs=P("dp", "tensor"), check_vma=False
    )
```

```python
import functools

import jax
import jax.numpy as jnp
from jax import lax
from jax.experimental import pallas as pl
from jax.experimental.pallas import tpu as pltpu
from jax.sharding import PartitionSpec as P

MESH = pl.DeviceIdType.MESH
HIGH = lax.Precision.HIGHEST
F32, BF16 = jnp.float32, jnp.bfloat16
D, FF, RA, RG = 4096, 14336, 8, 8
SHIFT = 0.1
TOK, HID, COLS, SLOTS = 1024, 1792, 256, 256
BLOCK = 256
NT = (((1,), (1,)), ((), ()))

N = HID // BLOCK
PEER, GATES = N - 1, N
ALONG_X = (15, 15, 16, 16, 16)
SCHEDULE = (
    (
        (
            (0, 0, 0), (0, 0, 1), (0, 0, 2), (0, 1, 0), (0, 1, 1), (0, 1, 2), (0, 6, 0), (2, 0, 0),
            (0, 2, 0), (0, 2, 1), (0, 2, 2), (0, 7, 0), (0, 7, 1), (2, 2, 0), (0, 0, 3), (0, 0, 4),
            (0, 3, 2), (0, 6, 1), (0, 0, 5), (0, 0, 6), (2, 1, 0), (2, 3, 0), (0, 4, 2), (0, 7, 2),
            (0, 1, 4), (0, 1, 3), (0, 2, 4), (0, 2, 3), (0, 5, 2), (2, 5, 0), (0, 3, 1), (0, 6, 2),
            (1, 0, 0), (0, 3, 0), (0, 1, 8), (0, 1, 9), (0, 7, 4), (1, 0, 1), (2, 4, 0),
        ),
        (0, 0),
    ),
    (
        (
            (0, 0, 7), (0, 4, 0), (0, 0, 8), (0, 4, 1), (1, 1, 0), (1, 2, 0), (0, 1, 7),
        ),
        (0, 1),
    ),
    (
        (
            (0, 3, 3), (0, 5, 0), (0, 3, 4), (0, 5, 1), (0, 2, 7), (0, 7, 3),
        ),
        (0, 2),
    ),
    (
        (
            (0, 6, 3), (1, 0, 2), (0, 1, 6), (0, 2, 8), (0, 1, 5), (2, 6, 0), (0, 2, 9), (0, 7, 5),
        ),
        (1, 0),
    ),
    (
        (
            (0, 4, 3), (0, 4, 4), (1, 1, 2), (1, 3, 0), (1, 6, 1), (1, 6, 2), (0, 3, 7), (2, 7, 0),
            (0, 5, 3), (0, 5, 4), (1, 2, 2),
        ),
        (0, 3),
    ),
    (
        (
            (0, 2, 5), (0, 2, 6), (0, 7, 6), (1, 1, 1), (0, 3, 6), (0, 3, 5), (0, 7, 7), (1, 4, 0),
        ),
        (1, 1),
    ),
    (
        (
            (1, 5, 0), (0, 4, 6), (1, 3, 2), (0, 4, 5),
        ),
        (0, 4),
    ),
    (
        (
            (0, 4, 7), (1, 2, 1), (1, 6, 0),
        ),
        (0, 5),
    ),
    (
        (
            (0, 5, 5), (0, 5, 6), (0, 5, 7),
        ),
        (1, 2),
    ),
    (
        (
            (1, 3, 1),
        ),
        (2, 6),
    ),
    (
        (
            (1, 4, 1), (1, 4, 2),
        ),
        (1, 3),
    ),
    (
        (
            (1, 5, 1), (1, 5, 2),
        ),
        (1, 4),
    ),
    (
        (
        ),
        (1, 5),
    ),
)

O, L, R, FAR, Z, ZL, ZR, ZF = range(8)
FAR_FIRST = (2, 1, 3, 0)


def copies(stage):
    rows, half = BLOCK, BLOCK // 2
    hop1 = [(O, 0, rows, "xp", L), (O, 0, rows, "xm", R), (O, 0, rows, "z", Z)]
    far = [(L, 0, half, "xp", FAR), (R, half, rows, "xm", FAR)]
    if stage == 0:
        return hop1 + far + [
            (Z, 0, rows, "xp", ZL),
            (Z, 0, rows, "xm", ZR),
            (ZL, 0, half, "xp", ZF),
            (ZR, half, rows, "xm", ZF),
        ]
    if stage == PEER:
        return [(O, 0, rows, "cross", Z), (Z, 0, rows, "cross", O), (L, 0, rows, "cross", ZL), (ZL, 0, rows, "cross", L)]
    if stage == GATES:
        return [None] * 8
    part = 16 * ALONG_X[stage - 1]
    return hop1 + far + [
        (Z, 0, part, "xp", ZL),
        (Z, 0, part, "xm", ZR),
        (FAR, 0, rows, "z", ZF),
    ] + [(L, part, rows, "z", ZL), (R, part, rows, "z", ZR)] * (part < rows)


def after(stage, i):
    if stage == PEER:
        return [(0, j) for j in ((), (2,), (0, 1, 3, 4), (5, 6, 7, 8))[i]]
    if stage == GATES:
        return [(GATES, i - 4)] if i >= 4 else []
    if stage == 0:
        return [(0, j) for j in ((), (), (), (0,), (1,), (2,), (2,), (5,), (6,))[i]]
    return [(stage, j) for j in ((), (), (), (0,), (1,), (2,), (2,), (3, 4), (0,), (1,))[i]]


GROUPS = ((0, 1280), (2560, 512), (3072, 256))


def brought(stage, group):
    if stage == PEER:
        which = ((0, 1, 3), (2,), (2,))[group]
    elif stage == 0:
        which = ((0, 1, 2, 3, 4), (5, 6), (7, 8))[group]
    else:
        which = ((0, 1, 2, 3, 4), (5, 6, 8, 9), (7,))[group]
    return [(stage, i) for i in which if i < len(copies(stage))]


def bundle(stage, i):
    if stage == PEER:
        return (0, 0, 1, 0)[i]
    if stage == GATES:
        return min(i, 4)
    if stage == 0:
        return (0, 1, 2, 3, 3, 4, 4, 5, 5)[i]
    return (0, 1, 2, 3, 3, 4, 4, 5, 4, 4)[i]


def receive_sem(stage, which):
    return stage * 6 + which if stage <= PEER else PEER * 6 + 2 + which


RECEIVE_SEMS = PEER * 6 + 2 + 5


def plan():
    arrived, steps = set(), []
    for actions, (part, block) in SCHEDULE:
        steps.append([])
        for what, at, which in actions + ((3, part, block),):
            needed = ()
            if what == 0:
                needed = after(at, which)
            elif what == 1:
                needed = brought(at, which)
            elif what == 3 and part != 1 and block == PEER:
                needed = [(GATES, i) for i in range(4, 8)]
            new = sorted({(at, bundle(at, i)) for at, i in needed} - arrived)
            arrived.update(new)
            steps[-1].append((new, (what, at, which)))
    return steps


PLAN = plan()
GIVE_FIRST = min(
    (i, n) for i, step in enumerate(PLAN) for n, (_, (what, at, which)) in enumerate(step) if (what, at) == (0, GATES) and which < 4
)
EARLY = 3


def column(slot):
    return slot * COLS if slot < 5 else 2560 + (slot - 5) * COLS


def sibling_column(col):
    return col + (1280 if col < 1280 else 768)


def kernel(
    li_hbm, ct_hbm, gate_hbm, w_hbm, len_ref, sin_hbm, shid_hbm, bi_hbm, bo_hbm, ev_hbm, q_hbm,
    o_ref,
    w, ct, gate, give_w, give_gate, relay, li, sin, shid, bi, bo, ev, qbuf, qfull, mat, ybuf, zbuf, gbuf, in64, s64, hid, act, out64,
    ss_w, rs_w, ss_s, rs_s, ss_q, rs_q, ss_y, rs_y, rs_z, ss_h, rs_h, ss_g, rs_g, lsem,
):
    dp, tn = lax.axis_index("dp"), lax.axis_index("tensor")
    x, z, c = dp // 4, (dp // 2) % 2, dp % 2
    zh, y = tn // 4, tn % 4
    xp, xm = (x + 1) % 4, (x + 3) % 4
    at = lambda xx, zz, cc: xx * 4 + zz * 2 + cc
    dev = {
        "xp": (at(xp, z, c), tn),
        "xm": (at(xm, z, c), tn),
        "z": (at(x, 1 - z, c), tn),
        "sib": (at(x, z, 1 - c), tn),
        "cross": (at(x, 1 - z, c), (1 - zh) * 4 + y),
        "peer": (dp, (1 - zh) * 4 + y),
    }

    kept = pl.multiple_of((5 + z) * BLOCK, BLOCK)
    given = pl.multiple_of((6 - z) * BLOCK, BLOCK)
    plain = (N - 2) * BLOCK
    q_me = c * 8 + z * 4 + x

    def quarter(i):
        return pl.ds(i * SLOTS, SLOTS)

    def done(ref, sem):
        pltpu.make_async_copy(ref, ref, sem).wait()

    NAMES = ("own", "plain", "give", "input", "insigns", "query", "signs", "c", "gate", "bi", "bo", "ev")

    def start(*names):
        for name in names:
            for src, dst in copies_in[name]():
                pltpu.make_async_copy(src, dst, lsem.at[NAMES.index(name)]).start()

    def loaded(*names):
        whole_of = {
            "own": w.at[pl.ds(0, 2 * BLOCK), pl.ds(0, COLS)],
            "plain": w.at[pl.ds(BLOCK, plain), pl.ds(0, COLS)],
            "give": give_gate, "input": li, "insigns": sin, "query": qbuf.at[q_me],
            "signs": shid.at[:, pl.ds(0, plain + BLOCK)], "c": ct, "gate": gate.at[:, pl.ds(0, plain + BLOCK)],
            "bi": bi, "bo": bo, "ev": ev,
        }
        for name in names:
            done(whole_of[name], lsem.at[NAMES.index(name)])

    def load_c():
        found = []
        far = (x + 2) % 4
        for half in range(2):
            cc = c if half == 0 else 1 - c
            for slot, (xx, zz) in enumerate(
                ((x, z), (xm, z), (xp, z), (far, z), (x, 1 - z), (xm, 1 - z), (xp, 1 - z), (far, 1 - z))
            ):
                first = pl.multiple_of(at(xx, zz, cc) * COLS, COLS)
                col = sibling_column(column(slot)) if half else column(slot)
                found.append((ct_hbm.at[:, pl.ds(first, COLS)], ct.at[:, pl.ds(col, COLS)]))
        return found

    def by_place(src, dst):
        return [
            (src.at[:, pl.ds(kept, BLOCK)], dst.at[:, pl.ds(0, BLOCK)]),
            (src.at[:, pl.ds(0, plain)], dst.at[:, pl.ds(BLOCK, plain)]),
        ]

    copies_in = {
        "own": lambda: [
            (w_hbm.at[pl.ds(kept, BLOCK)], w.at[pl.ds(0, BLOCK), pl.ds(0, COLS)]),
            (w_hbm.at[pl.ds(given, BLOCK)], give_w),
        ],
        "plain": lambda: [(w_hbm.at[pl.ds(0, plain)], w.at[pl.ds(BLOCK, plain), pl.ds(0, COLS)])],
        "give": lambda: [(gate_hbm.at[:, pl.ds(given, BLOCK)], give_gate)],
        "input": lambda: [(li_hbm, li)],
        "insigns": lambda: [(sin_hbm, sin)],
        "query": lambda: [(q_hbm, qbuf.at[q_me])],
        "signs": lambda: by_place(shid_hbm, shid),
        "c": load_c,
        "gate": lambda: by_place(gate_hbm, gate),
        "bi": lambda: [(bi_hbm, bi)],
        "bo": lambda: [(bo_hbm, bo)],
        "ev": lambda: [(ev_hbm, ev)],
    }

    start("own", "plain")
    barrier = pltpu.get_barrier_semaphore()
    for name in ("xp", "xm", "z", "sib", "cross"):
        pl.semaphore_signal(barrier, inc=1, device_id=dev[name], device_id_type=MESH)
    for i in range(1, 8):
        pl.semaphore_signal(barrier, inc=1, device_id=(dp, (tn + i) % 8), device_id_type=MESH)
    pl.semaphore_wait(barrier, 12)
    loaded("own", "plain")

    def remote(stage, i):
        if stage == GATES:
            rows = quarter(i % 4)
            to = ("cross", "z")[i // 4]
            src = (give_gate, relay)[i // 4].at[rows]
            dst = (relay.at[rows], gate.at[rows, pl.ds(PEER * BLOCK, BLOCK)])[i // 4]
        else:
            piece, low, high, to, there = copies(stage)[i]
            from_rows = pl.ds((0 if stage == PEER else stage * BLOCK) + low, high - low)
            rows = pl.ds(stage * BLOCK + low, high - low)
            cols = 3 * COLS if stage == PEER and i >= 2 else COLS
            src = w.at[from_rows, pl.ds(column(piece), cols)]
            if stage == 0 and i == 2:
                src = give_w
            dst = w.at[rows, pl.ds(column(there), cols)]
        return pltpu.make_async_remote_copy(
            src_ref=src, dst_ref=dst, send_sem=ss_w, recv_sem=rs_w.at[receive_sem(stage, bundle(stage, i))],
            device_id=dev[to], device_id_type=MESH,
        )

    def arrive(stage, which):
        if stage == GATES:
            ref = relay.at[quarter(which)] if which < 4 else gate.at[:, pl.ds(PEER * BLOCK, BLOCK)]
        else:
            if stage == PEER:
                col, cols = ((0, 5 * COLS), (column(ZL), 3 * COLS))[which]
            else:
                col, cols = (column((L, R, Z, FAR, ZL, ZF)[which]), 2 * COLS if which == 4 else COLS)
            ref = w.at[pl.ds(stage * BLOCK, BLOCK), pl.ds(col, cols)]
        done(ref, rs_w.at[receive_sem(stage, which)])

    def share_copy(stage, group):
        rows = pl.ds(stage * BLOCK, BLOCK)
        col, cols = GROUPS[group]
        return pltpu.make_async_remote_copy(
            src_ref=w.at[rows, pl.ds(col, cols)], dst_ref=w.at[rows, pl.ds(sibling_column(col), cols)],
            send_sem=ss_s, recv_sem=rs_s.at[stage, min(group, 1)],
            device_id=dev["sib"], device_id_type=MESH,
        )

    def shared(stage, part):
        col, cols = ((0, 1280), (2560, 768))[part]
        done(w.at[pl.ds(stage * BLOCK, BLOCK), pl.ds(sibling_column(col), cols)], rs_s.at[stage, part])

    row8 = lax.broadcasted_iota(jnp.int32, (8, 128), 0)
    col8 = lax.broadcasted_iota(jnp.int32, (8, 128), 1)
    by_b = (col8 % 8 == row8).astype(F32)
    by_a = (col8 % 64 // 8 == row8).astype(F32)
    row_t = lax.broadcasted_iota(jnp.int32, (128, 8), 0)
    col_t = lax.broadcasted_iota(jnp.int32, (128, 8), 1)
    by_b_t = (row_t % 8 == col_t).astype(F32)
    by_a_t = (row_t % 64 // 8 == col_t).astype(F32)
    dot = functools.partial(jnp.dot, precision=HIGH, preferred_element_type=F32)

    def query_copy(i, receiving=False):
        mine = c * 8 + z * 4
        src, dst, to = (
            (q_hbm, qbuf.at[mine + (xm if receiving else x)], "xp"),
            (q_hbm, qbuf.at[mine + (xp if receiving else x)], "xm"),
            (qbuf.at[mine + xm], qbuf.at[mine + ((x + 2) % 4 if receiving else xm)], "xp"),
            (qbuf.at[pl.ds(mine, 4)], qbuf.at[pl.ds(c * 8 + (1 - z) * 4 if receiving else mine, 4)], "z"),
            (qbuf.at[pl.ds(c * 8, 8)], qbuf.at[pl.ds((1 - c) * 8 if receiving else c * 8, 8)], "sib"),
        )[i]
        return pltpu.make_async_remote_copy(
            src_ref=src, dst_ref=dst, send_sem=ss_q, recv_sem=rs_q.at[(0, 1, 1, 2, 3)[i]],
            device_id=dev[to], device_id_type=MESH,
        )

    def query_far():
        query_copy(0, True).wait_recv()
        query_copy(2).start()

    def query_z():
        done(qbuf.at[pl.ds(c * 8 + z * 4, 2)], rs_q.at[1])
        loaded("query")
        query_copy(3).start()

    def query_sibling():
        query_copy(3, True).wait_recv()
        query_copy(4).start()

    def y_copy(i, owner):
        return pltpu.make_async_remote_copy(
            src_ref=ybuf.at[owner], dst_ref=ybuf.at[owner], send_sem=ss_y, recv_sem=rs_y,
            device_id=(dp, zh * 4 + (y + i) % 4), device_id_type=MESH,
        )

    def z_copy(owner):
        return pltpu.make_async_remote_copy(
            src_ref=zbuf.at[owner], dst_ref=zbuf.at[owner], send_sem=ss_y, recv_sem=rs_z,
            device_id=(dp, (1 - zh) * 4 + y), device_id_type=MESH,
        )

    def signs_copy():
        return pltpu.make_async_remote_copy(
            src_ref=shid_hbm.at[:, pl.ds(given, BLOCK)], dst_ref=shid.at[:, pl.ds(PEER * BLOCK, BLOCK)],
            send_sem=ss_h, recv_sem=rs_h, device_id=dev["peer"], device_id_type=MESH,
        )

    def input_part():
        loaded("input", "insigns")
        sign = (2 * sin[...] - 1).astype(F32).astype(BF16)
        ybuf[y] = lax.dot_general(sign, li[...], NT, preferred_element_type=F32) * D ** (-0.5)
        for i in range(1, 4):
            y_copy(i, y).start()

    def input_sum():
        done(ybuf.at[pl.ds(0, 3)], rs_y)
        zbuf[zh] = ybuf[0] + ybuf[1] + ybuf[2] + ybuf[3]
        z_copy(zh).start()

    def input_weigh():
        z_copy(1 - zh).wait_recv()
        full = zbuf[0] + zbuf[1]
        pos = lax.broadcasted_iota(jnp.int32, (8, SLOTS), 1)
        for e in range(TOK // SLOTS):
            count = len_ref[e]
            scale = FF ** (-0.5) / count.astype(F32)
            part = full[:, e * SLOTS : (e + 1) * SLOTS]
            part = jnp.where(pos < count, part * scale, 0.0)
            in64[pl.ds(e * SLOTS, SLOTS), :] = dot(part.T, by_a)

    def hidden_signs():
        loaded("signs")
        signs_copy().wait_recv()
        sign = (2 * shid[...] - 1).astype(F32)
        s64[...] = jnp.dot(by_b_t.astype(BF16), sign.astype(BF16), preferred_element_type=F32).astype(BF16)

    def query_matrix():
        loaded("bi", "bo", "ev")
        query_copy(4, True).wait_recv()
        for i in range(16):
            owner = i % 4 * 4 + i // 4 % 2 * 2 + i // 8
            qfull[pl.ds(4 * owner, 4), :] = qbuf[i]
        kron = dot(dot(by_a_t, bi[...]), by_a[:, :64]) * dot(dot(by_b_t, bo[...]), by_b[:, :64])
        values = jnp.sum(dot(ev[...], by_b[:, :64]) * by_a[:, :64], axis=0, keepdims=True)
        both = lax.dot_general(kron / (values + SHIFT), kron[:64], NT, precision=HIGH, preferred_element_type=F32)
        twice = dot(both, qfull[...])
        top = twice.astype(BF16)
        rest = (twice - top.astype(F32)).astype(BF16)
        both_parts = jnp.concatenate([top[:64], rest[:64]], axis=0)
        mat[pl.ds(0, 128), :] = both_parts
        mat[pl.ds(128, 128), :] = both_parts

    def activation(rows):
        g = gate[:, rows].astype(F32)
        return g * (0.5 + 0.5 * jnp.tanh(0.5 * g))

    def project(rows, product, factor):
        up = (product * factor).astype(BF16)
        out64[...] += lax.dot_general(up, s64[:, rows], NT, preferred_element_type=F32)

    def first_part(j):
        rows = pl.ds(pl.multiple_of(j * BLOCK, BLOCK), BLOCK)
        hid[j] = lax.dot_general(
            ct[:, pl.ds(0, 2560)], w[rows, pl.ds(0, 2560)], NT, preferred_element_type=F32
        )
        act[j] = activation(rows)

    def second_part(j):
        rows = pl.ds(pl.multiple_of(j * BLOCK, BLOCK), BLOCK)
        product = hid[j] + lax.dot_general(
            ct[:, pl.ds(2560, 1536)], w[rows, pl.ds(2560, 1536)], NT, preferred_element_type=F32
        )
        project(rows, product, act[j])

    def whole(j):
        rows = pl.ds(pl.multiple_of(j * BLOCK, BLOCK), BLOCK)
        product = lax.dot_general(ct[...], w[rows, :], NT, preferred_element_type=F32)
        project(rows, product, activation(rows))

    def step_actions(i):
        part, j = SCHEDULE[i][1]
        for n, (arrivals, (what, at, which)) in enumerate(PLAN[i]):
            if i == 0 and n == EARLY:
                start("give", "input", "insigns", "query", "signs", "c", "gate", "bi", "bo", "ev")
            for stage, copy in arrivals:
                arrive(stage, copy)
            if what == 0:
                if (i, n) == GIVE_FIRST:
                    loaded("give")
                remote(at, which).start()
            elif what == 1:
                share_copy(at, which).start()
            elif what == 2:
                small[at]()
        if i == 0:
            loaded("c", "gate")
        for half in ((0,), (1,), (0, 1))[part]:
            shared(j, half)

    def block_of(step, part):
        j = jnp.int32(-1)
        for i, (_, (which, block)) in enumerate(SCHEDULE):
            if which == part:
                j = jnp.where(step == i, block, j)
        return j

    def step(k, _):
        for i in range(len(SCHEDULE)):
            pl.when(k == i)(functools.partial(step_actions, i))
        for part, compute in enumerate((first_part, second_part, whole)):
            j = block_of(k, part)
            pl.when(j >= 0)(functools.partial(compute, j))
        return 0

    def input_start():
        query_copy(0).start()
        query_copy(1).start()
        signs_copy().start()
        input_part()

    small = (
        input_start, query_far, input_sum, hidden_signs, query_z, input_weigh, query_sibling, query_matrix,
    )
    out64[...] = jnp.zeros_like(out64)
    lax.fori_loop(0, len(SCHEDULE), step, 0)

    rows = [
        jnp.sum(in64[pl.ds(e * SLOTS, SLOTS), :] * out64[pl.ds(e * SLOTS, SLOTS), :], axis=0, keepdims=True)
        for e in range(TOK // SLOTS)
    ]
    gbuf[tn] = jnp.zeros((8, 128), F32)
    for e in range(TOK // SLOTS):
        gbuf[tn, pl.ds(e, 1), :] = rows[e]

    def g_copy(i, owner):
        return pltpu.make_async_remote_copy(
            src_ref=gbuf.at[owner], dst_ref=gbuf.at[owner], send_sem=ss_g, recv_sem=rs_g,
            device_id=(dp, (zh + 1 - i // 4) % 2 * 4 + (y + FAR_FIRST[i % 4]) % 4), device_id_type=MESH,
        )

    for i in range(7):
        g_copy(i, tn).start()
    done(w.at[pl.ds(0, 928)], ss_w)
    done(w.at[:, pl.ds(0, 2048)], ss_s)
    done(qbuf.at[pl.ds(0, 15)], ss_q)
    done(ybuf, ss_y)
    signs_copy().wait_send()
    done(gbuf.at[pl.ds(0, 7)], rs_g)
    total = gbuf[0]
    for i in range(1, 8):
        total = total + gbuf[i]
    top = total.astype(BF16)
    rest = (total - top.astype(F32)).astype(BF16)
    both = jnp.concatenate([top, rest], axis=1)
    o_ref[...] = jnp.dot(both, mat[...], preferred_element_type=F32)[:4, :]
    done(gbuf.at[pl.ds(0, 7)], ss_g)


def on_device(
    layer_input, output_cotangent, gate_preact, down_weight, lengths, input_signs, hidden_signs,
    basis_in, basis_out, eigenvalues, query_grads,
):
    any_spec = pl.BlockSpec(memory_space=pl.ANY)
    vmem, dma = pltpu.VMEM, pltpu.SemaphoreType.DMA
    specs = [any_spec] * 11
    specs[4] = pl.BlockSpec(memory_space=pltpu.SMEM)
    return pl.pallas_call(
        kernel,
        out_shape=pltpu.VMEM((4, 512), F32),
        in_specs=specs,
        out_specs=pl.BlockSpec(memory_space=pltpu.VMEM),
        scratch_shapes=[
            vmem((HID, D), BF16),
            vmem((TOK, D), BF16),
            vmem((TOK, HID), BF16),
            vmem((BLOCK, COLS), BF16),
            vmem((TOK, BLOCK), BF16),
            vmem((TOK, BLOCK), BF16),
            vmem((TOK, 512), BF16),
            vmem((8, 512), jnp.int32),
            vmem((8, HID), jnp.int32),
            vmem((8, 8), F32),
            vmem((8, 8), F32),
            vmem((8, 8), F32),
            vmem((16, 4, 512), F32),
            vmem((64, 512), F32),
            vmem((256, 512), BF16),
            vmem((4, 8, TOK), F32),
            vmem((2, 8, TOK), F32),
            vmem((8, 8, 128), F32),
            vmem((TOK, 128), F32),
            vmem((128, HID), BF16),
            vmem((N, TOK, BLOCK), F32),
            vmem((N, TOK, BLOCK), F32),
            vmem((TOK, 128), F32),
            dma, dma((RECEIVE_SEMS,)), dma, dma((N, 2)), dma, dma((4,)), dma, dma, dma, dma, dma, dma, dma, dma((12,)),
        ],
        compiler_params=pltpu.CompilerParams(
            collective_id=0, has_side_effects=True, vmem_limit_bytes=56 * 1024 * 1024
        ),
        cost_estimate=pl.CostEstimate(flops=2 * TOK * HID * D, bytes_accessed=30_000_000, transcendentals=TOK * HID),
        name="scores",
    )(
        layer_input.reshape(TOK, 512),
        output_cotangent.reshape(TOK, D),
        gate_preact.reshape(TOK, HID),
        down_weight,
        lengths,
        input_signs.T,
        hidden_signs.T,
        basis_in,
        basis_out,
        eigenvalues,
        query_grads.T,
    )


def solution(mesh):
    in_specs = (
        P("dp", None, "tensor"),
        P("dp", None, None),
        P("dp", None, "tensor"),
        P("tensor", "dp"),
        P("dp"),
        P("tensor", None),
        P("tensor", None),
        P(),
        P(),
        P(),
        P("tensor", "dp"),
    )
    return jax.shard_map(
        on_device, mesh=mesh, in_specs=in_specs, out_specs=P("dp", "tensor"), check_vma=False
    )
```

```python
import functools

import jax
import jax.numpy as jnp
from jax import lax
from jax.experimental import pallas as pl
from jax.experimental.pallas import tpu as pltpu
from jax.sharding import PartitionSpec as P

MESH = pl.DeviceIdType.MESH
HIGH = lax.Precision.HIGHEST
F32, BF16 = jnp.float32, jnp.bfloat16
D, FF, RA, RG = 4096, 14336, 8, 8
SHIFT = 0.1
TOK, HID, COLS, SLOTS = 1024, 1792, 256, 256
BLOCK = 256
NT = (((1,), (1,)), ((), ()))

N = HID // BLOCK
PEER, GATES = N - 1, N
ALONG_X = (15, 15, 16, 16, 16)
SCHEDULE = (
    (
        (
            (0, 0, 0), (0, 0, 1), (0, 0, 2), (0, 1, 0), (0, 1, 1), (0, 1, 2), (0, 6, 0), (2, 0, 0),
            (0, 2, 0), (0, 2, 1), (0, 2, 2), (0, 7, 0), (0, 7, 1), (2, 2, 0), (0, 0, 3), (0, 0, 4),
            (0, 3, 2), (0, 6, 1), (0, 0, 5), (0, 0, 6), (2, 1, 0), (2, 3, 0), (0, 4, 2), (0, 7, 2),
            (0, 1, 4), (0, 1, 3), (0, 2, 4), (0, 2, 3), (0, 5, 2), (2, 5, 0), (0, 3, 1), (0, 6, 2),
            (1, 0, 0), (0, 3, 0), (0, 1, 8), (0, 1, 9), (0, 7, 4), (1, 0, 1), (2, 4, 0),
        ),
        (0, 0),
    ),
    (
        (
            (0, 0, 7), (0, 4, 0), (0, 0, 8), (0, 4, 1), (1, 1, 0), (1, 2, 0), (0, 1, 7),
        ),
        (0, 1),
    ),
    (
        (
            (0, 3, 3), (0, 5, 0), (0, 3, 4), (0, 5, 1), (0, 2, 7), (0, 7, 3),
        ),
        (0, 2),
    ),
    (
        (
            (0, 6, 3), (1, 0, 2), (0, 1, 6), (0, 2, 8), (0, 1, 5), (2, 6, 0), (0, 2, 9), (0, 7, 5),
        ),
        (1, 0),
    ),
    (
        (
            (0, 4, 3), (0, 4, 4), (1, 1, 2), (1, 3, 0), (1, 6, 1), (1, 6, 2), (0, 3, 7), (2, 7, 0),
            (0, 5, 3), (0, 5, 4), (1, 2, 2),
        ),
        (0, 3),
    ),
    (
        (
            (0, 2, 5), (0, 2, 6), (0, 7, 6), (1, 1, 1), (0, 3, 6), (0, 3, 5), (0, 7, 7), (1, 4, 0),
        ),
        (1, 1),
    ),
    (
        (
            (1, 5, 0), (0, 4, 6), (1, 3, 2), (0, 4, 5),
        ),
        (0, 4),
    ),
    (
        (
            (0, 4, 7), (1, 2, 1), (1, 6, 0),
        ),
        (0, 5),
    ),
    (
        (
            (0, 5, 5), (0, 5, 6), (0, 5, 7),
        ),
        (1, 2),
    ),
    (
        (
            (1, 3, 1),
        ),
        (2, 6),
    ),
    (
        (
            (1, 4, 1), (1, 4, 2),
        ),
        (1, 3),
    ),
    (
        (
            (1, 5, 1), (1, 5, 2),
        ),
        (1, 4),
    ),
    (
        (
        ),
        (1, 5),
    ),
)

O, L, R, FAR, Z, ZL, ZR, ZF = range(8)
FAR_FIRST = (2, 1, 3, 0)


def copies(stage):
    rows, half = BLOCK, BLOCK // 2
    hop1 = [(O, 0, rows, "xp", L), (O, 0, rows, "xm", R), (O, 0, rows, "z", Z)]
    far = [(L, 0, half, "xp", FAR), (R, half, rows, "xm", FAR)]
    if stage == 0:
        return hop1 + far + [
            (Z, 0, rows, "xp", ZL),
            (Z, 0, rows, "xm", ZR),
            (ZL, 0, half, "xp", ZF),
            (ZR, half, rows, "xm", ZF),
        ]
    if stage == PEER:
        return [(O, 0, rows, "cross", Z), (Z, 0, rows, "cross", O), (L, 0, rows, "cross", ZL), (ZL, 0, rows, "cross", L)]
    if stage == GATES:
        return [None] * 8
    part = 16 * ALONG_X[stage - 1]
    return hop1 + far + [
        (Z, 0, part, "xp", ZL),
        (Z, 0, part, "xm", ZR),
        (FAR, 0, rows, "z", ZF),
    ] + [(L, part, rows, "z", ZL), (R, part, rows, "z", ZR)] * (part < rows)


def after(stage, i):
    if stage == PEER:
        return [(0, j) for j in ((), (2,), (0, 1, 3, 4), (5, 6, 7, 8))[i]]
    if stage == GATES:
        return [(GATES, i - 4)] if i >= 4 else []
    if stage == 0:
        return [(0, j) for j in ((), (), (), (0,), (1,), (2,), (2,), (5,), (6,))[i]]
    return [(stage, j) for j in ((), (), (), (0,), (1,), (2,), (2,), (3, 4), (0,), (1,))[i]]


GROUPS = ((0, 1280), (2560, 512), (3072, 256))


def brought(stage, group):
    if stage == PEER:
        which = ((0, 1, 3), (2,), (2,))[group]
    elif stage == 0:
        which = ((0, 1, 2, 3, 4), (5, 6), (7, 8))[group]
    else:
        which = ((0, 1, 2, 3, 4), (5, 6, 8, 9), (7,))[group]
    return [(stage, i) for i in which if i < len(copies(stage))]


def bundle(stage, i):
    if stage == PEER:
        return (0, 0, 1, 0)[i]
    if stage == GATES:
        return min(i, 4)
    if stage == 0:
        return (0, 1, 2, 3, 3, 4, 4, 5, 5)[i]
    return (0, 1, 2, 3, 3, 4, 4, 5, 4, 4)[i]


def receive_sem(stage, which):
    return stage * 6 + which if stage <= PEER else PEER * 6 + 2 + which


RECEIVE_SEMS = PEER * 6 + 2 + 5


def plan():
    arrived, steps = set(), []
    for actions, (part, block) in SCHEDULE:
        steps.append([])
        for what, at, which in actions + ((3, part, block),):
            needed = ()
            if what == 0:
                needed = after(at, which)
            elif what == 1:
                needed = brought(at, which)
            elif what == 3 and part != 1 and block == PEER:
                needed = [(GATES, i) for i in range(4, 8)]
            new = sorted({(at, bundle(at, i)) for at, i in needed} - arrived)
            arrived.update(new)
            steps[-1].append((new, (what, at, which)))
    return steps


PLAN = plan()
GIVE_FIRST = min(
    (i, n) for i, step in enumerate(PLAN) for n, (_, (what, at, which)) in enumerate(step) if (what, at) == (0, GATES) and which < 4
)
EARLY = 3


def column(slot):
    return slot * COLS if slot < 5 else 2560 + (slot - 5) * COLS


def sibling_column(col):
    return col + (1280 if col < 1280 else 768)


def kernel(
    li_hbm, ct_hbm, gate_hbm, w_hbm, len_ref, sin_hbm, shid_hbm, bi_hbm, bo_hbm, ev_hbm, q_hbm,
    o_ref,
    w, ct, gate, give_w, give_gate, relay, li, sin, shid, bi, bo, ev, qbuf, qfull, mat, ybuf, zbuf, gbuf, in64, s64, hid, act, out64,
    ss_w, rs_w, ss_s, rs_s, ss_q, rs_q, ss_y, rs_y, rs_z, ss_h, rs_h, ss_g, rs_g, lsem,
):
    dp, tn = lax.axis_index("dp"), lax.axis_index("tensor")
    x, z, c = dp // 4, (dp // 2) % 2, dp % 2
    zh, y = tn // 4, tn % 4
    xp, xm = (x + 1) % 4, (x + 3) % 4
    at = lambda xx, zz, cc: xx * 4 + zz * 2 + cc
    dev = {
        "xp": (at(xp, z, c), tn),
        "xm": (at(xm, z, c), tn),
        "z": (at(x, 1 - z, c), tn),
        "sib": (at(x, z, 1 - c), tn),
        "cross": (at(x, 1 - z, c), (1 - zh) * 4 + y),
        "peer": (dp, (1 - zh) * 4 + y),
    }

    kept = pl.multiple_of((5 + z) * BLOCK, BLOCK)
    given = pl.multiple_of((6 - z) * BLOCK, BLOCK)
    plain = (N - 2) * BLOCK
    q_me = c * 8 + z * 4 + x

    def quarter(i):
        return pl.ds(i * SLOTS, SLOTS)

    def done(ref, sem):
        pltpu.make_async_copy(ref, ref, sem).wait()

    NAMES = ("own", "plain", "give", "input", "insigns", "query", "signs", "c", "gate", "bi", "bo", "ev")

    def start(*names):
        for name in names:
            for src, dst in copies_in[name]():
                pltpu.make_async_copy(src, dst, lsem.at[NAMES.index(name)]).start()

    def loaded(*names):
        whole_of = {
            "own": w.at[pl.ds(0, 2 * BLOCK), pl.ds(0, COLS)],
            "plain": w.at[pl.ds(BLOCK, plain), pl.ds(0, COLS)],
            "give": give_gate, "input": li, "insigns": sin, "query": qbuf.at[q_me],
            "signs": shid.at[:, pl.ds(0, plain + BLOCK)], "c": ct, "gate": gate.at[:, pl.ds(0, plain + BLOCK)],
            "bi": bi, "bo": bo, "ev": ev,
        }
        for name in names:
            done(whole_of[name], lsem.at[NAMES.index(name)])

    def load_c():
        found = []
        far = (x + 2) % 4
        for half in range(2):
            cc = c if half == 0 else 1 - c
            for slot, (xx, zz) in enumerate(
                ((x, z), (xm, z), (xp, z), (far, z), (x, 1 - z), (xm, 1 - z), (xp, 1 - z), (far, 1 - z))
            ):
                first = pl.multiple_of(at(xx, zz, cc) * COLS, COLS)
                col = sibling_column(column(slot)) if half else column(slot)
                found.append((ct_hbm.at[:, pl.ds(first, COLS)], ct.at[:, pl.ds(col, COLS)]))
        return found

    def by_place(src, dst):
        return [
            (src.at[:, pl.ds(kept, BLOCK)], dst.at[:, pl.ds(0, BLOCK)]),
            (src.at[:, pl.ds(0, plain)], dst.at[:, pl.ds(BLOCK, plain)]),
        ]

    copies_in = {
        "own": lambda: [
            (w_hbm.at[pl.ds(kept, BLOCK)], w.at[pl.ds(0, BLOCK), pl.ds(0, COLS)]),
            (w_hbm.at[pl.ds(given, BLOCK)], give_w),
        ],
        "plain": lambda: [(w_hbm.at[pl.ds(0, plain)], w.at[pl.ds(BLOCK, plain), pl.ds(0, COLS)])],
        "give": lambda: [(gate_hbm.at[:, pl.ds(given, BLOCK)], give_gate)],
        "input": lambda: [(li_hbm, li)],
        "insigns": lambda: [(sin_hbm, sin)],
        "query": lambda: [(q_hbm, qbuf.at[q_me])],
        "signs": lambda: by_place(shid_hbm, shid),
        "c": load_c,
        "gate": lambda: by_place(gate_hbm, gate),
        "bi": lambda: [(bi_hbm, bi)],
        "bo": lambda: [(bo_hbm, bo)],
        "ev": lambda: [(ev_hbm, ev)],
    }

    start("own", "plain")
    barrier = pltpu.get_barrier_semaphore()
    for i in range(7):
        peer = (dp, (zh + 1 - i // 4) % 2 * 4 + (y + FAR_FIRST[i % 4]) % 4)
        pl.semaphore_signal(barrier, inc=1, device_id=peer, device_id_type=MESH)
    for name in ("xp", "xm", "z", "cross", "sib"):
        pl.semaphore_signal(barrier, inc=1, device_id=dev[name], device_id_type=MESH)
    pl.semaphore_wait(barrier, 12)
    loaded("own")

    def remote(stage, i):
        if stage == GATES:
            rows = quarter(i % 4)
            to = ("cross", "z")[i // 4]
            src = (give_gate, relay)[i // 4].at[rows]
            dst = (relay.at[rows], gate.at[rows, pl.ds(PEER * BLOCK, BLOCK)])[i // 4]
        else:
            piece, low, high, to, there = copies(stage)[i]
            from_rows = pl.ds((0 if stage == PEER else stage * BLOCK) + low, high - low)
            rows = pl.ds(stage * BLOCK + low, high - low)
            cols = 3 * COLS if stage == PEER and i >= 2 else COLS
            src = w.at[from_rows, pl.ds(column(piece), cols)]
            if stage == 0 and i == 2:
                src = give_w
            dst = w.at[rows, pl.ds(column(there), cols)]
        return pltpu.make_async_remote_copy(
            src_ref=src, dst_ref=dst, send_sem=ss_w, recv_sem=rs_w.at[receive_sem(stage, bundle(stage, i))],
            device_id=dev[to], device_id_type=MESH,
        )

    def arrive(stage, which):
        if stage == GATES:
            ref = relay.at[quarter(which)] if which < 4 else gate.at[:, pl.ds(PEER * BLOCK, BLOCK)]
        else:
            if stage == PEER:
                col, cols = ((0, 5 * COLS), (column(ZL), 3 * COLS))[which]
            else:
                col, cols = (column((L, R, Z, FAR, ZL, ZF)[which]), 2 * COLS if which == 4 else COLS)
            ref = w.at[pl.ds(stage * BLOCK, BLOCK), pl.ds(col, cols)]
        done(ref, rs_w.at[receive_sem(stage, which)])

    def share_copy(stage, group):
        rows = pl.ds(stage * BLOCK, BLOCK)
        col, cols = GROUPS[group]
        return pltpu.make_async_remote_copy(
            src_ref=w.at[rows, pl.ds(col, cols)], dst_ref=w.at[rows, pl.ds(sibling_column(col), cols)],
            send_sem=ss_s, recv_sem=rs_s.at[stage, min(group, 1)],
            device_id=dev["sib"], device_id_type=MESH,
        )

    def shared(stage, part):
        col, cols = ((0, 1280), (2560, 768))[part]
        done(w.at[pl.ds(stage * BLOCK, BLOCK), pl.ds(sibling_column(col), cols)], rs_s.at[stage, part])

    row8 = lax.broadcasted_iota(jnp.int32, (8, 128), 0)
    col8 = lax.broadcasted_iota(jnp.int32, (8, 128), 1)
    by_b = (col8 % 8 == row8).astype(F32)
    by_a = (col8 % 64 // 8 == row8).astype(F32)
    row_t = lax.broadcasted_iota(jnp.int32, (128, 8), 0)
    col_t = lax.broadcasted_iota(jnp.int32, (128, 8), 1)
    by_b_t = (row_t % 8 == col_t).astype(F32)
    by_a_t = (row_t % 64 // 8 == col_t).astype(F32)
    dot = functools.partial(jnp.dot, precision=HIGH, preferred_element_type=F32)

    def query_copy(i, receiving=False):
        mine = c * 8 + z * 4
        src, dst, to = (
            (q_hbm, qbuf.at[mine + (xm if receiving else x)], "xp"),
            (q_hbm, qbuf.at[mine + (xp if receiving else x)], "xm"),
            (qbuf.at[mine + xm], qbuf.at[mine + ((x + 2) % 4 if receiving else xm)], "xp"),
            (qbuf.at[pl.ds(mine, 4)], qbuf.at[pl.ds(c * 8 + (1 - z) * 4 if receiving else mine, 4)], "z"),
            (qbuf.at[pl.ds(c * 8, 8)], qbuf.at[pl.ds((1 - c) * 8 if receiving else c * 8, 8)], "sib"),
        )[i]
        return pltpu.make_async_remote_copy(
            src_ref=src, dst_ref=dst, send_sem=ss_q, recv_sem=rs_q.at[(0, 1, 1, 2, 3)[i]],
            device_id=dev[to], device_id_type=MESH,
        )

    def query_far():
        query_copy(0, True).wait_recv()
        query_copy(2).start()

    def query_z():
        done(qbuf.at[pl.ds(c * 8 + z * 4, 2)], rs_q.at[1])
        loaded("query")
        query_copy(3).start()

    def query_sibling():
        query_copy(3, True).wait_recv()
        query_copy(4).start()

    def y_copy(i, owner):
        return pltpu.make_async_remote_copy(
            src_ref=ybuf.at[owner], dst_ref=ybuf.at[owner], send_sem=ss_y, recv_sem=rs_y,
            device_id=(dp, zh * 4 + (y + i) % 4), device_id_type=MESH,
        )

    def z_copy(owner):
        return pltpu.make_async_remote_copy(
            src_ref=zbuf.at[owner], dst_ref=zbuf.at[owner], send_sem=ss_y, recv_sem=rs_z,
            device_id=(dp, (1 - zh) * 4 + y), device_id_type=MESH,
        )

    def signs_copy():
        return pltpu.make_async_remote_copy(
            src_ref=shid_hbm.at[:, pl.ds(given, BLOCK)], dst_ref=shid.at[:, pl.ds(PEER * BLOCK, BLOCK)],
            send_sem=ss_h, recv_sem=rs_h, device_id=dev["peer"], device_id_type=MESH,
        )

    def input_part():
        loaded("input", "insigns")
        sign = (2 * sin[...] - 1).astype(F32).astype(BF16)
        ybuf[y] = lax.dot_general(sign, li[...], NT, preferred_element_type=F32) * D ** (-0.5)
        for i in range(1, 4):
            y_copy(i, y).start()

    def input_sum():
        done(ybuf.at[pl.ds(0, 3)], rs_y)
        zbuf[zh] = ybuf[0] + ybuf[1] + ybuf[2] + ybuf[3]
        z_copy(zh).start()

    def input_weigh():
        z_copy(1 - zh).wait_recv()
        full = zbuf[0] + zbuf[1]
        pos = lax.broadcasted_iota(jnp.int32, (8, SLOTS), 1)
        for e in range(TOK // SLOTS):
            count = len_ref[e]
            scale = FF ** (-0.5) / count.astype(F32)
            part = full[:, e * SLOTS : (e + 1) * SLOTS]
            part = jnp.where(pos < count, part * scale, 0.0)
            in64[pl.ds(e * SLOTS, SLOTS), :] = dot(part.T, by_a)

    def hidden_signs():
        loaded("signs")
        signs_copy().wait_recv()
        sign = (2 * shid[...] - 1).astype(F32)
        s64[...] = jnp.dot(by_b_t.astype(BF16), sign.astype(BF16), preferred_element_type=F32).astype(BF16)

    def query_matrix():
        loaded("bi", "bo", "ev")
        query_copy(4, True).wait_recv()
        for i in range(16):
            owner = i % 4 * 4 + i // 4 % 2 * 2 + i // 8
            qfull[pl.ds(4 * owner, 4), :] = qbuf[i]
        kron = dot(dot(by_a_t, bi[...]), by_a[:, :64]) * dot(dot(by_b_t, bo[...]), by_b[:, :64])
        values = jnp.sum(dot(ev[...], by_b[:, :64]) * by_a[:, :64], axis=0, keepdims=True)
        both = lax.dot_general(kron / (values + SHIFT), kron[:64], NT, precision=HIGH, preferred_element_type=F32)
        twice = dot(both, qfull[...])
        top = twice.astype(BF16)
        rest = (twice - top.astype(F32)).astype(BF16)
        both_parts = jnp.concatenate([top[:64], rest[:64]], axis=0)
        mat[pl.ds(0, 128), :] = both_parts
        mat[pl.ds(128, 128), :] = both_parts

    def activation(rows):
        g = gate[:, rows].astype(F32)
        return g * (0.5 + 0.5 * jnp.tanh(0.5 * g))

    def project(rows, product, factor):
        up = (product * factor).astype(BF16)
        out64[...] += lax.dot_general(up, s64[:, rows], NT, preferred_element_type=F32)

    def first_part(j):
        rows = pl.ds(pl.multiple_of(j * BLOCK, BLOCK), BLOCK)
        hid[j] = lax.dot_general(
            ct[:, pl.ds(0, 2560)], w[rows, pl.ds(0, 2560)], NT, preferred_element_type=F32
        )
        act[j] = activation(rows)

    def second_part(j):
        rows = pl.ds(pl.multiple_of(j * BLOCK, BLOCK), BLOCK)
        product = hid[j] + lax.dot_general(
            ct[:, pl.ds(2560, 1536)], w[rows, pl.ds(2560, 1536)], NT, preferred_element_type=F32
        )
        project(rows, product, act[j])

    def whole(j):
        rows = pl.ds(pl.multiple_of(j * BLOCK, BLOCK), BLOCK)
        product = lax.dot_general(ct[...], w[rows, :], NT, preferred_element_type=F32)
        project(rows, product, activation(rows))

    def step_actions(i):
        part, j = SCHEDULE[i][1]
        for n, (arrivals, (what, at, which)) in enumerate(PLAN[i]):
            if i == 0 and n == EARLY:
                start("give", "input", "insigns", "query", "signs", "c", "gate", "bi", "bo", "ev")
                loaded("plain")
            for stage, copy in arrivals:
                arrive(stage, copy)
            if what == 0:
                if (i, n) == GIVE_FIRST:
                    loaded("give")
                remote(at, which).start()
            elif what == 1:
                share_copy(at, which).start()
            elif what == 2:
                small[at]()
        if i == 0:
            loaded("c", "gate")
        for half in ((0,), (1,), (0, 1))[part]:
            shared(j, half)

    def block_of(step, part):
        j = jnp.int32(-1)
        for i, (_, (which, block)) in enumerate(SCHEDULE):
            if which == part:
                j = jnp.where(step == i, block, j)
        return j

    def step(k, _):
        for i in range(len(SCHEDULE)):
            pl.when(k == i)(functools.partial(step_actions, i))
        for part, compute in enumerate((first_part, second_part, whole)):
            j = block_of(k, part)
            pl.when(j >= 0)(functools.partial(compute, j))
        return 0

    def input_start():
        query_copy(0).start()
        query_copy(1).start()
        signs_copy().start()
        input_part()

    small = (
        input_start, query_far, input_sum, hidden_signs, query_z, input_weigh, query_sibling, query_matrix,
    )
    out64[...] = jnp.zeros_like(out64)
    lax.fori_loop(0, len(SCHEDULE), step, 0)

    rows = [
        jnp.sum(in64[pl.ds(e * SLOTS, SLOTS), :] * out64[pl.ds(e * SLOTS, SLOTS), :], axis=0, keepdims=True)
        for e in range(TOK // SLOTS)
    ]
    gbuf[tn] = jnp.zeros((8, 128), F32)
    for e in range(TOK // SLOTS):
        gbuf[tn, pl.ds(e, 1), :] = rows[e]

    def g_copy(i, owner):
        return pltpu.make_async_remote_copy(
            src_ref=gbuf.at[owner], dst_ref=gbuf.at[owner], send_sem=ss_g, recv_sem=rs_g,
            device_id=(dp, (zh + 1 - i // 4) % 2 * 4 + (y + FAR_FIRST[i % 4]) % 4), device_id_type=MESH,
        )

    for i in range(7):
        g_copy(i, tn).start()
    done(w.at[pl.ds(0, 928)], ss_w)
    done(w.at[:, pl.ds(0, 2048)], ss_s)
    done(qbuf.at[pl.ds(0, 15)], ss_q)
    done(ybuf, ss_y)
    signs_copy().wait_send()
    done(gbuf.at[pl.ds(0, 7)], rs_g)
    total = gbuf[0]
    for i in range(1, 8):
        total = total + gbuf[i]
    top = total.astype(BF16)
    rest = (total - top.astype(F32)).astype(BF16)
    both = jnp.concatenate([top, rest], axis=1)
    o_ref[...] = jnp.dot(both, mat[...], preferred_element_type=F32)[:4, :]
    done(gbuf.at[pl.ds(0, 7)], ss_g)


def on_device(
    layer_input, output_cotangent, gate_preact, down_weight, lengths, input_signs, hidden_signs,
    basis_in, basis_out, eigenvalues, query_grads,
):
    any_spec = pl.BlockSpec(memory_space=pl.ANY)
    vmem, dma = pltpu.VMEM, pltpu.SemaphoreType.DMA
    specs = [any_spec] * 11
    specs[4] = pl.BlockSpec(memory_space=pltpu.SMEM)
    return pl.pallas_call(
        kernel,
        out_shape=pltpu.VMEM((4, 512), F32),
        in_specs=specs,
        out_specs=pl.BlockSpec(memory_space=pltpu.VMEM),
        scratch_shapes=[
            vmem((HID, D), BF16),
            vmem((TOK, D), BF16),
            vmem((TOK, HID), BF16),
            vmem((BLOCK, COLS), BF16),
            vmem((TOK, BLOCK), BF16),
            vmem((TOK, BLOCK), BF16),
            vmem((TOK, 512), BF16),
            vmem((8, 512), jnp.int32),
            vmem((8, HID), jnp.int32),
            vmem((8, 8), F32),
            vmem((8, 8), F32),
            vmem((8, 8), F32),
            vmem((16, 4, 512), F32),
            vmem((64, 512), F32),
            vmem((256, 512), BF16),
            vmem((4, 8, TOK), F32),
            vmem((2, 8, TOK), F32),
            vmem((8, 8, 128), F32),
            vmem((TOK, 128), F32),
            vmem((128, HID), BF16),
            vmem((N, TOK, BLOCK), F32),
            vmem((N, TOK, BLOCK), F32),
            vmem((TOK, 128), F32),
            dma, dma((RECEIVE_SEMS,)), dma, dma((N, 2)), dma, dma((4,)), dma, dma, dma, dma, dma, dma, dma, dma((12,)),
        ],
        compiler_params=pltpu.CompilerParams(
            collective_id=0, has_side_effects=True, vmem_limit_bytes=56 * 1024 * 1024
        ),
        cost_estimate=pl.CostEstimate(flops=2 * TOK * HID * D, bytes_accessed=30_000_000, transcendentals=TOK * HID),
        name="scores",
    )(
        layer_input.reshape(TOK, 512),
        output_cotangent.reshape(TOK, D),
        gate_preact.reshape(TOK, HID),
        down_weight,
        lengths,
        input_signs.T,
        hidden_signs.T,
        basis_in,
        basis_out,
        eigenvalues,
        query_grads.T,
    )


def solution(mesh):
    in_specs = (
        P("dp", None, "tensor"),
        P("dp", None, None),
        P("dp", None, "tensor"),
        P("tensor", "dp"),
        P("dp"),
        P("tensor", None),
        P("tensor", None),
        P(),
        P(),
        P(),
        P("tensor", "dp"),
    )
    return jax.shard_map(
        on_device, mesh=mesh, in_specs=in_specs, out_specs=P("dp", "tensor"), check_vma=False
    )
```

```python
import functools

import jax
import jax.numpy as jnp
from jax import lax
from jax.experimental import pallas as pl
from jax.experimental.pallas import tpu as pltpu
from jax.sharding import PartitionSpec as P

MESH = pl.DeviceIdType.MESH
HIGH = lax.Precision.HIGHEST
F32, BF16 = jnp.float32, jnp.bfloat16
D, FF, RA, RG = 4096, 14336, 8, 8
SHIFT = 0.1
TOK, HID, COLS, SLOTS = 1024, 1792, 256, 256
BLOCK = 256
NT = (((1,), (1,)), ((), ()))

N = HID // BLOCK
PEER, GATES = N - 1, N
ALONG_X = (15, 15, 16, 16, 16)
SCHEDULE = (
    (
        (
            (0, 0, 0), (0, 0, 1), (0, 0, 2), (0, 1, 0), (0, 1, 1), (0, 1, 2), (0, 6, 0), (2, 0, 0),
            (0, 2, 0), (0, 2, 1), (0, 2, 2), (0, 7, 0), (0, 7, 1), (2, 2, 0), (0, 0, 3), (0, 0, 4),
            (0, 3, 2), (0, 6, 1), (0, 0, 5), (0, 0, 6), (2, 1, 0), (2, 3, 0), (0, 4, 2), (0, 7, 2),
            (0, 1, 4), (0, 1, 3), (0, 2, 4), (0, 2, 3), (0, 5, 2), (2, 5, 0), (0, 3, 1), (0, 6, 2),
            (1, 0, 0), (0, 3, 0), (0, 1, 8), (0, 1, 9), (0, 7, 4), (1, 0, 1), (2, 4, 0),
        ),
        (0, 0),
    ),
    (
        (
            (0, 0, 7), (0, 4, 0), (0, 0, 8), (0, 4, 1), (1, 1, 0), (1, 2, 0), (0, 1, 7),
        ),
        (0, 1),
    ),
    (
        (
            (0, 3, 3), (0, 5, 0), (0, 3, 4), (0, 5, 1), (0, 2, 7), (0, 7, 3),
        ),
        (0, 2),
    ),
    (
        (
            (0, 6, 3), (1, 0, 2), (0, 1, 6), (0, 2, 8), (0, 1, 5), (2, 6, 0), (0, 2, 9), (0, 7, 5),
        ),
        (1, 0),
    ),
    (
        (
            (0, 4, 3), (0, 4, 4), (1, 1, 2), (1, 3, 0), (1, 6, 1), (1, 6, 2), (0, 3, 7), (2, 7, 0),
            (0, 5, 3), (0, 5, 4), (1, 2, 2),
        ),
        (0, 3),
    ),
    (
        (
            (0, 2, 5), (0, 2, 6), (0, 7, 6), (1, 1, 1), (0, 3, 6), (0, 3, 5), (0, 7, 7), (1, 4, 0),
        ),
        (1, 1),
    ),
    (
        (
            (1, 5, 0), (0, 4, 6), (1, 3, 2), (0, 4, 5),
        ),
        (0, 4),
    ),
    (
        (
            (0, 4, 7), (1, 2, 1), (1, 6, 0),
        ),
        (0, 5),
    ),
    (
        (
            (0, 5, 5), (0, 5, 6), (0, 5, 7),
        ),
        (1, 2),
    ),
    (
        (
            (1, 3, 1),
        ),
        (2, 6),
    ),
    (
        (
            (1, 4, 1), (1, 4, 2),
        ),
        (1, 3),
    ),
    (
        (
            (1, 5, 1), (1, 5, 2),
        ),
        (1, 4),
    ),
    (
        (
        ),
        (1, 5),
    ),
)

O, L, R, FAR, Z, ZL, ZR, ZF = range(8)
FAR_FIRST = (2, 1, 3, 0)


def copies(stage):
    rows, half = BLOCK, BLOCK // 2
    hop1 = [(O, 0, rows, "xp", L), (O, 0, rows, "xm", R), (O, 0, rows, "z", Z)]
    far = [(L, 0, half, "xp", FAR), (R, half, rows, "xm", FAR)]
    if stage == 0:
        return hop1 + far + [
            (Z, 0, rows, "xp", ZL),
            (Z, 0, rows, "xm", ZR),
            (ZL, 0, half, "xp", ZF),
            (ZR, half, rows, "xm", ZF),
        ]
    if stage == PEER:
        return [(O, 0, rows, "cross", Z), (Z, 0, rows, "cross", O), (L, 0, rows, "cross", ZL), (ZL, 0, rows, "cross", L)]
    if stage == GATES:
        return [None] * 8
    part = 16 * ALONG_X[stage - 1]
    return hop1 + far + [
        (Z, 0, part, "xp", ZL),
        (Z, 0, part, "xm", ZR),
        (FAR, 0, rows, "z", ZF),
    ] + [(L, part, rows, "z", ZL), (R, part, rows, "z", ZR)] * (part < rows)


def after(stage, i):
    if stage == PEER:
        return [(0, j) for j in ((), (2,), (0, 1, 3, 4), (5, 6, 7, 8))[i]]
    if stage == GATES:
        return [(GATES, i - 4)] if i >= 4 else []
    if stage == 0:
        return [(0, j) for j in ((), (), (), (0,), (1,), (2,), (2,), (5,), (6,))[i]]
    return [(stage, j) for j in ((), (), (), (0,), (1,), (2,), (2,), (3, 4), (0,), (1,))[i]]


GROUPS = ((0, 1280), (2560, 512), (3072, 256))


def brought(stage, group):
    if stage == PEER:
        which = ((0, 1, 3), (2,), (2,))[group]
    elif stage == 0:
        which = ((0, 1, 2, 3, 4), (5, 6), (7, 8))[group]
    else:
        which = ((0, 1, 2, 3, 4), (5, 6, 8, 9), (7,))[group]
    return [(stage, i) for i in which if i < len(copies(stage))]


def bundle(stage, i):
    if stage == PEER:
        return (0, 0, 1, 0)[i]
    if stage == GATES:
        return min(i, 4)
    if stage == 0:
        return (0, 1, 2, 3, 3, 4, 4, 5, 5)[i]
    return (0, 1, 2, 3, 3, 4, 4, 5, 4, 4)[i]


def receive_sem(stage, which):
    return stage * 6 + which if stage <= PEER else PEER * 6 + 2 + which


RECEIVE_SEMS = PEER * 6 + 2 + 5


def plan():
    arrived, steps = set(), []
    for actions, (part, block) in SCHEDULE:
        steps.append([])
        for what, at, which in actions + ((3, part, block),):
            needed = ()
            if what == 0:
                needed = after(at, which)
            elif what == 1:
                needed = brought(at, which)
            elif what == 3 and part != 1 and block == PEER:
                needed = [(GATES, i) for i in range(4, 8)]
            new = sorted({(at, bundle(at, i)) for at, i in needed} - arrived)
            arrived.update(new)
            steps[-1].append((new, (what, at, which)))
    return steps


PLAN = plan()
GIVE_FIRST = min(
    (i, n) for i, step in enumerate(PLAN) for n, (_, (what, at, which)) in enumerate(step) if (what, at) == (0, GATES) and which < 4
)
EARLY = 7


def column(slot):
    return slot * COLS if slot < 5 else 2560 + (slot - 5) * COLS


def sibling_column(col):
    return col + (1280 if col < 1280 else 768)


def kernel(
    li_hbm, ct_hbm, gate_hbm, w_hbm, len_ref, sin_hbm, shid_hbm, bi_hbm, bo_hbm, ev_hbm, q_hbm,
    o_ref,
    w, ct, gate, give_w, give_gate, relay, li, sin, shid, bi, bo, ev, qbuf, qfull, mat, ybuf, zbuf, gbuf, in64, s64, hid, act, out64,
    ss_w, rs_w, ss_s, rs_s, ss_q, rs_q, ss_y, rs_y, rs_z, ss_h, rs_h, ss_g, rs_g, lsem,
):
    dp, tn = lax.axis_index("dp"), lax.axis_index("tensor")
    x, z, c = dp // 4, (dp // 2) % 2, dp % 2
    zh, y = tn // 4, tn % 4
    xp, xm = (x + 1) % 4, (x + 3) % 4
    at = lambda xx, zz, cc: xx * 4 + zz * 2 + cc
    dev = {
        "xp": (at(xp, z, c), tn),
        "xm": (at(xm, z, c), tn),
        "z": (at(x, 1 - z, c), tn),
        "sib": (at(x, z, 1 - c), tn),
        "cross": (at(x, 1 - z, c), (1 - zh) * 4 + y),
        "peer": (dp, (1 - zh) * 4 + y),
    }

    kept = pl.multiple_of((5 + z) * BLOCK, BLOCK)
    given = pl.multiple_of((6 - z) * BLOCK, BLOCK)
    plain = (N - 2) * BLOCK
    q_me = c * 8 + z * 4 + x

    def quarter(i):
        return pl.ds(i * SLOTS, SLOTS)

    def done(ref, sem):
        pltpu.make_async_copy(ref, ref, sem).wait()

    NAMES = ("own", "plain", "give", "input", "insigns", "query", "signs", "c", "gate", "bi", "bo", "ev")

    def start(*names):
        for name in names:
            for src, dst in copies_in[name]():
                pltpu.make_async_copy(src, dst, lsem.at[NAMES.index(name)]).start()

    def loaded(*names):
        whole_of = {
            "own": w.at[pl.ds(0, 2 * BLOCK), pl.ds(0, COLS)],
            "plain": w.at[pl.ds(BLOCK, plain), pl.ds(0, COLS)],
            "give": give_gate, "input": li, "insigns": sin, "query": qbuf.at[q_me],
            "signs": shid.at[:, pl.ds(0, plain + BLOCK)], "c": ct, "gate": gate.at[:, pl.ds(0, plain + BLOCK)],
            "bi": bi, "bo": bo, "ev": ev,
        }
        for name in names:
            done(whole_of[name], lsem.at[NAMES.index(name)])

    def load_c():
        found = []
        far = (x + 2) % 4
        for half in range(2):
            cc = c if half == 0 else 1 - c
            for slot, (xx, zz) in enumerate(
                ((x, z), (xm, z), (xp, z), (far, z), (x, 1 - z), (xm, 1 - z), (xp, 1 - z), (far, 1 - z))
            ):
                first = pl.multiple_of(at(xx, zz, cc) * COLS, COLS)
                col = sibling_column(column(slot)) if half else column(slot)
                found.append((ct_hbm.at[:, pl.ds(first, COLS)], ct.at[:, pl.ds(col, COLS)]))
        return found

    def by_place(src, dst):
        return [
            (src.at[:, pl.ds(kept, BLOCK)], dst.at[:, pl.ds(0, BLOCK)]),
            (src.at[:, pl.ds(0, plain)], dst.at[:, pl.ds(BLOCK, plain)]),
        ]

    copies_in = {
        "own": lambda: [
            (w_hbm.at[pl.ds(kept, BLOCK)], w.at[pl.ds(0, BLOCK), pl.ds(0, COLS)]),
            (w_hbm.at[pl.ds(given, BLOCK)], give_w),
        ],
        "plain": lambda: [(w_hbm.at[pl.ds(0, plain)], w.at[pl.ds(BLOCK, plain), pl.ds(0, COLS)])],
        "give": lambda: [(gate_hbm.at[:, pl.ds(given, BLOCK)], give_gate)],
        "input": lambda: [(li_hbm, li)],
        "insigns": lambda: [(sin_hbm, sin)],
        "query": lambda: [(q_hbm, qbuf.at[q_me])],
        "signs": lambda: by_place(shid_hbm, shid),
        "c": load_c,
        "gate": lambda: by_place(gate_hbm, gate),
        "bi": lambda: [(bi_hbm, bi)],
        "bo": lambda: [(bo_hbm, bo)],
        "ev": lambda: [(ev_hbm, ev)],
    }

    start("own", "plain")
    barrier = pltpu.get_barrier_semaphore()
    for name in ("xp", "xm", "z", "sib", "cross"):
        pl.semaphore_signal(barrier, inc=1, device_id=dev[name], device_id_type=MESH)
    for i in range(1, 8):
        pl.semaphore_signal(barrier, inc=1, device_id=(dp, (tn + i) % 8), device_id_type=MESH)
    pl.semaphore_wait(barrier, 12)
    loaded("own", "plain")

    def remote(stage, i):
        if stage == GATES:
            rows = quarter(i % 4)
            to = ("cross", "z")[i // 4]
            src = (give_gate, relay)[i // 4].at[rows]
            dst = (relay.at[rows], gate.at[rows, pl.ds(PEER * BLOCK, BLOCK)])[i // 4]
        else:
            piece, low, high, to, there = copies(stage)[i]
            from_rows = pl.ds((0 if stage == PEER else stage * BLOCK) + low, high - low)
            rows = pl.ds(stage * BLOCK + low, high - low)
            cols = 3 * COLS if stage == PEER and i >= 2 else COLS
            src = w.at[from_rows, pl.ds(column(piece), cols)]
            if stage == 0 and i == 2:
                src = give_w
            dst = w.at[rows, pl.ds(column(there), cols)]
        return pltpu.make_async_remote_copy(
            src_ref=src, dst_ref=dst, send_sem=ss_w, recv_sem=rs_w.at[receive_sem(stage, bundle(stage, i))],
            device_id=dev[to], device_id_type=MESH,
        )

    def arrive(stage, which):
        if stage == GATES:
            ref = relay.at[quarter(which)] if which < 4 else gate.at[:, pl.ds(PEER * BLOCK, BLOCK)]
        else:
            if stage == PEER:
                col, cols = ((0, 5 * COLS), (column(ZL), 3 * COLS))[which]
            else:
                col, cols = (column((L, R, Z, FAR, ZL, ZF)[which]), 2 * COLS if which == 4 else COLS)
            ref = w.at[pl.ds(stage * BLOCK, BLOCK), pl.ds(col, cols)]
        done(ref, rs_w.at[receive_sem(stage, which)])

    def share_copy(stage, group):
        rows = pl.ds(stage * BLOCK, BLOCK)
        col, cols = GROUPS[group]
        return pltpu.make_async_remote_copy(
            src_ref=w.at[rows, pl.ds(col, cols)], dst_ref=w.at[rows, pl.ds(sibling_column(col), cols)],
            send_sem=ss_s, recv_sem=rs_s.at[stage, min(group, 1)],
            device_id=dev["sib"], device_id_type=MESH,
        )

    def shared(stage, part):
        col, cols = ((0, 1280), (2560, 768))[part]
        done(w.at[pl.ds(stage * BLOCK, BLOCK), pl.ds(sibling_column(col), cols)], rs_s.at[stage, part])

    row8 = lax.broadcasted_iota(jnp.int32, (8, 128), 0)
    col8 = lax.broadcasted_iota(jnp.int32, (8, 128), 1)
    by_b = (col8 % 8 == row8).astype(F32)
    by_a = (col8 % 64 // 8 == row8).astype(F32)
    row_t = lax.broadcasted_iota(jnp.int32, (128, 8), 0)
    col_t = lax.broadcasted_iota(jnp.int32, (128, 8), 1)
    by_b_t = (row_t % 8 == col_t).astype(F32)
    by_a_t = (row_t % 64 // 8 == col_t).astype(F32)
    dot = functools.partial(jnp.dot, precision=HIGH, preferred_element_type=F32)

    def query_copy(i, receiving=False):
        mine = c * 8 + z * 4
        src, dst, to = (
            (q_hbm, qbuf.at[mine + (xm if receiving else x)], "xp"),
            (q_hbm, qbuf.at[mine + (xp if receiving else x)], "xm"),
            (qbuf.at[mine + xm], qbuf.at[mine + ((x + 2) % 4 if receiving else xm)], "xp"),
            (qbuf.at[pl.ds(mine, 4)], qbuf.at[pl.ds(c * 8 + (1 - z) * 4 if receiving else mine, 4)], "z"),
            (qbuf.at[pl.ds(c * 8, 8)], qbuf.at[pl.ds((1 - c) * 8 if receiving else c * 8, 8)], "sib"),
        )[i]
        return pltpu.make_async_remote_copy(
            src_ref=src, dst_ref=dst, send_sem=ss_q, recv_sem=rs_q.at[(0, 1, 1, 2, 3)[i]],
            device_id=dev[to], device_id_type=MESH,
        )

    def query_far():
        query_copy(0, True).wait_recv()
        query_copy(2).start()

    def query_z():
        done(qbuf.at[pl.ds(c * 8 + z * 4, 2)], rs_q.at[1])
        loaded("query")
        query_copy(3).start()

    def query_sibling():
        query_copy(3, True).wait_recv()
        query_copy(4).start()

    def y_copy(i, owner):
        return pltpu.make_async_remote_copy(
            src_ref=ybuf.at[owner], dst_ref=ybuf.at[owner], send_sem=ss_y, recv_sem=rs_y,
            device_id=(dp, zh * 4 + (y + i) % 4), device_id_type=MESH,
        )

    def z_copy(owner):
        return pltpu.make_async_remote_copy(
            src_ref=zbuf.at[owner], dst_ref=zbuf.at[owner], send_sem=ss_y, recv_sem=rs_z,
            device_id=(dp, (1 - zh) * 4 + y), device_id_type=MESH,
        )

    def signs_copy():
        return pltpu.make_async_remote_copy(
            src_ref=shid_hbm.at[:, pl.ds(given, BLOCK)], dst_ref=shid.at[:, pl.ds(PEER * BLOCK, BLOCK)],
            send_sem=ss_h, recv_sem=rs_h, device_id=dev["peer"], device_id_type=MESH,
        )

    def input_part():
        loaded("input", "insigns")
        sign = (2 * sin[...] - 1).astype(F32).astype(BF16)
        ybuf[y] = lax.dot_general(sign, li[...], NT, preferred_element_type=F32) * D ** (-0.5)
        for i in range(1, 4):
            y_copy(i, y).start()

    def input_sum():
        done(ybuf.at[pl.ds(0, 3)], rs_y)
        zbuf[zh] = ybuf[0] + ybuf[1] + ybuf[2] + ybuf[3]
        z_copy(zh).start()

    def input_weigh():
        z_copy(1 - zh).wait_recv()
        full = zbuf[0] + zbuf[1]
        pos = lax.broadcasted_iota(jnp.int32, (8, SLOTS), 1)
        for e in range(TOK // SLOTS):
            count = len_ref[e]
            scale = FF ** (-0.5) / count.astype(F32)
            part = full[:, e * SLOTS : (e + 1) * SLOTS]
            part = jnp.where(pos < count, part * scale, 0.0)
            in64[pl.ds(e * SLOTS, SLOTS), :] = dot(part.T, by_a)

    def hidden_signs():
        loaded("signs")
        signs_copy().wait_recv()
        sign = (2 * shid[...] - 1).astype(F32)
        s64[...] = jnp.dot(by_b_t.astype(BF16), sign.astype(BF16), preferred_element_type=F32).astype(BF16)

    def query_matrix():
        loaded("bi", "bo", "ev")
        query_copy(4, True).wait_recv()
        for i in range(16):
            owner = i % 4 * 4 + i // 4 % 2 * 2 + i // 8
            qfull[pl.ds(4 * owner, 4), :] = qbuf[i]
        kron = dot(dot(by_a_t, bi[...]), by_a[:, :64]) * dot(dot(by_b_t, bo[...]), by_b[:, :64])
        values = jnp.sum(dot(ev[...], by_b[:, :64]) * by_a[:, :64], axis=0, keepdims=True)
        both = lax.dot_general(kron / (values + SHIFT), kron[:64], NT, precision=HIGH, preferred_element_type=F32)
        twice = dot(both, qfull[...])
        top = twice.astype(BF16)
        rest = (twice - top.astype(F32)).astype(BF16)
        both_parts = jnp.concatenate([top[:64], rest[:64]], axis=0)
        mat[pl.ds(0, 128), :] = both_parts
        mat[pl.ds(128, 128), :] = both_parts

    def activation(rows):
        g = gate[:, rows].astype(F32)
        return g * (0.5 + 0.5 * jnp.tanh(0.5 * g))

    def project(rows, product, factor):
        up = (product * factor).astype(BF16)
        out64[...] += lax.dot_general(up, s64[:, rows], NT, preferred_element_type=F32)

    def first_part(j):
        rows = pl.ds(pl.multiple_of(j * BLOCK, BLOCK), BLOCK)
        hid[j] = lax.dot_general(
            ct[:, pl.ds(0, 2560)], w[rows, pl.ds(0, 2560)], NT, preferred_element_type=F32
        )
        act[j] = activation(rows)

    def second_part(j):
        rows = pl.ds(pl.multiple_of(j * BLOCK, BLOCK), BLOCK)
        product = hid[j] + lax.dot_general(
            ct[:, pl.ds(2560, 1536)], w[rows, pl.ds(2560, 1536)], NT, preferred_element_type=F32
        )
        project(rows, product, act[j])

    def whole(j):
        rows = pl.ds(pl.multiple_of(j * BLOCK, BLOCK), BLOCK)
        product = lax.dot_general(ct[...], w[rows, :], NT, preferred_element_type=F32)
        project(rows, product, activation(rows))

    def step_actions(i):
        part, j = SCHEDULE[i][1]
        for n, (arrivals, (what, at, which)) in enumerate(PLAN[i]):
            if i == 0 and n == EARLY:
                start("give", "input", "insigns", "query", "signs", "c", "gate", "bi", "bo", "ev")
            for stage, copy in arrivals:
                arrive(stage, copy)
            if what == 0:
                if (i, n) == GIVE_FIRST:
                    loaded("give")
                remote(at, which).start()
            elif what == 1:
                share_copy(at, which).start()
            elif what == 2:
                small[at]()
        if i == 0:
            loaded("c", "gate")
        for half in ((0,), (1,), (0, 1))[part]:
            shared(j, half)

    def block_of(step, part):
        j = jnp.int32(-1)
        for i, (_, (which, block)) in enumerate(SCHEDULE):
            if which == part:
                j = jnp.where(step == i, block, j)
        return j

    def step(k, _):
        for i in range(len(SCHEDULE)):
            pl.when(k == i)(functools.partial(step_actions, i))
        for part, compute in enumerate((first_part, second_part, whole)):
            j = block_of(k, part)
            pl.when(j >= 0)(functools.partial(compute, j))
        return 0

    def input_start():
        query_copy(0).start()
        query_copy(1).start()
        signs_copy().start()
        input_part()

    small = (
        input_start, query_far, input_sum, hidden_signs, query_z, input_weigh, query_sibling, query_matrix,
    )
    out64[...] = jnp.zeros_like(out64)
    lax.fori_loop(0, len(SCHEDULE), step, 0)

    rows = [
        jnp.sum(in64[pl.ds(e * SLOTS, SLOTS), :] * out64[pl.ds(e * SLOTS, SLOTS), :], axis=0, keepdims=True)
        for e in range(TOK // SLOTS)
    ]
    gbuf[tn] = jnp.zeros((8, 128), F32)
    for e in range(TOK // SLOTS):
        gbuf[tn, pl.ds(e, 1), :] = rows[e]

    def g_copy(i, owner):
        return pltpu.make_async_remote_copy(
            src_ref=gbuf.at[owner], dst_ref=gbuf.at[owner], send_sem=ss_g, recv_sem=rs_g,
            device_id=(dp, (zh + 1 - i // 4) % 2 * 4 + (y + FAR_FIRST[i % 4]) % 4), device_id_type=MESH,
        )

    for i in range(7):
        g_copy(i, tn).start()
    done(w.at[pl.ds(0, 928)], ss_w)
    done(w.at[:, pl.ds(0, 2048)], ss_s)
    done(qbuf.at[pl.ds(0, 15)], ss_q)
    done(ybuf, ss_y)
    signs_copy().wait_send()
    done(gbuf.at[pl.ds(0, 7)], rs_g)
    total = gbuf[0]
    for i in range(1, 8):
        total = total + gbuf[i]
    top = total.astype(BF16)
    rest = (total - top.astype(F32)).astype(BF16)
    both = jnp.concatenate([top, rest], axis=1)
    o_ref[...] = jnp.dot(both, mat[...], preferred_element_type=F32)[:4, :]
    done(gbuf.at[pl.ds(0, 7)], ss_g)


def on_device(
    layer_input, output_cotangent, gate_preact, down_weight, lengths, input_signs, hidden_signs,
    basis_in, basis_out, eigenvalues, query_grads,
):
    any_spec = pl.BlockSpec(memory_space=pl.ANY)
    vmem, dma = pltpu.VMEM, pltpu.SemaphoreType.DMA
    specs = [any_spec] * 11
    specs[4] = pl.BlockSpec(memory_space=pltpu.SMEM)
    return pl.pallas_call(
        kernel,
        out_shape=pltpu.VMEM((4, 512), F32),
        in_specs=specs,
        out_specs=pl.BlockSpec(memory_space=pltpu.VMEM),
        scratch_shapes=[
            vmem((HID, D), BF16),
            vmem((TOK, D), BF16),
            vmem((TOK, HID), BF16),
            vmem((BLOCK, COLS), BF16),
            vmem((TOK, BLOCK), BF16),
            vmem((TOK, BLOCK), BF16),
            vmem((TOK, 512), BF16),
            vmem((8, 512), jnp.int32),
            vmem((8, HID), jnp.int32),
            vmem((8, 8), F32),
            vmem((8, 8), F32),
            vmem((8, 8), F32),
            vmem((16, 4, 512), F32),
            vmem((64, 512), F32),
            vmem((256, 512), BF16),
            vmem((4, 8, TOK), F32),
            vmem((2, 8, TOK), F32),
            vmem((8, 8, 128), F32),
            vmem((TOK, 128), F32),
            vmem((128, HID), BF16),
            vmem((N, TOK, BLOCK), F32),
            vmem((N, TOK, BLOCK), F32),
            vmem((TOK, 128), F32),
            dma, dma((RECEIVE_SEMS,)), dma, dma((N, 2)), dma, dma((4,)), dma, dma, dma, dma, dma, dma, dma, dma((12,)),
        ],
        compiler_params=pltpu.CompilerParams(
            collective_id=0, has_side_effects=True, vmem_limit_bytes=56 * 1024 * 1024
        ),
        cost_estimate=pl.CostEstimate(flops=2 * TOK * HID * D, bytes_accessed=30_000_000, transcendentals=TOK * HID),
        name="scores",
    )(
        layer_input.reshape(TOK, 512),
        output_cotangent.reshape(TOK, D),
        gate_preact.reshape(TOK, HID),
        down_weight,
        lengths,
        input_signs.T,
        hidden_signs.T,
        basis_in,
        basis_out,
        eigenvalues,
        query_grads.T,
    )


def solution(mesh):
    in_specs = (
        P("dp", None, "tensor"),
        P("dp", None, None),
        P("dp", None, "tensor"),
        P("tensor", "dp"),
        P("dp"),
        P("tensor", None),
        P("tensor", None),
        P(),
        P(),
        P(),
        P("tensor", "dp"),
    )
    return jax.shard_map(
        on_device, mesh=mesh, in_specs=in_specs, out_specs=P("dp", "tensor"), check_vma=False
    )
```
